32 devices in a mesh: mem: 8 (over z, x), lon: 4 (over y, core).
Axes of the slice: x: 2, y: 2, z: 4, core: 2. Of those that a mesh axis runs over, the one named last changes fastest.
Arguments:
- state: bfloat16 [256, 8192], P('mem', 'lon'), may hold values from -6 to 6
- hx: bfloat16 [128, 256, 128], P('lon'), may hold values from -6 to 6
- obs_value: float32 [128, 128], P('lon'), may hold values from -10 to 10
- obs_rinv: float32 [128, 128], P('lon'), may hold values from 0.3 to 3
- obs_count: int32 [128], P('lon'), may hold values from 1 to 128
- loc_pattern: int32 [64, 8], P('lon'), may hold values from 0 to 95, as said below
Outputs:
- analysis: bfloat16 [256, 8192], P('mem', 'lon')
The draws below stay inside these ranges and needn't reach their ends.
Inputs may be any that keep to these rules, and one draw needn't show every extreme that they name: obs_count[n] is how many of block n's first observations are valid; the rest are ignored. Each row of loc_pattern holds 8 different window positions out of 96: the previous region's blocks, the patch's own region's blocks, the next region's blocks, around the closed longitude loop.
All inputs are finite; a program needn't handle non-finite values.
Results may differ from the reference program's by a relative error of at most 0.0065.
Values may be sent and summed in bfloat16 or wider, within the bound.
No kernel may reach another device: no remote copies, remote signals or barrier semaphores. Data moves between devices by JAX's collectives and lax.ppermute only.
A program may use at most 64 MiB of HBM per device.

```python
import math
import jax
import jax.numpy as jnp
from jax import lax

K = 256
B = 128
PTS = 128
BLK_DEV = 32
USE = 8
ITERS = 6
RP = 16
NPATCH = 64
G = 8192
NBLK = 128


def draw_loc_pattern(key, part):
    window = 3 * BLK_DEV
    scores = jax.random.randint(key, (NPATCH, window), 0, 1 << 20) * window + jnp.arange(window, dtype=jnp.int32)[None, :]
    chosen = lax.top_k(scores, USE)[1]
    return chosen.astype(jnp.int32)


def plant(values, rng, least, high):
    dims = values.shape
    place = [jax.random.randint(jax.random.fold_in(rng, axis), (), 0, dims[axis]) for axis in range(len(dims))]
    values = values.at[tuple(place)].set(least)
    longest = dims.index(max(dims))
    place[longest] = (place[longest] + 1) % dims[longest]
    return values.at[tuple(place)].set(high)


def levels(own_key, extent, shards, smallest, top_value):
    factor_of = 1.0
    for dim, parts in shards:
        draws = jax.random.uniform(jax.random.fold_in(jax.random.fold_in(own_key, 6), dim), (parts,), jnp.float32, smallest / len(shards), top_value / len(shards))
        factor_of = factor_of * jnp.repeat(jnp.exp(draws), extent[dim] // parts).reshape((-1,) + (1,) * (len(extent) - 1 - dim))
    return factor_of


def centred(stream_key, extent, width, bound, split=(), kind=jnp.bfloat16):
    drawn = width * jax.random.normal(stream_key, extent, jnp.float32)
    if split:
        drawn = drawn * levels(stream_key, extent, split, -0.22, 0.18)
    return jnp.clip(drawn, -bound, bound).astype(kind)


def setup_inputs(seed: int = 0) -> dict:
    key_list = jax.random.split(jax.random.key(seed), 7)
    state = centred(key_list[0], (K, G), 1.0, 6.0, ((0, 8), (1, 4)))
    hx = centred(key_list[1], (NBLK, K, B), 1.0, 6.0, ((0, 4),))
    obs_value = centred(key_list[2], (NBLK, B), 2.0, 10.0, ((0, 4),), jnp.float32)
    obs_rinv = jnp.clip(jnp.exp(math.log(3.0) - 2.3025851 * jax.random.uniform(key_list[3], (NBLK, B), jnp.float32) ** levels(key_list[3], (NBLK, B), ((0, 4),), -0.2, 0.2)), 0.3, 3.0)
    obs_count = plant(jax.random.randint(key_list[4], (NBLK,), 1, B + 1), jax.random.fold_in(key_list[4], 1), 1, B).astype(jnp.int32)
    loc_pattern = draw_loc_pattern(jax.random.fold_in(key_list[6], 71), 0)
    return dict(state=state, hx=hx, obs_value=obs_value, obs_rinv=obs_rinv, obs_count=obs_count, loc_pattern=loc_pattern)


def reference(state, hx, obs_value, obs_rinv, obs_count, loc_pattern):
    high = lax.Precision.HIGHEST
    obs_mean = lax.optimization_barrier(jnp.sum(hx.astype(jnp.float32), axis=1)) / K
    obs_pert = (hx.astype(jnp.float32) - obs_mean[:, None, :]).astype(jnp.bfloat16)
    valid = jnp.arange(B, dtype=jnp.int32)[None, :] < obs_count[:, None]
    weight = jnp.where(valid, obs_rinv, jnp.float32(0.0))
    innov = weight * (obs_value - obs_mean)
    weight_b = weight.astype(jnp.bfloat16)
    innov_b = innov.astype(jnp.bfloat16)
    scaled = (weight_b.astype(jnp.float32)[:, None, :] * obs_pert.astype(jnp.float32)).astype(jnp.bfloat16)
    eye = jnp.eye(K, dtype=jnp.float32)

    def one_patch(patch):
        region = patch // RP
        rank = patch % RP
        picks = loc_pattern[patch]
        blocks = (region * BLK_DEV - BLK_DEV + picks) % NBLK
        offset = (picks.astype(jnp.float32) + 0.5) / BLK_DEV - 1.0 - (rank.astype(jnp.float32) + 0.5) / RP
        taper = jnp.exp(-0.5 * offset * offset)
        system = (K - 1.0) * eye
        forcing = jnp.zeros((K,), jnp.float32)
        for slot in range(USE):
            block = blocks[slot]
            gram = jnp.dot(obs_pert[block], scaled[block].T, preferred_element_type=jnp.float32)
            vec = jnp.dot(obs_pert[block], innov_b[block], preferred_element_type=jnp.float32)
            system = system + taper[slot] * gram
            forcing = forcing + taper[slot] * vec
        scale = jnp.sqrt(jnp.sum(system * system))
        iterate = system / scale
        root = eye
        for step in range(ITERS):
            factor = 1.5 * eye - 0.5 * jnp.dot(root, iterate, precision=high)
            iterate = jnp.dot(iterate, factor, precision=high)
            root = jnp.dot(factor, root, precision=high)
        root = root / jnp.sqrt(scale)
        mean_weight = jnp.dot(root, jnp.dot(root, forcing, precision=high), precision=high)
        transform = jnp.sqrt(jnp.float32(K - 1.0)) * root + mean_weight[:, None]
        columns = lax.dynamic_slice(state, (jnp.int32(0), (patch * PTS).astype(jnp.int32)), (K, PTS))
        state_mean = lax.optimization_barrier(jnp.sum(columns.astype(jnp.float32), axis=0)) / K
        deviation = columns.astype(jnp.float32) - state_mean[None, :]
        updated = state_mean[None, :] + jnp.dot(transform.T, deviation, precision=high)
        return updated.astype(jnp.bfloat16)
    result = lax.map(one_patch, jnp.arange(NPATCH, dtype=jnp.int32))
    return jnp.transpose(result, (1, 0, 2)).reshape(K, NPATCH * PTS)
```

```python
import functools

import jax
import jax.numpy as jnp
from jax import lax
from jax.experimental import pallas as pl
from jax.experimental.pallas import tpu as pltpu
from jax.sharding import PartitionSpec as P

ITERS = 6
PAD = 16
CHUNK = 4
F32 = jnp.float32
BF16 = jnp.bfloat16

VMEM = pl.BlockSpec(memory_space=pltpu.VMEM)
SMEM = pl.BlockSpec(memory_space=pltpu.SMEM)
ANY = pl.BlockSpec(memory_space=pl.ANY)


def split(value):
    high = value.astype(BF16)
    return high, (value - high.astype(F32)).astype(BF16)


def product(left, right):
    lhs = jnp.concatenate([left[0], left[0], left[1]], axis=1)
    rhs = jnp.concatenate([right[0], right[1], right[0]], axis=0)
    return jnp.dot(lhs, rhs, preferred_element_type=F32)


def share(pattern, row, side, patches, pert, weights, innov, left, right):
    blocks, members, width = pert.shape
    uses = pattern.shape[1]
    for slot in range(uses):
        position = pattern[row, slot]
        block = position - side * blocks
        here = jnp.logical_and(block >= 0, block < blocks)
        block = jnp.clip(block, 0, blocks - 1)
        spot = jnp.full((1, width), position, jnp.int32).astype(F32)
        rank = jnp.full((1, width), row, jnp.int32).astype(F32)
        offset = (spot + 0.5) / blocks - 1.0 - (rank + 0.5) / patches
        taper = jnp.exp(-0.5 * offset * offset) * jnp.where(here, 1.0, 0.0)
        cols = slice(slot * width, (slot + 1) * width)
        picked = pert[block]
        weight = taper * weights[pl.ds(block, 1), :]
        left[:members, cols] = (weight * picked.astype(F32)).astype(BF16)
        vector = taper * innov[pl.ds(block, 1), :]
        left[members:, cols] = jnp.broadcast_to(vector, (PAD, width)).astype(BF16)
        right[:, cols] = picked
    return lax.dot_general(
        left[...], right[...], (((1,), (1,)), ((), ())), preferred_element_type=F32
    )


def own_kernel(
    patches, here, count, pattern, hx, value, rinv, pert, weights, innov, own, raw, left, right, sems
):
    blocks, members, width = raw.shape
    copies = [
        pltpu.make_async_copy(hx.at[pl.ds(i, CHUNK)], raw.at[pl.ds(i, CHUNK)], sems.at[i // CHUNK])
        for i in range(0, blocks, CHUNK)
    ]
    for copy in copies:
        copy.start()
    lane = lax.broadcasted_iota(jnp.int32, (1, width), 1)
    for block in range(blocks):
        if block % CHUNK == 0:
            copies[block // CHUNK].wait()
        member = raw[block].astype(F32)
        mean = jnp.sum(member, axis=0, keepdims=True) / members
        pert[block] = (member - mean).astype(BF16)
        weight = jnp.where(lane < count[block], rinv[block : block + 1, :], 0.0)
        gap = weight * (value[block : block + 1, :] - mean)
        weights[block : block + 1, :] = weight.astype(BF16).astype(F32)
        innov[block : block + 1, :] = gap
    mine = own.shape[0]
    for patch in range(mine):
        row = here[0] * mine + patch
        own[patch] = share(pattern, row, 1, patches, pert, weights, innov, left, right)


def neighbour_kernel(
    patches, here, before, after, pert, weights, innov, to_before, to_after, left, right
):
    members = pert.shape[1]
    half = members // 2
    mine = to_before.shape[0]
    above = lax.broadcasted_iota(jnp.int32, (half, half), 0)
    across = lax.broadcasted_iota(jnp.int32, (half, half), 1)
    for pattern, side, out in ((before, 2, to_before), (after, 0, to_after)):
        for patch in range(mine):
            row = here[0] * mine + patch
            part = share(pattern, row, side, patches, pert, weights, innov, left, right)
            corner = part[half:members, half:]
            out[patch, :half, :] = part[:half, half:].astype(BF16)
            out[patch, half:members, :] = jnp.where(
                above >= across, part[:half, :half], corner
            ).astype(BF16)
            diagonal = jnp.sum(jnp.where(above == across, corner, 0.0), axis=0, keepdims=True)
            force = part[members : members + 1]
            rows = [diagonal, force[:, :half], force[:, half:]]
            parts = [split(value) for value in rows]
            index = lax.broadcasted_iota(jnp.int32, (PAD, half), 0)
            tail = jnp.zeros((PAD, half), F32)
            for i, (high, low) in enumerate(parts):
                tail = jnp.where(index == 2 * i, high.astype(F32), tail)
                tail = jnp.where(index == 2 * i + 1, low.astype(F32), tail)
            out[patch, members:, :] = tail.astype(BF16)


def analysis_kernel(here, own, before, after, state, out, columns, sem):
    mine, _, members = own.shape
    half = members // 2
    points = out.shape[1] // mine
    width = mine * points
    start = pl.multiple_of(here[0] * width, width)
    copy = pltpu.make_async_copy(state.at[:, pl.ds(start, width)], columns, sem)
    copy.start()
    above = lax.broadcasted_iota(jnp.int32, (half, half), 0)
    across = lax.broadcasted_iota(jnp.int32, (half, half), 1)
    row = lax.broadcasted_iota(jnp.int32, (members, members), 0)
    col = lax.broadcasted_iota(jnp.int32, (members, members), 1)
    eye = jnp.where(row == col, 1.0, 0.0)
    each = range(mine)
    iterate, scale, forcing = [], [], []
    for patch in each:
        packed = before[patch].astype(F32) + after[patch].astype(F32)
        upper = packed[:half]
        mixed = packed[half:members]
        tail = packed[members:]
        diagonal = tail[0:1] + tail[1:2]
        force = jnp.concatenate([tail[2:3] + tail[3:4], tail[4:5] + tail[5:6]], axis=1)
        flipped = mixed.T
        first = jnp.where(above >= across, mixed, flipped)
        second = jnp.where(above < across, mixed, flipped)
        second = jnp.where(above == across, diagonal, second)
        far = jnp.concatenate(
            [
                jnp.concatenate([first, upper], axis=1),
                jnp.concatenate([upper.T, second], axis=1),
            ],
            axis=0,
        )
        system = own[patch, :members, :] + far + (members - 1.0) * eye
        total = jnp.sum(jnp.sum(system * system, axis=0, keepdims=True), axis=1, keepdims=True)
        norm = jnp.sqrt(total)
        scale.append(norm)
        iterate.append(system / norm)
        forcing.append(force + own[patch, members : members + 1, :])
    factor = [1.5 * eye - 0.5 * iterate[p] for p in each]
    root = list(factor)
    parts = [split(factor[p]) for p in each]
    iterate = [product(split(iterate[p]), parts[p]) for p in each]
    for step in range(1, ITERS):
        rooted = [split(root[p]) for p in each]
        iterated = [split(iterate[p]) for p in each]
        factor = [1.5 * eye - 0.5 * product(rooted[p], iterated[p]) for p in each]
        parts = [split(factor[p]) for p in each]
        if step < ITERS - 1:
            iterate = [product(iterated[p], parts[p]) for p in each]
        root = [product(parts[p], rooted[p]) for p in each]
    copy.wait()
    for p in each:
        cols = slice(p * points, (p + 1) * points)
        member = columns[:, cols].astype(F32)
        mean = jnp.sum(member, axis=0, keepdims=True) / members
        rooted = split(root[p])
        spread = product(rooted, split(member - mean))
        force = jnp.broadcast_to(forcing[p], (PAD, members))
        gain = product(split(force), rooted)
        shift = product(split(gain), split(spread))[0:1]
        shift = mean + shift / scale[p]
        out[:, cols] = (
            shift + jnp.sqrt(members - 1.0) / jnp.sqrt(scale[p]) * spread
        ).astype(BF16)


def layout_kernel(pieces, out):
    count, _, width = pieces.shape
    for piece in range(count):
        out[:, piece * width : (piece + 1) * width] = pieces[piece]


def body(state, hx, obs_value, obs_rinv, obs_count, loc_pattern):
    blocks, members, width = hx.shape
    patches, uses = loc_pattern.shape
    mem_total = lax.axis_size("mem")
    mine = patches // mem_total
    local, points = state.shape
    ring = lax.axis_size("lon")
    up = [(i, (i + 1) % ring) for i in range(ring)]
    down = [(j, i) for i, j in up]
    here = lax.axis_index("mem").astype(jnp.int32).reshape(1)
    shape = jax.ShapeDtypeStruct
    padded = members + PAD

    before = lax.ppermute(loc_pattern, "lon", up)
    after = lax.ppermute(loc_pattern, "lon", down)
    everyone = lax.all_gather(state, "mem", axis=0, tiled=True)
    operands = [
        pltpu.VMEM((padded, uses * width), BF16),
        pltpu.VMEM((members, uses * width), BF16),
    ]
    limit = pltpu.CompilerParams(vmem_limit_bytes=16 * 1024 * 1024)
    gram = 2 * padded * members * uses * width
    pert, weights, innov, own = pl.pallas_call(
        functools.partial(own_kernel, patches),
        out_shape=(
            shape((blocks, members, width), BF16),
            shape((blocks, width), F32),
            shape((blocks, width), F32),
            shape((mine, padded, members), F32),
        ),
        in_specs=[SMEM, SMEM, SMEM, ANY, VMEM, VMEM],
        out_specs=(VMEM,) * 4,
        scratch_shapes=[pltpu.VMEM((blocks, members, width), BF16)]
        + operands
        + [pltpu.SemaphoreType.DMA((blocks // CHUNK,))],
        compiler_params=limit,
        cost_estimate=pl.CostEstimate(
            flops=mine * gram, bytes_accessed=2 * hx.size * 2, transcendentals=0
        ),
        name="own_share",
    )(here, obs_count, loc_pattern, hx, obs_value, obs_rinv)
    packed = shape((mine, padded, members // 2), BF16)
    to_before, to_after = pl.pallas_call(
        functools.partial(neighbour_kernel, patches),
        out_shape=(packed, packed),
        in_specs=[SMEM, SMEM, SMEM, VMEM, VMEM, VMEM],
        out_specs=(VMEM,) * 2,
        scratch_shapes=operands,
        compiler_params=limit,
        cost_estimate=pl.CostEstimate(
            flops=2 * mine * gram, bytes_accessed=hx.size * 2, transcendentals=0
        ),
        name="neighbour_share",
    )(here, before, after, pert, weights, innov)
    from_before = lax.ppermute(to_after, "lon", up)
    from_after = lax.ppermute(to_before, "lon", down)
    span = points // mem_total
    updated = pl.pallas_call(
        analysis_kernel,
        out_shape=shape((members, span), BF16),
        in_specs=[SMEM, VMEM, VMEM, VMEM, ANY],
        out_specs=VMEM,
        scratch_shapes=[pltpu.VMEM((members, span), BF16), pltpu.SemaphoreType.DMA],
        compiler_params=limit,
        cost_estimate=pl.CostEstimate(
            flops=mine * 16 * 3 * 2 * members**3, bytes_accessed=2**20, transcendentals=0
        ),
        name="analysis",
    )(here, own, from_before, from_after, everyone)
    pieces = lax.all_to_all(
        updated.reshape(mem_total, local, span), "mem", split_axis=0, concat_axis=0
    )
    return pl.pallas_call(
        layout_kernel,
        out_shape=shape((local, points), BF16),
        in_specs=[VMEM],
        out_specs=VMEM,
        name="layout",
    )(pieces)


def solution(mesh):
    in_specs = (
        P("mem", "lon"),
        P("lon", None, None),
        P("lon", None),
        P("lon", None),
        P("lon"),
        P("lon", None),
    )
    out_specs = P("mem", "lon")
    return jax.shard_map(body, mesh=mesh, in_specs=in_specs, out_specs=out_specs, check_vma=False)
```

```python
import functools

import jax
import jax.numpy as jnp
from jax import lax
from jax.experimental import pallas as pl
from jax.experimental.pallas import tpu as pltpu
from jax.sharding import PartitionSpec as P

ITERS = 6
PAD = 16
CHUNK = 4
PAIR = 2
F32 = jnp.float32
BF16 = jnp.bfloat16

VMEM = pl.BlockSpec(memory_space=pltpu.VMEM)
SMEM = pl.BlockSpec(memory_space=pltpu.SMEM)
HBM = pl.BlockSpec(memory_space=pltpu.HBM)


def stay(value):
    return pltpu.with_memory_space_constraint(value, pltpu.HBM)


def split(value):
    high = value.astype(BF16)
    return high, (value - high.astype(F32)).astype(BF16)


def product(left, right):
    lhs = jnp.concatenate([left[0], left[0], left[1]], axis=1)
    rhs = jnp.concatenate([right[0], right[1], right[0]], axis=0)
    return jnp.dot(lhs, rhs, preferred_element_type=F32)


def share(pattern, row, side, patches, pert, weights, innov, left, right):
    blocks, members, width = pert.shape
    uses = pattern.shape[0]
    for slot in range(uses):
        position = pattern[slot, row]
        block = position - side * blocks
        here = jnp.logical_and(block >= 0, block < blocks)
        block = jnp.clip(block, 0, blocks - 1)
        spot = jnp.full((1, width), position, jnp.int32).astype(F32)
        rank = jnp.full((1, width), row, jnp.int32).astype(F32)
        offset = (spot + 0.5) / blocks - 1.0 - (rank + 0.5) / patches
        taper = jnp.exp(-0.5 * offset * offset) * jnp.where(here, 1.0, 0.0)
        cols = slice(slot * width, (slot + 1) * width)
        picked = pert[block]
        weight = taper * weights[pl.ds(block, 1), :]
        left[:members, cols] = (weight * picked.astype(F32)).astype(BF16)
        vector = taper * innov[pl.ds(block, 1), :]
        left[members:, cols] = jnp.broadcast_to(vector, (PAD, width)).astype(BF16)
        right[:, cols] = picked
    return lax.dot_general(
        left[...], right[...], (((1,), (1,)), ((), ())), preferred_element_type=F32
    )


def own_kernel(
    patches,
    here,
    count_all,
    pattern_all,
    hx,
    value_all,
    rinv_all,
    pert,
    weights,
    innov,
    own,
    raw,
    count,
    pattern,
    value,
    rinv,
    left,
    right,
    sems,
    small,
):
    blocks, members, width = raw.shape
    smalls = [
        pltpu.make_async_copy(source, target, small.at[i])
        for i, (source, target) in enumerate(
            ((count_all, count), (value_all, value), (rinv_all, rinv), (pattern_all, pattern))
        )
    ]
    copies = [
        pltpu.make_async_copy(hx.at[pl.ds(i, CHUNK)], raw.at[pl.ds(i, CHUNK)], sems.at[i // CHUNK])
        for i in range(0, blocks, CHUNK)
    ]
    for copy in smalls + copies:
        copy.start()
    for copy in smalls:
        copy.wait()
    lane = lax.broadcasted_iota(jnp.int32, (1, width), 1)
    for block in range(blocks):
        if block % CHUNK == 0:
            copies[block // CHUNK].wait()
        member = raw[block].astype(F32)
        mean = jnp.sum(member, axis=0, keepdims=True) / members
        pert[block] = (member - mean).astype(BF16)
        weight = jnp.where(lane < count[block], rinv[block : block + 1, :], 0.0)
        gap = weight * (value[block : block + 1, :] - mean)
        weights[block : block + 1, :] = weight.astype(BF16).astype(F32)
        innov[block : block + 1, :] = gap
    mine = own.shape[0]
    for patch in range(mine):
        row = here[0] * mine + patch
        own[patch] = share(pattern, row, 1, patches, pert, weights, innov, left, right)


def neighbour_kernel(
    patches,
    here,
    before,
    after,
    pert,
    weights,
    innov,
    state,
    paired,
    to_before,
    to_after,
    *rest,
):
    slabs, (left, right, sems) = rest[:-3], rest[-3:]
    span = slabs[0].shape[2]
    length = len(slabs)
    layer, side = here[0] // PAIR, here[0] % PAIR
    moves = []
    for shift, slab in enumerate(slabs):
        target = lax.rem(layer + shift, length) * PAIR + side
        cols = pl.ds(pl.multiple_of(target * span, span), span)
        moves.append((state.at[:, cols], slab.at[side]))
        moves.append((paired.at[:, cols], slab.at[1 - side]))
    moves = [pltpu.make_async_copy(*move, sems.at[i]) for i, move in enumerate(moves)]
    for move in moves:
        move.start()
    members = pert.shape[1]
    half = members // 2
    mine = to_before.shape[0]
    above = lax.broadcasted_iota(jnp.int32, (half, half), 0)
    across = lax.broadcasted_iota(jnp.int32, (half, half), 1)
    for pattern, side, out in ((before, 2, to_before), (after, 0, to_after)):
        for patch in range(mine):
            row = here[0] * mine + patch
            part = share(pattern, row, side, patches, pert, weights, innov, left, right)
            corner = part[half:members, half:]
            out[patch, :half, :] = part[:half, half:].astype(BF16)
            out[patch, half:members, :] = jnp.where(
                above >= across, part[:half, :half], corner
            ).astype(BF16)
            diagonal = jnp.sum(jnp.where(above == across, corner, 0.0), axis=0, keepdims=True)
            force = part[members : members + 1]
            rows = [diagonal, force[:, :half], force[:, half:]]
            parts = [split(value) for value in rows]
            index = lax.broadcasted_iota(jnp.int32, (PAD, half), 0)
            tail = jnp.zeros((PAD, half), F32)
            for i, (high, low) in enumerate(parts):
                tail = jnp.where(index == 2 * i, high.astype(F32), tail)
                tail = jnp.where(index == 2 * i + 1, low.astype(F32), tail)
            out[patch, members:, :] = tail.astype(BF16)
    for move in moves:
        move.wait()


def analysis_kernel(here, own, before, after, *rest):
    slabs, (out, columns, sems) = rest[:-3], rest[-3:]
    mine, _, members = own.shape
    half = members // 2
    points = out.shape[1] // mine
    length = len(slabs)
    _, local, _ = slabs[0].shape
    copies = []
    for shift, slab in enumerate(slabs):
        source = lax.rem(here[0] // PAIR - shift + length, length)
        for i in range(PAIR):
            rows = pl.ds(pl.multiple_of((source * PAIR + i) * local, local), local)
            copies.append(
                pltpu.make_async_copy(slab.at[i], columns.at[rows], sems.at[shift * PAIR + i])
            )
    for copy in copies:
        copy.start()
    above = lax.broadcasted_iota(jnp.int32, (half, half), 0)
    across = lax.broadcasted_iota(jnp.int32, (half, half), 1)
    row = lax.broadcasted_iota(jnp.int32, (members, members), 0)
    col = lax.broadcasted_iota(jnp.int32, (members, members), 1)
    eye = jnp.where(row == col, 1.0, 0.0)
    each = range(mine)
    iterate, scale, forcing = [], [], []
    for patch in each:
        packed = before[patch].astype(F32) + after[patch].astype(F32)
        upper = packed[:half]
        mixed = packed[half:members]
        tail = packed[members:]
        diagonal = tail[0:1] + tail[1:2]
        force = jnp.concatenate([tail[2:3] + tail[3:4], tail[4:5] + tail[5:6]], axis=1)
        flipped = mixed.T
        first = jnp.where(above >= across, mixed, flipped)
        second = jnp.where(above < across, mixed, flipped)
        second = jnp.where(above == across, diagonal, second)
        far = jnp.concatenate(
            [
                jnp.concatenate([first, upper], axis=1),
                jnp.concatenate([upper.T, second], axis=1),
            ],
            axis=0,
        )
        system = own[patch, :members, :] + far + (members - 1.0) * eye
        total = jnp.sum(jnp.sum(system * system, axis=0, keepdims=True), axis=1, keepdims=True)
        norm = jnp.sqrt(total)
        scale.append(norm)
        iterate.append(system / norm)
        forcing.append(force + own[patch, members : members + 1, :])
    factor = [1.5 * eye - 0.5 * iterate[p] for p in each]
    root = list(factor)
    parts = [split(factor[p]) for p in each]
    iterate = [product(split(iterate[p]), parts[p]) for p in each]
    for step in range(1, ITERS):
        rooted = [split(root[p]) for p in each]
        iterated = [split(iterate[p]) for p in each]
        factor = [1.5 * eye - 0.5 * product(rooted[p], iterated[p]) for p in each]
        parts = [split(factor[p]) for p in each]
        if step < ITERS - 1:
            iterate = [product(iterated[p], parts[p]) for p in each]
        root = [product(parts[p], rooted[p]) for p in each]
    for copy in copies:
        copy.wait()
    for p in each:
        cols = slice(p * points, (p + 1) * points)
        member = columns[:, cols].astype(F32)
        mean = jnp.sum(member, axis=0, keepdims=True) / members
        rooted = split(root[p])
        spread = product(rooted, split(member - mean))
        force = jnp.broadcast_to(forcing[p], (PAD, members))
        gain = product(split(force), rooted)
        shift = product(split(gain), split(spread))[0:1]
        shift = mean + shift / scale[p]
        out[:, cols] = (
            shift + jnp.sqrt(members - 1.0) / jnp.sqrt(scale[p]) * spread
        ).astype(BF16)


def layout_kernel(pieces, out):
    count, _, width = pieces.shape
    for piece in range(count):
        out[:, piece * width : (piece + 1) * width] = pieces[piece]


def body(state, hx, obs_value, obs_rinv, obs_count, loc_pattern):
    blocks, members, width = hx.shape
    patches, uses = loc_pattern.shape
    mem_total = lax.axis_size("mem")
    mine = patches // mem_total
    local, points = state.shape
    ring = lax.axis_size("lon")
    up = [(i, (i + 1) % ring) for i in range(ring)]
    down = [(j, i) for i, j in up]
    here = lax.axis_index("mem").astype(jnp.int32).reshape(1)
    shape = jax.ShapeDtypeStruct
    padded = members + PAD

    span = points // mem_total
    length = mem_total // PAIR
    swap = [(i, i + 1 - 2 * (i % PAIR)) for i in range(mem_total)]

    pattern = loc_pattern.T
    before = lax.ppermute(pattern, "lon", up)
    after = lax.ppermute(pattern, "lon", down)
    paired = lax.ppermute(state, "mem", swap)
    operands = [
        pltpu.VMEM((padded, uses * width), BF16),
        pltpu.VMEM((members, uses * width), BF16),
    ]
    limit = pltpu.CompilerParams(vmem_limit_bytes=16 * 1024 * 1024)
    gram = 2 * padded * members * uses * width
    pert, weights, innov, own = pl.pallas_call(
        functools.partial(own_kernel, patches),
        out_shape=(
            shape((blocks, members, width), BF16),
            shape((blocks, width), F32),
            shape((blocks, width), F32),
            shape((mine, padded, members), F32),
        ),
        in_specs=[SMEM] + [HBM] * 5,
        out_specs=(VMEM,) * 4,
        scratch_shapes=[
            pltpu.VMEM((blocks, members, width), BF16),
            pltpu.SMEM(obs_count.shape, jnp.int32),
            pltpu.SMEM(pattern.shape, jnp.int32),
            pltpu.VMEM(obs_value.shape, F32),
            pltpu.VMEM(obs_rinv.shape, F32),
        ]
        + operands
        + [pltpu.SemaphoreType.DMA((blocks // CHUNK,)), pltpu.SemaphoreType.DMA((4,))],
        compiler_params=limit,
        cost_estimate=pl.CostEstimate(
            flops=mine * gram, bytes_accessed=2 * hx.size * 2, transcendentals=0
        ),
        name="own_share",
    )(here, *(stay(value) for value in (obs_count, pattern, hx, obs_value, obs_rinv)))
    packed = shape((mine, padded, members // 2), BF16)
    slab = shape((PAIR, local, span), BF16)
    to_before, to_after, *slabs = pl.pallas_call(
        functools.partial(neighbour_kernel, patches),
        out_shape=(packed, packed) + (slab,) * length,
        in_specs=[SMEM] * 3 + [VMEM] * 3 + [HBM] * 2,
        out_specs=(VMEM,) * (2 + length),
        scratch_shapes=operands + [pltpu.SemaphoreType.DMA((PAIR * length,))],
        compiler_params=limit,
        cost_estimate=pl.CostEstimate(
            flops=2 * mine * gram, bytes_accessed=hx.size * 2, transcendentals=0
        ),
        name="neighbour_share",
    )(here, before, after, pert, weights, innov, state, paired)
    from_before = lax.ppermute(to_after, "lon", up)
    from_after = lax.ppermute(to_before, "lon", down)
    for shift in range(1, length):
        turn = [(i, (i + shift * PAIR) % mem_total) for i in range(mem_total)]
        slabs[shift] = lax.ppermute(slabs[shift], "mem", turn)
    updated = pl.pallas_call(
        analysis_kernel,
        out_shape=shape((members, span), BF16),
        in_specs=[SMEM] + [VMEM] * (3 + length),
        out_specs=VMEM,
        scratch_shapes=[
            pltpu.VMEM((members, span), BF16),
            pltpu.SemaphoreType.DMA((PAIR * length,)),
        ],
        compiler_params=limit,
        cost_estimate=pl.CostEstimate(
            flops=mine * 16 * 3 * 2 * members**3, bytes_accessed=2**20, transcendentals=0
        ),
        name="analysis",
    )(here, own, from_before, from_after, *slabs)
    pieces = lax.all_to_all(
        updated.reshape(mem_total, local, span), "mem", split_axis=0, concat_axis=0
    )
    return pl.pallas_call(
        layout_kernel,
        out_shape=shape((local, points), BF16),
        in_specs=[VMEM],
        out_specs=VMEM,
        name="layout",
    )(pieces)


def solution(mesh):
    in_specs = (
        P("mem", "lon"),
        P("lon", None, None),
        P("lon", None),
        P("lon", None),
        P("lon"),
        P("lon", None),
    )
    out_specs = P("mem", "lon")
    return jax.shard_map(body, mesh=mesh, in_specs=in_specs, out_specs=out_specs, check_vma=False)
```

```python
import functools

import jax
import jax.numpy as jnp
from jax import lax
from jax.experimental import pallas as pl
from jax.experimental.pallas import tpu as pltpu
from jax.sharding import PartitionSpec as P

ITERS = 6
PAD = 16
CHUNK = 4
PAIR = 2
F32 = jnp.float32
BF16 = jnp.bfloat16

VMEM = pl.BlockSpec(memory_space=pltpu.VMEM)
SMEM = pl.BlockSpec(memory_space=pltpu.SMEM)
HBM = pl.BlockSpec(memory_space=pltpu.HBM)


def stay(value):
    return pltpu.with_memory_space_constraint(value, pltpu.HBM)


def split(value):
    high = value.astype(BF16)
    return high, (value - high.astype(F32)).astype(BF16)


def product(left, right):
    lhs = jnp.concatenate([left[0], left[0], left[1]], axis=1)
    rhs = jnp.concatenate([right[0], right[1], right[0]], axis=0)
    return jnp.dot(lhs, rhs, preferred_element_type=F32)


def share(pattern, row, side, patches, pert, weights, innov, left, right):
    blocks, members, width = pert.shape
    uses = pattern.shape[0]
    for slot in range(uses):
        position = pattern[slot, row]
        block = position - side * blocks
        here = jnp.logical_and(block >= 0, block < blocks)
        block = jnp.clip(block, 0, blocks - 1)
        spot = jnp.full((1, width), position, jnp.int32).astype(F32)
        rank = jnp.full((1, width), row, jnp.int32).astype(F32)
        offset = (spot + 0.5) / blocks - 1.0 - (rank + 0.5) / patches
        taper = jnp.exp(-0.5 * offset * offset) * jnp.where(here, 1.0, 0.0)
        cols = slice(slot * width, (slot + 1) * width)
        picked = pert[block]
        weight = taper * weights[pl.ds(block, 1), :]
        left[:members, cols] = (weight * picked.astype(F32)).astype(BF16)
        vector = taper * innov[pl.ds(block, 1), :]
        left[members:, cols] = jnp.broadcast_to(vector, (PAD, width)).astype(BF16)
        right[:, cols] = picked
    return lax.dot_general(
        left[...], right[...], (((1,), (1,)), ((), ())), preferred_element_type=F32
    )


def own_kernel(
    patches,
    here,
    count_all,
    pattern_all,
    hx,
    value_all,
    rinv_all,
    pert,
    weights,
    innov,
    own,
    raw,
    count,
    pattern,
    value,
    rinv,
    left,
    right,
    sems,
    small,
):
    blocks, members, width = raw.shape
    smalls = [
        pltpu.make_async_copy(source, target, small.at[i])
        for i, (source, target) in enumerate(
            ((count_all, count), (value_all, value), (rinv_all, rinv), (pattern_all, pattern))
        )
    ]
    copies = [
        pltpu.make_async_copy(hx.at[pl.ds(i, CHUNK)], raw.at[pl.ds(i, CHUNK)], sems.at[i // CHUNK])
        for i in range(0, blocks, CHUNK)
    ]
    for copy in smalls + copies:
        copy.start()
    for copy in smalls:
        copy.wait()
    lane = lax.broadcasted_iota(jnp.int32, (1, width), 1)
    for block in range(blocks):
        if block % CHUNK == 0:
            copies[block // CHUNK].wait()
        member = raw[block].astype(F32)
        mean = jnp.sum(member, axis=0, keepdims=True) / members
        pert[block] = (member - mean).astype(BF16)
        weight = jnp.where(lane < count[block], rinv[block : block + 1, :], 0.0)
        gap = weight * (value[block : block + 1, :] - mean)
        weights[block : block + 1, :] = weight.astype(BF16).astype(F32)
        innov[block : block + 1, :] = gap
    mine = own.shape[0]
    for patch in range(mine):
        row = here[0] * mine + patch
        own[patch] = share(pattern, row, 1, patches, pert, weights, innov, left, right)


def neighbour_kernel(
    patches,
    here,
    before,
    after,
    pert,
    weights,
    innov,
    state,
    paired,
    to_before,
    to_after,
    *rest,
):
    slabs, (left, right, sems) = rest[:-3], rest[-3:]
    span = slabs[0].shape[2]
    length = len(slabs)
    layer, side = here[0] // PAIR, here[0] % PAIR
    moves = []
    for shift, slab in enumerate(slabs):
        target = lax.rem(layer + shift, length) * PAIR + side
        cols = pl.ds(pl.multiple_of(target * span, span), span)
        moves.append((state.at[:, cols], slab.at[side]))
        moves.append((paired.at[:, cols], slab.at[1 - side]))
    moves = [pltpu.make_async_copy(*move, sems.at[i]) for i, move in enumerate(moves)]
    for move in moves:
        move.start()
    members = pert.shape[1]
    half = members // 2
    mine = to_before.shape[0]
    above = lax.broadcasted_iota(jnp.int32, (half, half), 0)
    across = lax.broadcasted_iota(jnp.int32, (half, half), 1)
    for pattern, side, out in ((before, 2, to_before), (after, 0, to_after)):
        for patch in range(mine):
            row = here[0] * mine + patch
            part = share(pattern, row, side, patches, pert, weights, innov, left, right)
            corner = part[half:members, half:]
            out[patch, :half, :] = part[:half, half:].astype(BF16)
            out[patch, half:members, :] = jnp.where(
                above >= across, part[:half, :half], corner
            ).astype(BF16)
            diagonal = jnp.sum(jnp.where(above == across, corner, 0.0), axis=0, keepdims=True)
            force = part[members : members + 1]
            rows = [diagonal, force[:, :half], force[:, half:]]
            parts = [split(value) for value in rows]
            index = lax.broadcasted_iota(jnp.int32, (PAD, half), 0)
            tail = jnp.zeros((PAD, half), F32)
            for i, (high, low) in enumerate(parts):
                tail = jnp.where(index == 2 * i, high.astype(F32), tail)
                tail = jnp.where(index == 2 * i + 1, low.astype(F32), tail)
            out[patch, members:, :] = tail.astype(BF16)
    for move in moves:
        move.wait()


def total(value):
    return jnp.sum(jnp.sum(value, axis=0, keepdims=True), axis=1, keepdims=True)


def root_kernel(own, before, after, root_out, rows_out):
    mine, _, members = own.shape
    half = members // 2
    above = lax.broadcasted_iota(jnp.int32, (half, half), 0)
    across = lax.broadcasted_iota(jnp.int32, (half, half), 1)
    row = lax.broadcasted_iota(jnp.int32, (members, members), 0)
    col = lax.broadcasted_iota(jnp.int32, (members, members), 1)
    diagonal = row == col

    def less(value, amount):
        return value - jnp.where(diagonal, amount, 0.0)

    def dot(left, right):
        return jnp.dot(left, right, preferred_element_type=F32)

    each = range(mine)
    rest, share_of, scale, forcing = [], [], [], []
    base = members - 1.0
    for patch in each:
        packed = before[patch].astype(F32) + after[patch].astype(F32)
        upper = packed[:half]
        mixed = packed[half:members]
        last = packed[members:]
        corner = last[0:1] + last[1:2]
        force = jnp.concatenate([last[2:3] + last[3:4], last[4:5] + last[5:6]], axis=1)
        flipped = mixed.T
        first = jnp.where(above >= across, mixed, flipped)
        second = jnp.where(above < across, mixed, flipped)
        second = jnp.where(above == across, corner, second)
        far = jnp.concatenate(
            [
                jnp.concatenate([first, upper], axis=1),
                jnp.concatenate([upper.T, second], axis=1),
            ],
            axis=0,
        )
        grams = own[patch, :members, :] + far
        trace = total(jnp.where(diagonal, grams, 0.0))
        norm = jnp.sqrt(total(grams * grams) + 2.0 * base * trace + base * base * members)
        scale.append(norm)
        forcing.append(force + own[patch, members : members + 1, :])
        share_of.append((trace / members + base) / norm)
        rest.append(less(grams, trace / members) * (1.0 / norm))
    lead, tail = [None] * mine, [None] * mine
    for step in range(ITERS):
        final = step == ITERS - 1
        small = [rest[p].astype(BF16) for p in each]
        squares, crosses = [None] * mine, [None] * mine
        for p in each:
            if step == 0:
                squares[p] = dot(small[p], small[p])
            elif final:
                crosses[p] = dot(tail[p].astype(BF16), small[p])
            else:
                both = dot(jnp.concatenate([small[p], tail[p].astype(BF16)], axis=0), small[p])
                squares[p], crosses[p] = both[:members], both[members:]
        for p in each:
            factor = 1.5 - 0.5 * share_of[p]
            if step == 0:
                lead[p], tail[p] = factor, -0.5 * rest[p]
            else:
                part = total(tail[p] * rest[p]) / members
                tail[p] = (
                    factor * tail[p] - 0.5 * lead[p] * rest[p] - 0.5 * less(crosses[p], part)
                )
                lead[p] = factor * lead[p] - 0.5 * part
        if final:
            break
        for p in each:
            squares[p] = less(squares[p], total(rest[p] * rest[p]) / members)
        cubes = [dot(squares[p].astype(BF16), small[p]) for p in each]
        for p in each:
            m = share_of[p]
            factor = 1.5 - 0.5 * m
            part = total(rest[p] * rest[p]) / members
            third = total(rest[p] * squares[p]) / members
            share_of[p] = m * factor * factor + (0.25 * m - factor) * part + 0.25 * third
            rest[p] = (
                (factor * factor - m * factor + 0.25 * part) * rest[p]
                + (0.25 * m - factor) * squares[p]
                + 0.25 * less(cubes[p], third)
            )
    for p in each:
        high = tail[p].astype(BF16)
        root_out[p] = high
        force = jnp.broadcast_to(forcing[p], (PAD, members))
        gain = (lead[p] * force + dot(force.astype(BF16), high)) / scale[p]
        index = lax.broadcasted_iota(jnp.int32, (PAD, members), 0)
        spread = jnp.sqrt(base) / jnp.sqrt(scale[p])
        rows_out[p] = jnp.where(index == 0, gain, jnp.where(index == 1, lead[p], spread))


def apply_kernel(here, root, rows, *rest):
    slabs, (out, columns) = rest[:-2], rest[-2:]
    mine, members, _ = root.shape
    points = out.shape[1] // mine
    length = len(slabs)
    _, local, _ = slabs[0].shape
    for shift, slab in enumerate(slabs):
        source = lax.rem(here[0] // PAIR - shift + length, length)
        for i in range(PAIR):
            place = pl.ds(pl.multiple_of((source * PAIR + i) * local, local), local)
            columns[place, :] = slab[i]
    for p in range(mine):
        cols = slice(p * points, (p + 1) * points)
        member = columns[:, cols].astype(F32)
        mean = jnp.sum(member, axis=0, keepdims=True) / members
        deviation = member - mean
        spread = rows[p, 1:2, :points] * deviation + jnp.dot(
            root[p], deviation.astype(BF16), preferred_element_type=F32
        )
        shift = mean + product(split(rows[p]), split(spread))[0:1]
        out[:, cols] = (shift + rows[p, 2:3, :points] * spread).astype(BF16)


def layout_kernel(pieces, out, sems):
    count, _, width = pieces.shape
    copies = [
        pltpu.make_async_copy(
            pieces.at[i], out.at[:, pl.ds(i * width, width)], sems.at[i]
        )
        for i in range(count)
    ]
    for copy in copies:
        copy.start()
    for copy in copies:
        copy.wait()


def body(state, hx, obs_value, obs_rinv, obs_count, loc_pattern):
    blocks, members, width = hx.shape
    patches, uses = loc_pattern.shape
    mem_total = lax.axis_size("mem")
    mine = patches // mem_total
    local, points = state.shape
    ring = lax.axis_size("lon")
    up = [(i, (i + 1) % ring) for i in range(ring)]
    down = [(j, i) for i, j in up]
    here = lax.axis_index("mem").astype(jnp.int32).reshape(1)
    shape = jax.ShapeDtypeStruct
    padded = members + PAD

    span = points // mem_total
    length = mem_total // PAIR
    swap = [(i, i + 1 - 2 * (i % PAIR)) for i in range(mem_total)]

    pattern = loc_pattern.T
    before = lax.ppermute(pattern, "lon", up)
    after = lax.ppermute(pattern, "lon", down)
    paired = lax.ppermute(state, "mem", swap)
    operands = [
        pltpu.VMEM((padded, uses * width), BF16),
        pltpu.VMEM((members, uses * width), BF16),
    ]
    limit = pltpu.CompilerParams(vmem_limit_bytes=16 * 1024 * 1024)
    gram = 2 * padded * members * uses * width
    pert, weights, innov, own = pl.pallas_call(
        functools.partial(own_kernel, patches),
        out_shape=(
            shape((blocks, members, width), BF16),
            shape((blocks, width), F32),
            shape((blocks, width), F32),
            shape((mine, padded, members), F32),
        ),
        in_specs=[SMEM] + [HBM] * 5,
        out_specs=(VMEM,) * 4,
        scratch_shapes=[
            pltpu.VMEM((blocks, members, width), BF16),
            pltpu.SMEM(obs_count.shape, jnp.int32),
            pltpu.SMEM(pattern.shape, jnp.int32),
            pltpu.VMEM(obs_value.shape, F32),
            pltpu.VMEM(obs_rinv.shape, F32),
        ]
        + operands
        + [pltpu.SemaphoreType.DMA((blocks // CHUNK,)), pltpu.SemaphoreType.DMA((4,))],
        compiler_params=limit,
        cost_estimate=pl.CostEstimate(
            flops=mine * gram, bytes_accessed=2 * hx.size * 2, transcendentals=0
        ),
        name="own_share",
    )(here, *(stay(value) for value in (obs_count, pattern, hx, obs_value, obs_rinv)))
    packed = shape((mine, padded, members // 2), BF16)
    slab = shape((PAIR, local, span), BF16)
    to_before, to_after, *slabs = pl.pallas_call(
        functools.partial(neighbour_kernel, patches),
        out_shape=(packed, packed) + (slab,) * length,
        in_specs=[SMEM] * 3 + [VMEM] * 3 + [HBM] * 2,
        out_specs=(VMEM,) * (2 + length),
        scratch_shapes=operands + [pltpu.SemaphoreType.DMA((PAIR * length,))],
        compiler_params=limit,
        cost_estimate=pl.CostEstimate(
            flops=2 * mine * gram, bytes_accessed=hx.size * 2, transcendentals=0
        ),
        name="neighbour_share",
    )(here, before, after, pert, weights, innov, state, paired)
    from_before = lax.ppermute(to_after, "lon", up)
    from_after = lax.ppermute(to_before, "lon", down)
    for shift in range(1, length):
        turn = [(i, (i + shift * PAIR) % mem_total) for i in range(mem_total)]
        slabs[shift] = lax.ppermute(slabs[shift], "mem", turn)
    root, rows = pl.pallas_call(
        root_kernel,
        out_shape=(shape((mine, members, members), BF16), shape((mine, PAD, members), F32)),
        in_specs=[VMEM] * 3,
        out_specs=(VMEM,) * 2,
        compiler_params=limit,
        cost_estimate=pl.CostEstimate(
            flops=mine * 15 * 2 * members**3, bytes_accessed=2**20, transcendentals=0
        ),
        name="root",
    )(own, from_before, from_after)
    updated = pl.pallas_call(
        apply_kernel,
        out_shape=shape((members, span), BF16),
        in_specs=[SMEM] + [VMEM] * (2 + length),
        out_specs=VMEM,
        scratch_shapes=[pltpu.VMEM((members, span), BF16)],
        compiler_params=limit,
        cost_estimate=pl.CostEstimate(
            flops=2 * members**2 * span, bytes_accessed=2**19, transcendentals=0
        ),
        name="apply",
    )(here, root, rows, *slabs)
    pieces = lax.all_to_all(
        updated.reshape(mem_total, local, span), "mem", split_axis=0, concat_axis=0
    )
    return pl.pallas_call(
        layout_kernel,
        out_shape=shape((local, points), BF16),
        in_specs=[pl.BlockSpec(memory_space=pl.ANY)],
        out_specs=HBM,
        scratch_shapes=[pltpu.SemaphoreType.DMA((mem_total,))],
        name="layout",
    )(pieces)


def solution(mesh):
    in_specs = (
        P("mem", "lon"),
        P("lon", None, None),
        P("lon", None),
        P("lon", None),
        P("lon"),
        P("lon", None),
    )
    out_specs = P("mem", "lon")
    return jax.shard_map(body, mesh=mesh, in_specs=in_specs, out_specs=out_specs, check_vma=False)
```

```python
import functools

import jax
import jax.numpy as jnp
from jax import lax
from jax.experimental import pallas as pl
from jax.experimental.pallas import tpu as pltpu
from jax.sharding import PartitionSpec as P

ITERS = 6
PAD = 16
CHUNK = 4
PAIR = 2
F32 = jnp.float32
BF16 = jnp.bfloat16

VMEM = pl.BlockSpec(memory_space=pltpu.VMEM)
SMEM = pl.BlockSpec(memory_space=pltpu.SMEM)
HBM = pl.BlockSpec(memory_space=pltpu.HBM)


def stay(value):
    return pltpu.with_memory_space_constraint(value, pltpu.HBM)


def split(value):
    high = value.astype(BF16)
    return high, (value - high.astype(F32)).astype(BF16)


def product(left, right):
    lhs = jnp.concatenate([left[0], left[0], left[1]], axis=1)
    rhs = jnp.concatenate([right[0], right[1], right[0]], axis=0)
    return jnp.dot(lhs, rhs, preferred_element_type=F32)


def share(pattern, row, side, patches, pert, weights, innov, left, right):
    blocks, members, width = pert.shape
    uses = pattern.shape[0]
    for slot in range(uses):
        position = pattern[slot, row]
        block = position - side * blocks
        here = jnp.logical_and(block >= 0, block < blocks)
        block = jnp.clip(block, 0, blocks - 1)
        spot = jnp.full((1, width), position, jnp.int32).astype(F32)
        rank = jnp.full((1, width), row, jnp.int32).astype(F32)
        offset = (spot + 0.5) / blocks - 1.0 - (rank + 0.5) / patches
        taper = jnp.exp(-0.5 * offset * offset) * jnp.where(here, 1.0, 0.0)
        cols = slice(slot * width, (slot + 1) * width)
        picked = pert[block]
        weight = taper * weights[pl.ds(block, 1), :]
        left[:members, cols] = (weight * picked.astype(F32)).astype(BF16)
        vector = taper * innov[pl.ds(block, 1), :]
        left[members:, cols] = jnp.broadcast_to(vector, (PAD, width)).astype(BF16)
        right[:, cols] = picked
    return lax.dot_general(
        left[...], right[...], (((1,), (1,)), ((), ())), preferred_element_type=F32
    )


def perturb_kernel(
    count_all, hx, value_all, rinv_all, pert, weights, innov, raw, count, value, rinv, sems, small
):
    blocks, members, width = raw.shape
    smalls = [
        pltpu.make_async_copy(source, target, small.at[i])
        for i, (source, target) in enumerate(
            ((count_all, count), (value_all, value), (rinv_all, rinv))
        )
    ]
    copies = [
        pltpu.make_async_copy(hx.at[pl.ds(i, CHUNK)], raw.at[pl.ds(i, CHUNK)], sems.at[i // CHUNK])
        for i in range(0, blocks, CHUNK)
    ]
    for copy in smalls + copies:
        copy.start()
    for copy in smalls:
        copy.wait()
    lane = lax.broadcasted_iota(jnp.int32, (1, width), 1)
    for block in range(blocks):
        if block % CHUNK == 0:
            copies[block // CHUNK].wait()
        member = raw[block].astype(F32)
        mean = jnp.sum(member, axis=0, keepdims=True) / members
        pert[block] = (member - mean).astype(BF16)
        weight = jnp.where(lane < count[block], rinv[block : block + 1, :], 0.0)
        gap = weight * (value[block : block + 1, :] - mean)
        weights[block : block + 1, :] = weight.astype(BF16).astype(F32)
        innov[block : block + 1, :] = gap


def own_kernel(patches, here, pattern, pert, weights, innov, sent, own, left, right):
    mine = own.shape[0]
    for patch in range(mine):
        row = here[0] * mine + patch
        own[patch] = share(pattern, row, 1, patches, pert, weights, innov, left, right)


def neighbour_kernel(
    patches,
    here,
    before,
    after,
    pert,
    weights,
    innov,
    state,
    paired,
    to_before,
    to_after,
    *rest,
):
    slabs, (left, right, sems) = rest[:-3], rest[-3:]
    span = slabs[0].shape[2]
    length = len(slabs)
    layer, side = here[0] // PAIR, here[0] % PAIR
    moves = []
    for shift, slab in enumerate(slabs):
        target = lax.rem(layer + shift, length) * PAIR + side
        cols = pl.ds(pl.multiple_of(target * span, span), span)
        moves.append((state.at[:, cols], slab.at[side]))
        moves.append((paired.at[:, cols], slab.at[1 - side]))
    moves = [pltpu.make_async_copy(*move, sems.at[i]) for i, move in enumerate(moves)]
    for move in moves:
        move.start()
    members = pert.shape[1]
    half = members // 2
    mine = to_before.shape[0]
    above = lax.broadcasted_iota(jnp.int32, (half, half), 0)
    across = lax.broadcasted_iota(jnp.int32, (half, half), 1)
    for pattern, side, out in ((before, 2, to_before), (after, 0, to_after)):
        for patch in range(mine):
            row = here[0] * mine + patch
            part = share(pattern, row, side, patches, pert, weights, innov, left, right)
            corner = part[half:members, half:]
            out[patch, :half, :] = part[:half, half:].astype(BF16)
            out[patch, half:members, :] = jnp.where(
                above >= across, part[:half, :half], corner
            ).astype(BF16)
            diagonal = jnp.sum(jnp.where(above == across, corner, 0.0), axis=0, keepdims=True)
            force = part[members : members + 1]
            rows = [diagonal, force[:, :half], force[:, half:]]
            parts = [split(value) for value in rows]
            index = lax.broadcasted_iota(jnp.int32, (PAD, half), 0)
            tail = jnp.zeros((PAD, half), F32)
            for i, (high, low) in enumerate(parts):
                tail = jnp.where(index == 2 * i, high.astype(F32), tail)
                tail = jnp.where(index == 2 * i + 1, low.astype(F32), tail)
            out[patch, members:, :] = tail.astype(BF16)
    for move in moves:
        move.wait()


def total(value):
    return jnp.sum(jnp.sum(value, axis=0, keepdims=True), axis=1, keepdims=True)


def root_kernel(own, before, after, root_out, rows_out):
    mine, _, members = own.shape
    half = members // 2
    above = lax.broadcasted_iota(jnp.int32, (half, half), 0)
    across = lax.broadcasted_iota(jnp.int32, (half, half), 1)
    row = lax.broadcasted_iota(jnp.int32, (members, members), 0)
    col = lax.broadcasted_iota(jnp.int32, (members, members), 1)
    diagonal = row == col

    def less(value, amount):
        return value - jnp.where(diagonal, amount, 0.0)

    def dot(left, right):
        return jnp.dot(left, right, preferred_element_type=F32)

    each = range(mine)
    rest, share_of, scale, forcing = [], [], [], []
    base = members - 1.0
    for patch in each:
        packed = before[patch].astype(F32) + after[patch].astype(F32)
        upper = packed[:half]
        mixed = packed[half:members]
        last = packed[members:]
        corner = last[0:1] + last[1:2]
        force = jnp.concatenate([last[2:3] + last[3:4], last[4:5] + last[5:6]], axis=1)
        flipped = mixed.T
        first = jnp.where(above >= across, mixed, flipped)
        second = jnp.where(above < across, mixed, flipped)
        second = jnp.where(above == across, corner, second)
        far = jnp.concatenate(
            [
                jnp.concatenate([first, upper], axis=1),
                jnp.concatenate([upper.T, second], axis=1),
            ],
            axis=0,
        )
        grams = own[patch, :members, :] + far
        trace = total(jnp.where(diagonal, grams, 0.0))
        norm = jnp.sqrt(total(grams * grams) + 2.0 * base * trace + base * base * members)
        scale.append(norm)
        forcing.append(force + own[patch, members : members + 1, :])
        share_of.append((trace / members + base) / norm)
        rest.append(less(grams, trace / members) * (1.0 / norm))
    lead, tail = [None] * mine, [None] * mine
    for step in range(ITERS):
        final = step == ITERS - 1
        small = [rest[p].astype(BF16) for p in each]
        squares, crosses = [None] * mine, [None] * mine
        for p in each:
            if step == 0:
                squares[p] = dot(small[p], small[p])
            elif final:
                crosses[p] = dot(tail[p].astype(BF16), small[p])
            else:
                both = dot(jnp.concatenate([small[p], tail[p].astype(BF16)], axis=0), small[p])
                squares[p], crosses[p] = both[:members], both[members:]
        for p in each:
            factor = 1.5 - 0.5 * share_of[p]
            if step == 0:
                lead[p], tail[p] = factor, -0.5 * rest[p]
            else:
                part = total(tail[p] * rest[p]) / members
                tail[p] = (
                    factor * tail[p] - 0.5 * lead[p] * rest[p] - 0.5 * less(crosses[p], part)
                )
                lead[p] = factor * lead[p] - 0.5 * part
        if final:
            break
        for p in each:
            squares[p] = less(squares[p], total(rest[p] * rest[p]) / members)
        cubes = [dot(squares[p].astype(BF16), small[p]) for p in each]
        for p in each:
            m = share_of[p]
            factor = 1.5 - 0.5 * m
            part = total(rest[p] * rest[p]) / members
            third = total(rest[p] * squares[p]) / members
            share_of[p] = m * factor * factor + (0.25 * m - factor) * part + 0.25 * third
            rest[p] = (
                (factor * factor - m * factor + 0.25 * part) * rest[p]
                + (0.25 * m - factor) * squares[p]
                + 0.25 * less(cubes[p], third)
            )
    for p in each:
        high = tail[p].astype(BF16)
        root_out[p] = high
        force = jnp.broadcast_to(forcing[p], (PAD, members))
        gain = (lead[p] * force + dot(force.astype(BF16), high)) / scale[p]
        index = lax.broadcasted_iota(jnp.int32, (PAD, members), 0)
        spread = jnp.sqrt(base) / jnp.sqrt(scale[p])
        rows_out[p] = jnp.where(index == 0, gain, jnp.where(index == 1, lead[p], spread))


def apply_kernel(here, root, rows, *rest):
    slabs, (out, columns) = rest[:-2], rest[-2:]
    mine, members, _ = root.shape
    points = out.shape[1] // mine
    length = len(slabs)
    _, local, _ = slabs[0].shape
    for shift, slab in enumerate(slabs):
        source = lax.rem(here[0] // PAIR - shift + length, length)
        for i in range(PAIR):
            place = pl.ds(pl.multiple_of((source * PAIR + i) * local, local), local)
            columns[place, :] = slab[i]
    for p in range(mine):
        cols = slice(p * points, (p + 1) * points)
        member = columns[:, cols].astype(F32)
        mean = jnp.sum(member, axis=0, keepdims=True) / members
        deviation = member - mean
        spread = rows[p, 1:2, :points] * deviation + jnp.dot(
            root[p], deviation.astype(BF16), preferred_element_type=F32
        )
        shift = mean + product(split(rows[p]), split(spread))[0:1]
        out[:, cols] = (shift + rows[p, 2:3, :points] * spread).astype(BF16)


def body(state, hx, obs_value, obs_rinv, obs_count, loc_pattern):
    blocks, members, width = hx.shape
    patches, uses = loc_pattern.shape
    mem_total = lax.axis_size("mem")
    mine = patches // mem_total
    local, points = state.shape
    ring = lax.axis_size("lon")
    up = [(i, (i + 1) % ring) for i in range(ring)]
    down = [(j, i) for i, j in up]
    here = lax.axis_index("mem").astype(jnp.int32).reshape(1)
    shape = jax.ShapeDtypeStruct
    padded = members + PAD

    span = points // mem_total
    length = mem_total // PAIR
    swap = [(i, i + 1 - 2 * (i % PAIR)) for i in range(mem_total)]

    pattern = loc_pattern.T
    before = lax.ppermute(pattern, "lon", up)
    after = lax.ppermute(pattern, "lon", down)
    paired = lax.ppermute(state, "mem", swap)
    operands = [
        pltpu.VMEM((padded, uses * width), BF16),
        pltpu.VMEM((members, uses * width), BF16),
    ]
    limit = pltpu.CompilerParams(vmem_limit_bytes=16 * 1024 * 1024)
    gram = 2 * padded * members * uses * width
    pert, weights, innov = pl.pallas_call(
        perturb_kernel,
        out_shape=(
            shape((blocks, members, width), BF16),
            shape((blocks, width), F32),
            shape((blocks, width), F32),
        ),
        in_specs=[HBM] * 4,
        out_specs=(VMEM,) * 3,
        scratch_shapes=[
            pltpu.VMEM((blocks, members, width), BF16),
            pltpu.SMEM(obs_count.shape, jnp.int32),
            pltpu.VMEM(obs_value.shape, F32),
            pltpu.VMEM(obs_rinv.shape, F32),
            pltpu.SemaphoreType.DMA((blocks // CHUNK,)),
            pltpu.SemaphoreType.DMA((3,)),
        ],
        compiler_params=limit,
        cost_estimate=pl.CostEstimate(
            flops=hx.size * 4, bytes_accessed=2 * hx.size * 2, transcendentals=0
        ),
        name="perturb",
    )(*(stay(value) for value in (obs_count, hx, obs_value, obs_rinv)))
    packed = shape((mine, padded, members // 2), BF16)
    slab = shape((PAIR, local, span), BF16)
    to_before, to_after, *slabs = pl.pallas_call(
        functools.partial(neighbour_kernel, patches),
        out_shape=(packed, packed) + (slab,) * length,
        in_specs=[SMEM] * 3 + [VMEM] * 3 + [HBM] * 2,
        out_specs=(VMEM,) * (2 + length),
        scratch_shapes=operands + [pltpu.SemaphoreType.DMA((PAIR * length,))],
        compiler_params=limit,
        cost_estimate=pl.CostEstimate(
            flops=2 * mine * gram, bytes_accessed=hx.size * 2, transcendentals=0
        ),
        name="neighbour_share",
    )(here, before, after, pert, weights, innov, state, paired)
    own = pl.pallas_call(
        functools.partial(own_kernel, patches),
        out_shape=shape((mine, padded, members), F32),
        in_specs=[SMEM] * 2 + [VMEM] * 3 + [pl.BlockSpec(memory_space=pl.ANY)],
        out_specs=VMEM,
        scratch_shapes=operands,
        compiler_params=limit,
        cost_estimate=pl.CostEstimate(
            flops=mine * gram, bytes_accessed=2 * hx.size, transcendentals=0
        ),
        name="own_share",
    )(here, pattern, pert, weights, innov, to_before)
    from_before = lax.ppermute(to_after, "lon", up)
    from_after = lax.ppermute(to_before, "lon", down)
    for shift in range(1, length):
        turn = [(i, (i + shift * PAIR) % mem_total) for i in range(mem_total)]
        slabs[shift] = lax.ppermute(slabs[shift], "mem", turn)
    root, rows = pl.pallas_call(
        root_kernel,
        out_shape=(shape((mine, members, members), BF16), shape((mine, PAD, members), F32)),
        in_specs=[VMEM] * 3,
        out_specs=(VMEM,) * 2,
        compiler_params=limit,
        cost_estimate=pl.CostEstimate(
            flops=mine * 15 * 2 * members**3, bytes_accessed=2**20, transcendentals=0
        ),
        name="root",
    )(own, from_before, from_after)
    updated = pl.pallas_call(
        apply_kernel,
        out_shape=shape((members, span), BF16),
        in_specs=[SMEM] + [VMEM] * (2 + length),
        out_specs=VMEM,
        scratch_shapes=[pltpu.VMEM((members, span), BF16)],
        compiler_params=limit,
        cost_estimate=pl.CostEstimate(
            flops=2 * members**2 * span, bytes_accessed=2**19, transcendentals=0
        ),
        name="apply",
    )(here, root, rows, *slabs)
    pieces = lax.all_to_all(
        updated.reshape(mem_total, local, span), "mem", split_axis=0, concat_axis=0
    )
    return jnp.swapaxes(pieces, 0, 1).reshape(local, points)


def solution(mesh):
    in_specs = (
        P("mem", "lon"),
        P("lon", None, None),
        P("lon", None),
        P("lon", None),
        P("lon"),
        P("lon", None),
    )
    out_specs = P("mem", "lon")
    return jax.shard_map(body, mesh=mesh, in_specs=in_specs, out_specs=out_specs, check_vma=False)
```

```python
import functools

import jax
import jax.numpy as jnp
from jax import lax
from jax.experimental import pallas as pl
from jax.experimental.pallas import tpu as pltpu
from jax.sharding import PartitionSpec as P

ITERS = 6
PAD = 16
CHUNK = 4
PAIR = 2
F32 = jnp.float32
BF16 = jnp.bfloat16

VMEM = pl.BlockSpec(memory_space=pltpu.VMEM)
SMEM = pl.BlockSpec(memory_space=pltpu.SMEM)
HBM = pl.BlockSpec(memory_space=pltpu.HBM)


def stay(value):
    return pltpu.with_memory_space_constraint(value, pltpu.HBM)


def split(value):
    high = value.astype(BF16)
    return high, (value - high.astype(F32)).astype(BF16)


def product(left, right):
    lhs = jnp.concatenate([left[0], left[0], left[1]], axis=1)
    rhs = jnp.concatenate([right[0], right[1], right[0]], axis=0)
    return jnp.dot(lhs, rhs, preferred_element_type=F32)


def share(pattern, row, side, patches, pert, weights, innov):
    blocks, _, width = pert.shape
    left, right = [], []
    for slot in range(pattern.shape[0]):
        position = pattern[slot, row]
        block = position - side * blocks
        here = jnp.logical_and(block >= 0, block < blocks)
        block = jnp.clip(block, 0, blocks - 1)
        spot = jnp.full((1, width), position, jnp.int32).astype(F32)
        rank = jnp.full((1, width), row, jnp.int32).astype(F32)
        offset = (spot + 0.5) / blocks - 1.0 - (rank + 0.5) / patches
        taper = jnp.exp(-0.5 * offset * offset) * jnp.where(here, 1.0, 0.0)
        picked = pert[block]
        weight = (taper * weights[pl.ds(block, 1), :]).astype(BF16)
        vector = jnp.broadcast_to(taper * innov[pl.ds(block, 1), :], (PAD, width)).astype(BF16)
        left.append(jnp.concatenate([weight * picked, vector], axis=0))
        right.append(picked)
    return lax.dot_general(
        jnp.concatenate(left, axis=1),
        jnp.concatenate(right, axis=1),
        (((1,), (1,)), ((), ())),
        preferred_element_type=F32,
    )


def perturb_kernel(
    count_all, hx, value_all, rinv_all, pert, weights, innov, raw, count, value, rinv, sems, small
):
    blocks, members, width = raw.shape
    smalls = [
        pltpu.make_async_copy(source, target, small.at[i])
        for i, (source, target) in enumerate(
            ((count_all, count), (value_all, value), (rinv_all, rinv))
        )
    ]
    copies = [
        pltpu.make_async_copy(hx.at[pl.ds(i, CHUNK)], raw.at[pl.ds(i, CHUNK)], sems.at[i // CHUNK])
        for i in range(0, blocks, CHUNK)
    ]
    for copy in smalls + copies:
        copy.start()
    for copy in smalls:
        copy.wait()
    lane = lax.broadcasted_iota(jnp.int32, (1, width), 1)
    for block in range(blocks):
        if block % CHUNK == 0:
            copies[block // CHUNK].wait()
        member = raw[block].astype(F32)
        mean = jnp.sum(member, axis=0, keepdims=True) / members
        pert[block] = (member - mean).astype(BF16)
        weight = jnp.where(lane < count[block], rinv[block : block + 1, :], 0.0)
        gap = weight * (value[block : block + 1, :] - mean)
        weights[block : block + 1, :] = weight.astype(BF16).astype(F32)
        innov[block : block + 1, :] = gap


def own_kernel(patches, here, pattern, pert, weights, innov, sent, own):
    mine = own.shape[0]
    for patch in range(mine):
        row = here[0] * mine + patch
        own[patch] = share(pattern, row, 1, patches, pert, weights, innov)


def pack(part, out, patch):
    _, padded, half = out.shape
    members = padded - PAD
    above = lax.broadcasted_iota(jnp.int32, (half, half), 0)
    across = lax.broadcasted_iota(jnp.int32, (half, half), 1)
    corner = part[half:members, half:]
    out[patch, :half, :] = part[:half, half:].astype(BF16)
    out[patch, half:members, :] = jnp.where(above >= across, part[:half, :half], corner).astype(
        BF16
    )
    diagonal = jnp.sum(jnp.where(above == across, corner, 0.0), axis=0, keepdims=True)
    force = part[members : members + 1]
    index = lax.broadcasted_iota(jnp.int32, (PAD, half), 0)
    tail = jnp.zeros((PAD, half), F32)
    for i, value in enumerate((diagonal, force[:, :half], force[:, half:])):
        high, low = split(value)
        tail = jnp.where(index == 2 * i, high.astype(F32), tail)
        tail = jnp.where(index == 2 * i + 1, low.astype(F32), tail)
    out[patch, members:, :] = tail.astype(BF16)


def far_kernel(patches, side, here, pattern, pert, weights, innov, out):
    mine = out.shape[0]
    for patch in range(mine):
        row = here[0] * mine + patch
        pack(share(pattern, row, here[side], patches, pert, weights, innov), out, patch)


def near_kernel(patches, side, here, pattern, pert, weights, innov, state, paired, sent, out, *rest):
    slabs, sems = rest[:-1], rest[-1]
    span = slabs[0].shape[2]
    length = len(slabs)
    layer, place = here[0] // PAIR, here[0] % PAIR
    moves = []
    for shift, slab in enumerate(slabs):
        target = lax.rem(layer + shift, length) * PAIR + place
        cols = pl.ds(pl.multiple_of(target * span, span), span)
        moves.append((state.at[:, cols], slab.at[place]))
        moves.append((paired.at[:, cols], slab.at[1 - place]))
    moves = [pltpu.make_async_copy(*move, sems.at[i]) for i, move in enumerate(moves)]
    for move in moves:
        move.start()
    far_kernel(patches, side, here, pattern, pert, weights, innov, out)
    for move in moves:
        move.wait()


def total(value):
    return jnp.sum(jnp.sum(value, axis=0, keepdims=True), axis=1, keepdims=True)


def root_kernel(own, before, after, root_out, rows_out):
    mine, _, members = own.shape
    half = members // 2
    above = lax.broadcasted_iota(jnp.int32, (half, half), 0)
    across = lax.broadcasted_iota(jnp.int32, (half, half), 1)
    row = lax.broadcasted_iota(jnp.int32, (members, members), 0)
    col = lax.broadcasted_iota(jnp.int32, (members, members), 1)
    diagonal = row == col

    def dot(left, right):
        return jnp.dot(left, right, preferred_element_type=F32)

    each = range(mine)
    rest, factor, scale, forcing = [], [], [], []
    base = members - 1.0
    for patch in each:
        packed = before[patch].astype(F32) + after[patch].astype(F32)
        upper = packed[:half]
        mixed = packed[half:members]
        last = packed[members:]
        corner = last[0:1] + last[1:2]
        force = jnp.concatenate([last[2:3] + last[3:4], last[4:5] + last[5:6]], axis=1)
        flipped = mixed.T
        first = jnp.where(above >= across, mixed, flipped)
        second = jnp.where(above < across, mixed, flipped)
        second = jnp.where(above == across, corner, second)
        far = jnp.concatenate(
            [
                jnp.concatenate([first, upper], axis=1),
                jnp.concatenate([upper.T, second], axis=1),
            ],
            axis=0,
        )
        grams = own[patch, :members, :] + far
        trace = total(jnp.where(diagonal, grams, 0.0))
        norm = jnp.sqrt(total(grams * grams) + 2.0 * base * trace + base * base * members)
        scale.append(norm)
        forcing.append(force + own[patch, members : members + 1, :])
        factor.append(1.5 - 0.5 * (trace / members + base) / norm)
        level = trace / members
        rest.append((grams - jnp.where(diagonal, level, 0.0)) * (-0.5 / norm))
    lead, tail = list(factor), list(rest)
    small = [rest[p].astype(BF16) for p in each]
    squares = [dot(small[p], small[p]) for p in each]
    for step in range(1, ITERS):
        cubes = [dot(squares[p].astype(BF16), small[p]) for p in each]
        for p in each:
            f = factor[p]
            rest[p] = (
                (3.0 * f * f - 3.0 * f) * rest[p] + (3.0 * f - 1.5) * squares[p] + cubes[p]
            )
            factor[p] = 1.5 - 1.5 * f * f + f * f * f
            small[p] = rest[p].astype(BF16)
        for p in each:
            narrow = tail[p].astype(BF16)
            if step < ITERS - 1:
                both = dot(jnp.concatenate([small[p], narrow], axis=0), small[p])
                squares[p], cross = both[:members], both[members:]
            else:
                cross = dot(narrow, small[p])
            tail[p] = factor[p] * tail[p] + lead[p] * rest[p] + cross
            lead[p] = factor[p] * lead[p]
    for p in each:
        high = tail[p].astype(BF16)
        root_out[p] = high
        force = jnp.broadcast_to(forcing[p], (PAD, members))
        gain = (lead[p] * force + dot(force.astype(BF16), high)) / scale[p]
        index = lax.broadcasted_iota(jnp.int32, (PAD, members), 0)
        spread = jnp.sqrt(base) / jnp.sqrt(scale[p])
        rows_out[p] = jnp.where(index == 0, gain, jnp.where(index == 1, lead[p], spread))


def apply_kernel(here, root, rows, *rest):
    slabs, (out, columns) = rest[:-2], rest[-2:]
    mine, members, _ = root.shape
    points = out.shape[1] // mine
    length = len(slabs)
    _, local, _ = slabs[0].shape
    for shift, slab in enumerate(slabs):
        source = lax.rem(here[0] // PAIR - shift + length, length)
        for i in range(PAIR):
            place = pl.ds(pl.multiple_of((source * PAIR + i) * local, local), local)
            columns[place, :] = slab[i]
    for p in range(mine):
        cols = slice(p * points, (p + 1) * points)
        member = columns[:, cols].astype(F32)
        mean = jnp.sum(member, axis=0, keepdims=True) / members
        deviation = member - mean
        spread = rows[p, 1:2, :points] * deviation + jnp.dot(
            root[p], deviation.astype(BF16), preferred_element_type=F32
        )
        shift = mean + product(split(rows[p]), split(spread))[0:1]
        out[:, cols] = (shift + rows[p, 2:3, :points] * spread).astype(BF16)


def body(state, hx, obs_value, obs_rinv, obs_count, loc_pattern):
    blocks, members, width = hx.shape
    patches, uses = loc_pattern.shape
    mem_total = lax.axis_size("mem")
    mine = patches // mem_total
    local, points = state.shape
    ring = lax.axis_size("lon")
    near = [(i, i + 1 - 2 * (i % 2)) for i in range(ring)]
    far = [(i, (i - 1 + 2 * (i % 2)) % ring) for i in range(ring)]
    odd = lax.axis_index("lon") % 2
    here = jnp.stack([lax.axis_index("mem"), 2 * odd, 2 - 2 * odd]).astype(jnp.int32)
    shape = jax.ShapeDtypeStruct
    padded = members + PAD

    span = points // mem_total
    length = mem_total // PAIR
    swap = [(i, i + 1 - 2 * (i % PAIR)) for i in range(mem_total)]

    pattern = loc_pattern.T
    far_pattern = lax.ppermute(pattern, "lon", far)
    near_pattern = lax.ppermute(pattern, "lon", near)
    paired = lax.ppermute(state, "mem", swap)
    limit = pltpu.CompilerParams(vmem_limit_bytes=16 * 1024 * 1024)
    gram = 2 * padded * members * uses * width
    pert, weights, innov = pl.pallas_call(
        perturb_kernel,
        out_shape=(
            shape((blocks, members, width), BF16),
            shape((blocks, width), F32),
            shape((blocks, width), F32),
        ),
        in_specs=[HBM] * 4,
        out_specs=(VMEM,) * 3,
        scratch_shapes=[
            pltpu.VMEM((blocks, members, width), BF16),
            pltpu.SMEM(obs_count.shape, jnp.int32),
            pltpu.VMEM(obs_value.shape, F32),
            pltpu.VMEM(obs_rinv.shape, F32),
            pltpu.SemaphoreType.DMA((blocks // CHUNK,)),
            pltpu.SemaphoreType.DMA((3,)),
        ],
        compiler_params=limit,
        cost_estimate=pl.CostEstimate(
            flops=hx.size * 4, bytes_accessed=2 * hx.size * 2, transcendentals=0
        ),
        name="perturb",
    )(*(stay(value) for value in (obs_count, hx, obs_value, obs_rinv)))
    packed = shape((mine, padded, members // 2), BF16)
    slab = shape((PAIR, local, span), BF16)
    cost = pl.CostEstimate(flops=mine * gram, bytes_accessed=hx.size, transcendentals=0)
    to_far = pl.pallas_call(
        functools.partial(far_kernel, patches, 2),
        out_shape=packed,
        in_specs=[SMEM] * 2 + [VMEM] * 3,
        out_specs=VMEM,
        compiler_params=limit,
        cost_estimate=cost,
        name="far_share",
    )(here, far_pattern, pert, weights, innov)
    from_far = lax.ppermute(to_far, "lon", far)
    to_near, *slabs = pl.pallas_call(
        functools.partial(near_kernel, patches, 1),
        out_shape=(packed,) + (slab,) * length,
        in_specs=[SMEM] * 2 + [VMEM] * 3 + [HBM] * 2 + [pl.BlockSpec(memory_space=pl.ANY)],
        out_specs=(VMEM,) * (1 + length),
        scratch_shapes=[pltpu.SemaphoreType.DMA((PAIR * length,))],
        compiler_params=limit,
        cost_estimate=cost,
        name="near_share",
    )(here, near_pattern, pert, weights, innov, state, paired, to_far)
    from_near = lax.ppermute(to_near, "lon", near)
    own = pl.pallas_call(
        functools.partial(own_kernel, patches),
        out_shape=shape((mine, padded, members), F32),
        in_specs=[SMEM] * 2 + [VMEM] * 3 + [pl.BlockSpec(memory_space=pl.ANY)],
        out_specs=VMEM,
        compiler_params=limit,
        cost_estimate=cost,
        name="own_share",
    )(here, pattern, pert, weights, innov, to_near)
    for shift in range(1, length):
        turn = [(i, (i + shift * PAIR) % mem_total) for i in range(mem_total)]
        slabs[shift] = lax.ppermute(slabs[shift], "mem", turn)
    root, rows = pl.pallas_call(
        root_kernel,
        out_shape=(shape((mine, members, members), BF16), shape((mine, PAD, members), F32)),
        in_specs=[VMEM] * 3,
        out_specs=(VMEM,) * 2,
        compiler_params=limit,
        cost_estimate=pl.CostEstimate(
            flops=mine * 15 * 2 * members**3, bytes_accessed=2**20, transcendentals=0
        ),
        name="root",
    )(own, from_far, from_near)
    updated = pl.pallas_call(
        apply_kernel,
        out_shape=shape((members, span), BF16),
        in_specs=[SMEM] + [VMEM] * (2 + length),
        out_specs=VMEM,
        scratch_shapes=[pltpu.VMEM((members, span), BF16)],
        compiler_params=limit,
        cost_estimate=pl.CostEstimate(
            flops=2 * members**2 * span, bytes_accessed=2**19, transcendentals=0
        ),
        name="apply",
    )(here, root, rows, *slabs)
    pieces = lax.all_to_all(
        updated.reshape(mem_total, local, span), "mem", split_axis=0, concat_axis=0
    )
    return jnp.swapaxes(pieces, 0, 1).reshape(local, points)


def solution(mesh):
    in_specs = (
        P("mem", "lon"),
        P("lon", None, None),
        P("lon", None),
        P("lon", None),
        P("lon"),
        P("lon", None),
    )
    out_specs = P("mem", "lon")
    return jax.shard_map(body, mesh=mesh, in_specs=in_specs, out_specs=out_specs, check_vma=False)
```

```python
import functools

import jax
import jax.numpy as jnp
from jax import lax
from jax.experimental import pallas as pl
from jax.experimental.pallas import tpu as pltpu
from jax.sharding import PartitionSpec as P

ITERS = 6
PAD = 16
CHUNK = 4
PAIR = 2
F32 = jnp.float32
BF16 = jnp.bfloat16

VMEM = pl.BlockSpec(memory_space=pltpu.VMEM)
SMEM = pl.BlockSpec(memory_space=pltpu.SMEM)
HBM = pl.BlockSpec(memory_space=pltpu.HBM)


def stay(value):
    return pltpu.with_memory_space_constraint(value, pltpu.HBM)


def split(value):
    high = value.astype(BF16)
    return high, (value - high.astype(F32)).astype(BF16)


def product(left, right):
    lhs = jnp.concatenate([left[0], left[0], left[1]], axis=1)
    rhs = jnp.concatenate([right[0], right[1], right[0]], axis=0)
    return jnp.dot(lhs, rhs, preferred_element_type=F32)


def share(pattern, row, side, patches, pert, weights, innov):
    blocks, _, width = pert.shape
    left, right = [], []
    for slot in range(pattern.shape[0]):
        position = pattern[slot, row]
        block = position - side * blocks
        here = jnp.logical_and(block >= 0, block < blocks)
        block = jnp.clip(block, 0, blocks - 1)
        spot = jnp.full((1, width), position, jnp.int32).astype(F32)
        rank = jnp.full((1, width), row, jnp.int32).astype(F32)
        offset = (spot + 0.5) / blocks - 1.0 - (rank + 0.5) / patches
        taper = jnp.exp(-0.5 * offset * offset) * jnp.where(here, 1.0, 0.0)
        picked = pert[block]
        weight = (taper * weights[pl.ds(block, 1), :]).astype(BF16)
        vector = jnp.broadcast_to(taper * innov[pl.ds(block, 1), :], (PAD, width)).astype(BF16)
        left.append(jnp.concatenate([weight * picked, vector], axis=0))
        right.append(picked)
    return lax.dot_general(
        jnp.concatenate(left, axis=1),
        jnp.concatenate(right, axis=1),
        (((1,), (1,)), ((), ())),
        preferred_element_type=F32,
    )


def perturb_kernel(
    count_all, hx, value_all, rinv_all, pert, weights, innov, raw, count, value, rinv, sems, small
):
    blocks, members, width = raw.shape
    smalls = [
        pltpu.make_async_copy(source, target, small.at[i])
        for i, (source, target) in enumerate(
            ((count_all, count), (value_all, value), (rinv_all, rinv))
        )
    ]
    copies = [
        pltpu.make_async_copy(hx.at[pl.ds(i, CHUNK)], raw.at[pl.ds(i, CHUNK)], sems.at[i // CHUNK])
        for i in range(0, blocks, CHUNK)
    ]
    for copy in smalls + copies:
        copy.start()
    for copy in smalls:
        copy.wait()
    lane = lax.broadcasted_iota(jnp.int32, (1, width), 1)
    for block in range(blocks):
        if block % CHUNK == 0:
            copies[block // CHUNK].wait()
        member = raw[block].astype(F32)
        mean = jnp.sum(member, axis=0, keepdims=True) / members
        pert[block] = (member - mean).astype(BF16)
        weight = jnp.where(lane < count[block], rinv[block : block + 1, :], 0.0)
        gap = weight * (value[block : block + 1, :] - mean)
        weights[block : block + 1, :] = weight.astype(BF16).astype(F32)
        innov[block : block + 1, :] = gap


def own_kernel(patches, here, pattern, pert, weights, innov, sent, own):
    mine = own.shape[0]
    for patch in range(mine):
        row = here[0] * mine + patch
        own[patch] = share(pattern, row, 1, patches, pert, weights, innov)


def pack(part, out, patch):
    _, padded, half = out.shape
    members = padded - PAD
    above = lax.broadcasted_iota(jnp.int32, (half, half), 0)
    across = lax.broadcasted_iota(jnp.int32, (half, half), 1)
    corner = part[half:members, half:]
    out[patch, :half, :] = part[:half, half:].astype(BF16)
    out[patch, half:members, :] = jnp.where(above >= across, part[:half, :half], corner).astype(
        BF16
    )
    diagonal = jnp.sum(jnp.where(above == across, corner, 0.0), axis=0, keepdims=True)
    force = part[members : members + 1]
    index = lax.broadcasted_iota(jnp.int32, (PAD, half), 0)
    tail = jnp.zeros((PAD, half), F32)
    for i, value in enumerate((diagonal, force[:, :half], force[:, half:])):
        high, low = split(value)
        tail = jnp.where(index == 2 * i, high.astype(F32), tail)
        tail = jnp.where(index == 2 * i + 1, low.astype(F32), tail)
    out[patch, members:, :] = tail.astype(BF16)


def far_kernel(patches, here, side, pattern, pert, weights, innov, out):
    mine = out.shape[0]
    for patch in range(mine):
        row = here[0] * mine + patch
        pack(share(pattern, row, side[0], patches, pert, weights, innov), out, patch)


def near_kernel(patches, here, side, pattern, pert, weights, innov, state, paired, sent, out, *rest):
    slabs, sems = rest[:-1], rest[-1]
    span = slabs[0].shape[2]
    length = len(slabs)
    layer, place = here[0] // PAIR, here[0] % PAIR
    moves = []
    for shift, slab in enumerate(slabs):
        target = lax.rem(layer + shift, length) * PAIR + place
        cols = pl.ds(pl.multiple_of(target * span, span), span)
        moves.append((state.at[:, cols], slab.at[place]))
        moves.append((paired.at[:, cols], slab.at[1 - place]))
    moves = [pltpu.make_async_copy(*move, sems.at[i]) for i, move in enumerate(moves)]
    for move in moves:
        move.start()
    far_kernel(patches, here, side, pattern, pert, weights, innov, out)
    for move in moves:
        move.wait()


def total(value):
    return jnp.sum(jnp.sum(value, axis=0, keepdims=True), axis=1, keepdims=True)


def root_kernel(own, before, after, root_out, rows_out):
    mine, _, members = own.shape
    half = members // 2
    above = lax.broadcasted_iota(jnp.int32, (half, half), 0)
    across = lax.broadcasted_iota(jnp.int32, (half, half), 1)
    row = lax.broadcasted_iota(jnp.int32, (members, members), 0)
    col = lax.broadcasted_iota(jnp.int32, (members, members), 1)
    diagonal = row == col

    def dot(left, right):
        return jnp.dot(left, right, preferred_element_type=F32)

    each = range(mine)
    rest, factor, scale, forcing = [], [], [], []
    base = members - 1.0
    for patch in each:
        packed = before[patch].astype(F32) + after[patch].astype(F32)
        upper = packed[:half]
        mixed = packed[half:members]
        last = packed[members:]
        corner = last[0:1] + last[1:2]
        force = jnp.concatenate([last[2:3] + last[3:4], last[4:5] + last[5:6]], axis=1)
        flipped = mixed.T
        first = jnp.where(above >= across, mixed, flipped)
        second = jnp.where(above < across, mixed, flipped)
        second = jnp.where(above == across, corner, second)
        far = jnp.concatenate(
            [
                jnp.concatenate([first, upper], axis=1),
                jnp.concatenate([upper.T, second], axis=1),
            ],
            axis=0,
        )
        grams = own[patch, :members, :] + far
        trace = total(jnp.where(diagonal, grams, 0.0))
        norm = jnp.sqrt(total(grams * grams) + 2.0 * base * trace + base * base * members)
        scale.append(norm)
        forcing.append(force + own[patch, members : members + 1, :])
        factor.append(1.5 - 0.5 * (trace / members + base) / norm)
        level = trace / members
        rest.append((grams - jnp.where(diagonal, level, 0.0)) * (-0.5 / norm))
    lead, tail = list(factor), list(rest)
    small = [rest[p].astype(BF16) for p in each]
    squares = [dot(small[p], small[p]) for p in each]
    for step in range(1, ITERS):
        cubes = [dot(squares[p].astype(BF16), small[p]) for p in each]
        for p in each:
            f = factor[p]
            rest[p] = (
                (3.0 * f * f - 3.0 * f) * rest[p] + (3.0 * f - 1.5) * squares[p] + cubes[p]
            )
            factor[p] = 1.5 - 1.5 * f * f + f * f * f
            small[p] = rest[p].astype(BF16)
        for p in each:
            narrow = tail[p].astype(BF16)
            if step < ITERS - 1:
                both = dot(jnp.concatenate([small[p], narrow], axis=0), small[p])
                squares[p], cross = both[:members], both[members:]
            else:
                cross = dot(narrow, small[p])
            tail[p] = factor[p] * tail[p] + lead[p] * rest[p] + cross
            lead[p] = factor[p] * lead[p]
    for p in each:
        high = tail[p].astype(BF16)
        root_out[p] = high
        force = jnp.broadcast_to(forcing[p], (PAD, members))
        gain = (lead[p] * force + dot(force.astype(BF16), high)) / scale[p]
        index = lax.broadcasted_iota(jnp.int32, (PAD, members), 0)
        spread = jnp.sqrt(base) / jnp.sqrt(scale[p])
        rows_out[p] = jnp.where(index == 0, gain, jnp.where(index == 1, lead[p], spread))


def partner(here, shift, count):
    assert count & (count - 1) == 0
    return here ^ shift


def apply_kernel(here, root, rows, *rest):
    columns, out = rest[-2:]
    count = (len(rest) - 2) * PAIR // (PAIR + 1)
    slabs, pieces = rest[: count // PAIR], rest[count // PAIR : -2]
    mine, members, _ = root.shape
    points = out.shape[1] // mine
    length = len(slabs)
    _, local, _ = slabs[0].shape
    for shift, slab in enumerate(slabs):
        source = lax.rem(here[0] // PAIR - shift + length, length)
        for i in range(PAIR):
            place = pl.ds(pl.multiple_of((source * PAIR + i) * local, local), local)
            columns[place, :] = slab[i]
    for p in range(mine):
        cols = slice(p * points, (p + 1) * points)
        member = columns[:, cols].astype(F32)
        mean = jnp.sum(member, axis=0, keepdims=True) / members
        deviation = member - mean
        spread = rows[p, 1:2, :points] * deviation + jnp.dot(
            root[p], deviation.astype(BF16), preferred_element_type=F32
        )
        shift = mean + product(split(rows[p]), split(spread))[0:1]
        out[:, cols] = (shift + rows[p, 2:3, :points] * spread).astype(BF16)
    for shift, piece in enumerate(pieces):
        target = partner(here[0], shift, count)
        piece[...] = out[pl.ds(pl.multiple_of(target * local, local), local), :]


def layout_kernel(here, *rest):
    pieces, (out, whole, sem) = rest[:-3], rest[-3:]
    count = len(pieces)
    _, span = pieces[0].shape
    for shift, piece in enumerate(pieces):
        source = partner(here[0], shift, count)
        whole[:, pl.ds(pl.multiple_of(source * span, span), span)] = piece[...]
    copy = pltpu.make_async_copy(whole, out, sem)
    copy.start()
    copy.wait()


def body(state, hx, obs_value, obs_rinv, obs_count, loc_pattern):
    blocks, members, width = hx.shape
    patches, uses = loc_pattern.shape
    mem_total = lax.axis_size("mem")
    mine = patches // mem_total
    local, points = state.shape
    ring = lax.axis_size("lon")
    near = [(i, i + 1 - 2 * (i % 2)) for i in range(ring)]
    far = [(i, (i - 1 + 2 * (i % 2)) % ring) for i in range(ring)]
    odd = lax.axis_index("lon") % 2
    here, near_side, far_side = (
        value.astype(jnp.int32).reshape(1) for value in (lax.axis_index("mem"), 2 * odd, 2 - 2 * odd)
    )
    shape = jax.ShapeDtypeStruct
    padded = members + PAD

    span = points // mem_total
    length = mem_total // PAIR
    swap = [(i, i + 1 - 2 * (i % PAIR)) for i in range(mem_total)]

    pattern = loc_pattern.T
    far_pattern = lax.ppermute(pattern, "lon", far)
    near_pattern = lax.ppermute(pattern, "lon", near)
    paired = lax.ppermute(state, "mem", swap)
    limit = pltpu.CompilerParams(vmem_limit_bytes=16 * 1024 * 1024)
    gram = 2 * padded * members * uses * width
    pert, weights, innov = pl.pallas_call(
        perturb_kernel,
        out_shape=(
            shape((blocks, members, width), BF16),
            shape((blocks, width), F32),
            shape((blocks, width), F32),
        ),
        in_specs=[HBM] * 4,
        out_specs=(VMEM,) * 3,
        scratch_shapes=[
            pltpu.VMEM((blocks, members, width), BF16),
            pltpu.SMEM(obs_count.shape, jnp.int32),
            pltpu.VMEM(obs_value.shape, F32),
            pltpu.VMEM(obs_rinv.shape, F32),
            pltpu.SemaphoreType.DMA((blocks // CHUNK,)),
            pltpu.SemaphoreType.DMA((3,)),
        ],
        compiler_params=limit,
        cost_estimate=pl.CostEstimate(
            flops=hx.size * 4, bytes_accessed=2 * hx.size * 2, transcendentals=0
        ),
        name="perturb",
    )(*(stay(value) for value in (obs_count, hx, obs_value, obs_rinv)))
    packed = shape((mine, padded, members // 2), BF16)
    slab = shape((PAIR, local, span), BF16)
    cost = pl.CostEstimate(flops=mine * gram, bytes_accessed=hx.size, transcendentals=0)
    to_far = pl.pallas_call(
        functools.partial(far_kernel, patches),
        out_shape=packed,
        in_specs=[SMEM] * 3 + [VMEM] * 3,
        out_specs=VMEM,
        compiler_params=limit,
        cost_estimate=cost,
        name="far_share",
    )(here, far_side, far_pattern, pert, weights, innov)
    from_far = lax.ppermute(to_far, "lon", far)
    to_near, *slabs = pl.pallas_call(
        functools.partial(near_kernel, patches),
        out_shape=(packed,) + (slab,) * length,
        in_specs=[SMEM] * 3 + [VMEM] * 3 + [HBM] * 2 + [pl.BlockSpec(memory_space=pl.ANY)],
        out_specs=(VMEM,) * (1 + length),
        scratch_shapes=[pltpu.SemaphoreType.DMA((PAIR * length,))],
        compiler_params=limit,
        cost_estimate=cost,
        name="near_share",
    )(here, near_side, near_pattern, pert, weights, innov, state, paired, to_far)
    from_near = lax.ppermute(to_near, "lon", near)
    own = pl.pallas_call(
        functools.partial(own_kernel, patches),
        out_shape=shape((mine, padded, members), F32),
        in_specs=[SMEM] * 2 + [VMEM] * 3 + [pl.BlockSpec(memory_space=pl.ANY)],
        out_specs=VMEM,
        compiler_params=limit,
        cost_estimate=cost,
        name="own_share",
    )(here, pattern, pert, weights, innov, to_near)
    for shift in range(1, length):
        turn = [(i, (i + shift * PAIR) % mem_total) for i in range(mem_total)]
        slabs[shift] = lax.ppermute(slabs[shift], "mem", turn)
    root, rows = pl.pallas_call(
        root_kernel,
        out_shape=(shape((mine, members, members), BF16), shape((mine, PAD, members), F32)),
        in_specs=[VMEM] * 3,
        out_specs=(VMEM,) * 2,
        compiler_params=limit,
        cost_estimate=pl.CostEstimate(
            flops=mine * 15 * 2 * members**3, bytes_accessed=2**20, transcendentals=0
        ),
        name="root",
    )(own, from_far, from_near)
    pieces = pl.pallas_call(
        apply_kernel,
        out_shape=(shape((local, span), BF16),) * mem_total,
        in_specs=[SMEM] + [VMEM] * (2 + length),
        out_specs=(VMEM,) * mem_total,
        scratch_shapes=[pltpu.VMEM((members, span), BF16)] * 2,
        compiler_params=limit,
        cost_estimate=pl.CostEstimate(
            flops=2 * members**2 * span, bytes_accessed=2**19, transcendentals=0
        ),
        name="apply",
    )(here, root, rows, *slabs)
    pieces = list(pieces)
    for shift in range(1, mem_total):
        swap = [(i, partner(i, shift, mem_total)) for i in range(mem_total)]
        pieces[shift] = lax.ppermute(pieces[shift], "mem", swap)
    return pl.pallas_call(
        layout_kernel,
        out_shape=shape((local, points), BF16),
        in_specs=[SMEM] + [VMEM] * mem_total,
        out_specs=HBM,
        scratch_shapes=[pltpu.VMEM((local, points), BF16), pltpu.SemaphoreType.DMA],
        compiler_params=limit,
        name="layout",
    )(here, *pieces)


def solution(mesh):
    in_specs = (
        P("mem", "lon"),
        P("lon", None, None),
        P("lon", None),
        P("lon", None),
        P("lon"),
        P("lon", None),
    )
    out_specs = P("mem", "lon")
    return jax.shard_map(body, mesh=mesh, in_specs=in_specs, out_specs=out_specs, check_vma=False)
```

```python
import functools

import jax
import jax.numpy as jnp
from jax import lax
from jax.experimental import pallas as pl
from jax.experimental.pallas import tpu as pltpu
from jax.sharding import PartitionSpec as P

ITERS = 6
PAD = 16
CHUNK = 4
PAIR = 2
F32 = jnp.float32
BF16 = jnp.bfloat16

VMEM = pl.BlockSpec(memory_space=pltpu.VMEM)
SMEM = pl.BlockSpec(memory_space=pltpu.SMEM)
HBM = pl.BlockSpec(memory_space=pltpu.HBM)


def stay(value):
    return pltpu.with_memory_space_constraint(value, pltpu.HBM)


def split(value):
    high = value.astype(BF16)
    return high, (value - high.astype(F32)).astype(BF16)


def product(left, right):
    lhs = jnp.concatenate([left[0], left[0], left[1]], axis=1)
    rhs = jnp.concatenate([right[0], right[1], right[0]], axis=0)
    return jnp.dot(lhs, rhs, preferred_element_type=F32)


def share(pattern, row, side, patches, pert, weights, innov):
    blocks, _, width = pert.shape
    left, right = [], []
    for slot in range(pattern.shape[0]):
        position = pattern[slot, row]
        block = position - side * blocks
        here = jnp.logical_and(block >= 0, block < blocks)
        block = jnp.clip(block, 0, blocks - 1)
        spot = jnp.full((1, width), position, jnp.int32).astype(F32)
        rank = jnp.full((1, width), row, jnp.int32).astype(F32)
        offset = (spot + 0.5) / blocks - 1.0 - (rank + 0.5) / patches
        taper = jnp.exp(-0.5 * offset * offset) * jnp.where(here, 1.0, 0.0)
        picked = pert[block]
        weight = (taper * weights[pl.ds(block, 1), :]).astype(BF16)
        vector = jnp.broadcast_to(taper * innov[pl.ds(block, 1), :], (PAD, width)).astype(BF16)
        left.append(jnp.concatenate([weight * picked, vector], axis=0))
        right.append(picked)
    return lax.dot_general(
        jnp.concatenate(left, axis=1),
        jnp.concatenate(right, axis=1),
        (((1,), (1,)), ((), ())),
        preferred_element_type=F32,
    )


def perturb_kernel(
    count_all, hx, value_all, rinv_all, pert, weights, innov, raw, count, value, rinv, sems, small
):
    blocks, members, width = raw.shape
    smalls = [
        pltpu.make_async_copy(source, target, small.at[i])
        for i, (source, target) in enumerate(
            ((count_all, count), (value_all, value), (rinv_all, rinv))
        )
    ]
    copies = [
        pltpu.make_async_copy(hx.at[pl.ds(i, CHUNK)], raw.at[pl.ds(i, CHUNK)], sems.at[i // CHUNK])
        for i in range(0, blocks, CHUNK)
    ]
    for copy in smalls + copies:
        copy.start()
    for copy in smalls:
        copy.wait()
    lane = lax.broadcasted_iota(jnp.int32, (1, width), 1)
    for block in range(blocks):
        if block % CHUNK == 0:
            copies[block // CHUNK].wait()
        member = raw[block].astype(F32)
        mean = jnp.sum(member, axis=0, keepdims=True) / members
        pert[block] = (member - mean).astype(BF16)
        weight = jnp.where(lane < count[block], rinv[block : block + 1, :], 0.0)
        gap = weight * (value[block : block + 1, :] - mean)
        weights[block : block + 1, :] = weight.astype(BF16).astype(F32)
        innov[block : block + 1, :] = gap


def own_kernel(
    patches, here, pattern, pert, weights, innov, state, paired, sent, own, slabs, sems
):
    mine = own.shape[0]
    length, _, _, span = slabs.shape
    place = here[0] % PAIR
    moves = []
    for layer in range(length):
        start = (layer * PAIR + place) * span
        cols = pl.ds(pl.multiple_of(start, span), span)
        moves.append((state.at[:, cols], slabs.at[layer, place]))
        moves.append((paired.at[:, cols], slabs.at[layer, 1 - place]))
    moves = [pltpu.make_async_copy(*move, sems.at[i]) for i, move in enumerate(moves)]
    for move in moves:
        move.start()
    for patch in range(mine):
        row = here[0] * mine + patch
        own[patch] = share(pattern, row, 1, patches, pert, weights, innov)
    for move in moves:
        move.wait()


def pack(part, out, patch):
    _, padded, half = out.shape
    members = padded - PAD
    above = lax.broadcasted_iota(jnp.int32, (half, half), 0)
    across = lax.broadcasted_iota(jnp.int32, (half, half), 1)
    corner = part[half:members, half:]
    out[patch, :half, :] = part[:half, half:].astype(BF16)
    out[patch, half:members, :] = jnp.where(above >= across, part[:half, :half], corner).astype(
        BF16
    )
    diagonal = jnp.sum(jnp.where(above == across, corner, 0.0), axis=0, keepdims=True)
    force = part[members : members + 1]
    index = lax.broadcasted_iota(jnp.int32, (PAD, half), 0)
    tail = jnp.zeros((PAD, half), F32)
    for i, value in enumerate((diagonal, force[:, :half], force[:, half:])):
        high, low = split(value)
        tail = jnp.where(index == 2 * i, high.astype(F32), tail)
        tail = jnp.where(index == 2 * i + 1, low.astype(F32), tail)
    out[patch, members:, :] = tail.astype(BF16)


def neighbour_kernel(patches, here, side, pattern, pert, weights, innov, *rest):
    out = rest[-1]
    mine = out.shape[0]
    for patch in range(mine):
        row = here[0] * mine + patch
        pack(share(pattern, row, side[0], patches, pert, weights, innov), out, patch)


def total(value):
    return jnp.sum(jnp.sum(value, axis=0, keepdims=True), axis=1, keepdims=True)


def root_kernel(own, before, after, root_out, rows_out):
    mine, _, members = own.shape
    half = members // 2
    above = lax.broadcasted_iota(jnp.int32, (half, half), 0)
    across = lax.broadcasted_iota(jnp.int32, (half, half), 1)
    row = lax.broadcasted_iota(jnp.int32, (members, members), 0)
    col = lax.broadcasted_iota(jnp.int32, (members, members), 1)
    diagonal = row == col

    def dot(left, right):
        return jnp.dot(left, right, preferred_element_type=F32)

    each = range(mine)
    rest, factor, scale, forcing = [], [], [], []
    base = members - 1.0
    for patch in each:
        packed = before[patch].astype(F32) + after[patch].astype(F32)
        upper = packed[:half]
        mixed = packed[half:members]
        last = packed[members:]
        corner = last[0:1] + last[1:2]
        force = jnp.concatenate([last[2:3] + last[3:4], last[4:5] + last[5:6]], axis=1)
        flipped = mixed.T
        first = jnp.where(above >= across, mixed, flipped)
        second = jnp.where(above < across, mixed, flipped)
        second = jnp.where(above == across, corner, second)
        far = jnp.concatenate(
            [
                jnp.concatenate([first, upper], axis=1),
                jnp.concatenate([upper.T, second], axis=1),
            ],
            axis=0,
        )
        grams = own[patch, :members, :] + far
        trace = total(jnp.where(diagonal, grams, 0.0))
        norm = jnp.sqrt(total(grams * grams) + 2.0 * base * trace + base * base * members)
        scale.append(norm)
        forcing.append(force + own[patch, members : members + 1, :])
        factor.append(1.5 - 0.5 * (trace / members + base) / norm)
        level = trace / members
        rest.append((grams - jnp.where(diagonal, level, 0.0)) * (-0.5 / norm))
    lead, tail = list(factor), list(rest)
    small = [rest[p].astype(BF16) for p in each]
    squares = [dot(small[p], small[p]) for p in each]
    for step in range(1, ITERS):
        cubes = [dot(squares[p].astype(BF16), small[p]) for p in each]
        for p in each:
            f = factor[p]
            rest[p] = (
                (3.0 * f * f - 3.0 * f) * rest[p] + (3.0 * f - 1.5) * squares[p] + cubes[p]
            )
            factor[p] = 1.5 - 1.5 * f * f + f * f * f
            small[p] = rest[p].astype(BF16)
        for p in each:
            narrow = tail[p].astype(BF16)
            if step < ITERS - 1:
                both = dot(jnp.concatenate([small[p], narrow], axis=0), small[p])
                squares[p], cross = both[:members], both[members:]
            else:
                cross = dot(narrow, small[p])
            tail[p] = factor[p] * tail[p] + lead[p] * rest[p] + cross
            lead[p] = factor[p] * lead[p]
    for p in each:
        high = tail[p].astype(BF16)
        root_out[p] = high
        force = jnp.broadcast_to(forcing[p], (PAD, members))
        gain = (lead[p] * force + dot(force.astype(BF16), high)) / scale[p]
        index = lax.broadcasted_iota(jnp.int32, (PAD, members), 0)
        spread = jnp.sqrt(base) / jnp.sqrt(scale[p])
        rows_out[p] = jnp.where(index == 0, gain, jnp.where(index == 1, lead[p], spread))


def apply_kernel(root, rows, state, out):
    mine, members, _ = root.shape
    points = out.shape[1] // mine
    for p in range(mine):
        cols = slice(p * points, (p + 1) * points)
        member = state[:, cols].astype(F32)
        mean = jnp.sum(member, axis=0, keepdims=True) / members
        deviation = member - mean
        spread = rows[p, 1:2, :points] * deviation + jnp.dot(
            root[p], deviation.astype(BF16), preferred_element_type=F32
        )
        shift = mean + product(split(rows[p]), split(spread))[0:1]
        out[:, cols] = (shift + rows[p, 2:3, :points] * spread).astype(BF16)


def body(state, hx, obs_value, obs_rinv, obs_count, loc_pattern):
    blocks, members, width = hx.shape
    patches, uses = loc_pattern.shape
    mem_total = lax.axis_size("mem")
    mine = patches // mem_total
    local, points = state.shape
    ring = lax.axis_size("lon")
    near = [(i, i + 1 - 2 * (i % 2)) for i in range(ring)]
    far = [(i, (i - 1 + 2 * (i % 2)) % ring) for i in range(ring)]
    odd = lax.axis_index("lon") % 2
    here, near_side, far_side = (
        value.astype(jnp.int32).reshape(1) for value in (lax.axis_index("mem"), 2 * odd, 2 - 2 * odd)
    )
    shape = jax.ShapeDtypeStruct
    padded = members + PAD

    span = points // mem_total
    length = mem_total // PAIR
    swap = [(i, i + 1 - 2 * (i % PAIR)) for i in range(mem_total)]

    pattern = loc_pattern.T
    far_pattern = lax.ppermute(pattern, "lon", far)
    near_pattern = lax.ppermute(pattern, "lon", near)
    limit = pltpu.CompilerParams(vmem_limit_bytes=16 * 1024 * 1024)
    gram = 2 * padded * members * uses * width
    pert, weights, innov = pl.pallas_call(
        perturb_kernel,
        out_shape=(
            shape((blocks, members, width), BF16),
            shape((blocks, width), F32),
            shape((blocks, width), F32),
        ),
        in_specs=[HBM] * 4,
        out_specs=(VMEM,) * 3,
        scratch_shapes=[
            pltpu.VMEM((blocks, members, width), BF16),
            pltpu.SMEM(obs_count.shape, jnp.int32),
            pltpu.VMEM(obs_value.shape, F32),
            pltpu.VMEM(obs_rinv.shape, F32),
            pltpu.SemaphoreType.DMA((blocks // CHUNK,)),
            pltpu.SemaphoreType.DMA((3,)),
        ],
        compiler_params=limit,
        cost_estimate=pl.CostEstimate(
            flops=hx.size * 4, bytes_accessed=2 * hx.size * 2, transcendentals=0
        ),
        name="perturb",
    )(*(stay(value) for value in (obs_count, hx, obs_value, obs_rinv)))
    packed = shape((mine, padded, members // 2), BF16)
    cost = pl.CostEstimate(flops=mine * gram, bytes_accessed=hx.size, transcendentals=0)

    def shares(side, theirs, *earlier):
        return pl.pallas_call(
            functools.partial(neighbour_kernel, patches),
            out_shape=packed,
            in_specs=[SMEM] * 3 + [VMEM] * 3 + [pl.BlockSpec(memory_space=pl.ANY)] * len(earlier),
            out_specs=VMEM,
            compiler_params=limit,
            cost_estimate=cost,
            name="neighbour_share",
        )(here, side, theirs, pert, weights, innov, *earlier)

    to_far = shares(far_side, far_pattern)
    from_far = lax.ppermute(to_far, "lon", far)
    later, _ = lax.optimization_barrier((state, to_far))
    paired = lax.ppermute(later, "mem", swap)
    to_near = shares(near_side, near_pattern, to_far)
    from_near = lax.ppermute(to_near, "lon", near)
    own, slabs = pl.pallas_call(
        functools.partial(own_kernel, patches),
        out_shape=(
            shape((mine, padded, members), F32),
            shape((length, PAIR, local, span), BF16),
        ),
        in_specs=[SMEM] * 2 + [VMEM] * 3 + [HBM] * 2 + [pl.BlockSpec(memory_space=pl.ANY)],
        out_specs=(VMEM,) * 2,
        scratch_shapes=[pltpu.SemaphoreType.DMA((PAIR * length,))],
        compiler_params=limit,
        cost_estimate=cost,
        name="own_share",
    )(here, pattern, pert, weights, innov, state, paired, to_near)
    layers = [[i * PAIR + j for i in range(length)] for j in range(PAIR)]
    columns = lax.all_to_all(
        slabs, "mem", split_axis=0, concat_axis=0, axis_index_groups=layers
    ).reshape(members, span)
    root, rows = pl.pallas_call(
        root_kernel,
        out_shape=(shape((mine, members, members), BF16), shape((mine, PAD, members), F32)),
        in_specs=[VMEM] * 3,
        out_specs=(VMEM,) * 2,
        compiler_params=limit,
        cost_estimate=pl.CostEstimate(
            flops=mine * 15 * 2 * members**3, bytes_accessed=2**20, transcendentals=0
        ),
        name="root",
    )(own, from_far, from_near)
    updated = pl.pallas_call(
        apply_kernel,
        out_shape=shape((members, span), BF16),
        in_specs=[VMEM] * 3,
        out_specs=VMEM,
        compiler_params=limit,
        cost_estimate=pl.CostEstimate(
            flops=2 * members**2 * span, bytes_accessed=2**19, transcendentals=0
        ),
        name="apply",
    )(root, rows, columns)
    pieces = lax.all_to_all(
        updated.reshape(mem_total, local, span), "mem", split_axis=0, concat_axis=0
    )
    return jnp.swapaxes(pieces, 0, 1).reshape(local, points)


def solution(mesh):
    in_specs = (
        P("mem", "lon"),
        P("lon", None, None),
        P("lon", None),
        P("lon", None),
        P("lon"),
        P("lon", None),
    )
    out_specs = P("mem", "lon")
    return jax.shard_map(body, mesh=mesh, in_specs=in_specs, out_specs=out_specs, check_vma=False)
```

```python
import functools

import jax
import jax.numpy as jnp
from jax import lax
from jax.experimental import pallas as pl
from jax.experimental.pallas import tpu as pltpu
from jax.sharding import PartitionSpec as P

ITERS = 6
PAD = 16
CHUNK = 4
PAIR = 2
F32 = jnp.float32
BF16 = jnp.bfloat16

VMEM = pl.BlockSpec(memory_space=pltpu.VMEM)
SMEM = pl.BlockSpec(memory_space=pltpu.SMEM)
HBM = pl.BlockSpec(memory_space=pltpu.HBM)


def stay(value):
    return pltpu.with_memory_space_constraint(value, pltpu.HBM)


def split(value):
    high = value.astype(BF16)
    return high, (value - high.astype(F32)).astype(BF16)


def product(left, right):
    lhs = jnp.concatenate([left[0], left[0], left[1]], axis=1)
    rhs = jnp.concatenate([right[0], right[1], right[0]], axis=0)
    return jnp.dot(lhs, rhs, preferred_element_type=F32)


def share(pattern, row, side, patches, pert, weights, innov):
    blocks, _, width = pert.shape
    left, right = [], []
    for slot in range(pattern.shape[0]):
        position = pattern[slot, row]
        block = position - side * blocks
        here = jnp.logical_and(block >= 0, block < blocks)
        block = jnp.clip(block, 0, blocks - 1)
        spot = jnp.full((1, width), position, jnp.int32).astype(F32)
        rank = jnp.full((1, width), row, jnp.int32).astype(F32)
        offset = (spot + 0.5) / blocks - 1.0 - (rank + 0.5) / patches
        taper = jnp.exp(-0.5 * offset * offset) * jnp.where(here, 1.0, 0.0)
        picked = pert[block]
        weight = (taper * weights[pl.ds(block, 1), :]).astype(BF16)
        vector = jnp.broadcast_to(taper * innov[pl.ds(block, 1), :], (PAD, width)).astype(BF16)
        left.append(jnp.concatenate([weight * picked, vector], axis=0))
        right.append(picked)
    return lax.dot_general(
        jnp.concatenate(left, axis=1),
        jnp.concatenate(right, axis=1),
        (((1,), (1,)), ((), ())),
        preferred_element_type=F32,
    )


def perturb_kernel(
    count_all, hx, value_all, rinv_all, pert, weights, innov, raw, count, value, rinv, sems, small
):
    blocks, members, width = raw.shape
    smalls = [
        pltpu.make_async_copy(source, target, small.at[i])
        for i, (source, target) in enumerate(
            ((count_all, count), (value_all, value), (rinv_all, rinv))
        )
    ]
    copies = [
        pltpu.make_async_copy(hx.at[pl.ds(i, CHUNK)], raw.at[pl.ds(i, CHUNK)], sems.at[i // CHUNK])
        for i in range(0, blocks, CHUNK)
    ]
    for copy in smalls + copies:
        copy.start()
    for copy in smalls:
        copy.wait()
    lane = lax.broadcasted_iota(jnp.int32, (1, width), 1)
    for block in range(blocks):
        if block % CHUNK == 0:
            copies[block // CHUNK].wait()
        member = raw[block].astype(F32)
        mean = jnp.sum(member, axis=0, keepdims=True) / members
        pert[block] = (member - mean).astype(BF16)
        weight = jnp.where(lane < count[block], rinv[block : block + 1, :], 0.0)
        gap = weight * (value[block : block + 1, :] - mean)
        weights[block : block + 1, :] = weight.astype(BF16).astype(F32)
        innov[block : block + 1, :] = gap


def own_kernel(patches, here, pattern, pert, weights, innov, sent, own):
    mine = own.shape[0]
    for patch in range(mine):
        row = here[0] * mine + patch
        own[patch] = share(pattern, row, 1, patches, pert, weights, innov)


def pack(part, out, patch):
    _, padded, half = out.shape
    members = padded - PAD
    above = lax.broadcasted_iota(jnp.int32, (half, half), 0)
    across = lax.broadcasted_iota(jnp.int32, (half, half), 1)
    corner = part[half:members, half:]
    out[patch, :half, :] = part[:half, half:].astype(BF16)
    out[patch, half:members, :] = jnp.where(above >= across, part[:half, :half], corner).astype(
        BF16
    )
    diagonal = jnp.sum(jnp.where(above == across, corner, 0.0), axis=0, keepdims=True)
    force = part[members : members + 1]
    index = lax.broadcasted_iota(jnp.int32, (PAD, half), 0)
    tail = jnp.zeros((PAD, half), F32)
    for i, value in enumerate((diagonal, force[:, :half], force[:, half:])):
        high, low = split(value)
        tail = jnp.where(index == 2 * i, high.astype(F32), tail)
        tail = jnp.where(index == 2 * i + 1, low.astype(F32), tail)
    out[patch, members:, :] = tail.astype(BF16)


def far_kernel(patches, here, side, pattern, pert, weights, innov, out):
    mine = out.shape[0]
    for patch in range(mine):
        row = here[0] * mine + patch
        pack(share(pattern, row, side[0], patches, pert, weights, innov), out, patch)


def near_kernel(patches, here, side, pattern, pert, weights, innov, state, paired, sent, out, *rest):
    slabs, sems = rest[:-1], rest[-1]
    span = slabs[0].shape[2]
    length = len(slabs)
    layer, place = here[0] // PAIR, here[0] % PAIR
    moves = []
    for shift, slab in enumerate(slabs):
        target = (layer ^ shift) * PAIR + place
        cols = pl.ds(pl.multiple_of(target * span, span), span)
        moves.append((state.at[:, cols], slab.at[place]))
        moves.append((paired.at[:, cols], slab.at[1 - place]))
    moves = [pltpu.make_async_copy(*move, sems.at[i]) for i, move in enumerate(moves)]
    for move in moves:
        move.start()
    far_kernel(patches, here, side, pattern, pert, weights, innov, out)
    for move in moves:
        move.wait()


def total(value):
    return jnp.sum(jnp.sum(value, axis=0, keepdims=True), axis=1, keepdims=True)


def root_kernel(own, before, after, root_out, rows_out):
    mine, _, members = own.shape
    half = members // 2
    above = lax.broadcasted_iota(jnp.int32, (half, half), 0)
    across = lax.broadcasted_iota(jnp.int32, (half, half), 1)
    row = lax.broadcasted_iota(jnp.int32, (members, members), 0)
    col = lax.broadcasted_iota(jnp.int32, (members, members), 1)
    diagonal = row == col

    def dot(left, right):
        return jnp.dot(left, right, preferred_element_type=F32)

    each = range(mine)
    rest, factor, scale, forcing = [], [], [], []
    base = members - 1.0
    for patch in each:
        packed = before[patch].astype(F32) + after[patch].astype(F32)
        upper = packed[:half]
        mixed = packed[half:members]
        last = packed[members:]
        corner = last[0:1] + last[1:2]
        force = jnp.concatenate([last[2:3] + last[3:4], last[4:5] + last[5:6]], axis=1)
        flipped = mixed.T
        first = jnp.where(above >= across, mixed, flipped)
        second = jnp.where(above < across, mixed, flipped)
        second = jnp.where(above == across, corner, second)
        far = jnp.concatenate(
            [
                jnp.concatenate([first, upper], axis=1),
                jnp.concatenate([upper.T, second], axis=1),
            ],
            axis=0,
        )
        grams = own[patch, :members, :] + far
        trace = total(jnp.where(diagonal, grams, 0.0))
        norm = jnp.sqrt(total(grams * grams) + 2.0 * base * trace + base * base * members)
        scale.append(norm)
        forcing.append(force + own[patch, members : members + 1, :])
        factor.append(1.5 - 0.5 * (trace / members + base) / norm)
        level = trace / members
        rest.append((grams - jnp.where(diagonal, level, 0.0)) * (-0.5 / norm))
    lead, tail = list(factor), list(rest)
    small = [rest[p].astype(BF16) for p in each]
    squares = [dot(small[p], small[p]) for p in each]
    for step in range(1, ITERS):
        cubes = [dot(squares[p].astype(BF16), small[p]) for p in each]
        for p in each:
            f = factor[p]
            rest[p] = (
                (3.0 * f * f - 3.0 * f) * rest[p] + (3.0 * f - 1.5) * squares[p] + cubes[p]
            )
            factor[p] = 1.5 - 1.5 * f * f + f * f * f
            small[p] = rest[p].astype(BF16)
        for p in each:
            narrow = tail[p].astype(BF16)
            if step < ITERS - 1:
                both = dot(jnp.concatenate([small[p], narrow], axis=0), small[p])
                squares[p], cross = both[:members], both[members:]
            else:
                cross = dot(narrow, small[p])
            tail[p] = factor[p] * tail[p] + lead[p] * rest[p] + cross
            lead[p] = factor[p] * lead[p]
    for p in each:
        high = tail[p].astype(BF16)
        root_out[p] = high
        force = jnp.broadcast_to(forcing[p], (PAD, members))
        gain = (lead[p] * force + dot(force.astype(BF16), high)) / scale[p]
        index = lax.broadcasted_iota(jnp.int32, (PAD, members), 0)
        spread = jnp.sqrt(base) / jnp.sqrt(scale[p])
        rows_out[p] = jnp.where(index == 0, gain, jnp.where(index == 1, lead[p], spread))


def apply_kernel(here, root, rows, *rest):
    slabs, (out, columns) = rest[:-2], rest[-2:]
    mine, members, _ = root.shape
    points = out.shape[1] // mine
    length = len(slabs)
    _, local, _ = slabs[0].shape
    for shift, slab in enumerate(slabs):
        source = (here[0] // PAIR) ^ shift
        for i in range(PAIR):
            place = pl.ds(pl.multiple_of((source * PAIR + i) * local, local), local)
            columns[place, :] = slab[i]
    for p in range(mine):
        cols = slice(p * points, (p + 1) * points)
        member = columns[:, cols].astype(F32)
        mean = jnp.sum(member, axis=0, keepdims=True) / members
        deviation = member - mean
        spread = rows[p, 1:2, :points] * deviation + jnp.dot(
            root[p], deviation.astype(BF16), preferred_element_type=F32
        )
        shift = mean + product(split(rows[p]), split(spread))[0:1]
        out[:, cols] = (shift + rows[p, 2:3, :points] * spread).astype(BF16)


def body(state, hx, obs_value, obs_rinv, obs_count, loc_pattern):
    blocks, members, width = hx.shape
    patches, uses = loc_pattern.shape
    mem_total = lax.axis_size("mem")
    mine = patches // mem_total
    local, points = state.shape
    ring = lax.axis_size("lon")
    near = [(i, i + 1 - 2 * (i % 2)) for i in range(ring)]
    far = [(i, (i - 1 + 2 * (i % 2)) % ring) for i in range(ring)]
    odd = lax.axis_index("lon") % 2
    here, near_side, far_side = (
        value.astype(jnp.int32).reshape(1) for value in (lax.axis_index("mem"), 2 * odd, 2 - 2 * odd)
    )
    shape = jax.ShapeDtypeStruct
    padded = members + PAD

    span = points // mem_total
    length = mem_total // PAIR
    swap = [(i, i ^ 1) for i in range(mem_total)]
    assert mem_total & (mem_total - 1) == 0

    pattern = loc_pattern.T
    far_pattern = lax.ppermute(pattern, "lon", far)
    near_pattern = lax.ppermute(pattern, "lon", near)
    paired = lax.ppermute(state, "mem", swap)
    limit = pltpu.CompilerParams(vmem_limit_bytes=16 * 1024 * 1024)
    gram = 2 * padded * members * uses * width
    pert, weights, innov = pl.pallas_call(
        perturb_kernel,
        out_shape=(
            shape((blocks, members, width), BF16),
            shape((blocks, width), F32),
            shape((blocks, width), F32),
        ),
        in_specs=[HBM] * 4,
        out_specs=(VMEM,) * 3,
        scratch_shapes=[
            pltpu.VMEM((blocks, members, width), BF16),
            pltpu.SMEM(obs_count.shape, jnp.int32),
            pltpu.VMEM(obs_value.shape, F32),
            pltpu.VMEM(obs_rinv.shape, F32),
            pltpu.SemaphoreType.DMA((blocks // CHUNK,)),
            pltpu.SemaphoreType.DMA((3,)),
        ],
        compiler_params=limit,
        cost_estimate=pl.CostEstimate(
            flops=hx.size * 4, bytes_accessed=2 * hx.size * 2, transcendentals=0
        ),
        name="perturb",
    )(*(stay(value) for value in (obs_count, hx, obs_value, obs_rinv)))
    packed = shape((mine, padded, members // 2), BF16)
    slab = shape((PAIR, local, span), BF16)
    cost = pl.CostEstimate(flops=mine * gram, bytes_accessed=hx.size, transcendentals=0)
    to_far = pl.pallas_call(
        functools.partial(far_kernel, patches),
        out_shape=packed,
        in_specs=[SMEM] * 3 + [VMEM] * 3,
        out_specs=VMEM,
        compiler_params=limit,
        cost_estimate=cost,
        name="far_share",
    )(here, far_side, far_pattern, pert, weights, innov)
    from_far = lax.ppermute(to_far, "lon", far)
    to_near, *slabs = pl.pallas_call(
        functools.partial(near_kernel, patches),
        out_shape=(packed,) + (slab,) * length,
        in_specs=[SMEM] * 3 + [VMEM] * 3 + [HBM] * 2 + [pl.BlockSpec(memory_space=pl.ANY)],
        out_specs=(VMEM,) * (1 + length),
        scratch_shapes=[pltpu.SemaphoreType.DMA((PAIR * length,))],
        compiler_params=limit,
        cost_estimate=cost,
        name="near_share",
    )(here, near_side, near_pattern, pert, weights, innov, state, paired, to_far)
    from_near = lax.ppermute(to_near, "lon", near)
    own = pl.pallas_call(
        functools.partial(own_kernel, patches),
        out_shape=shape((mine, padded, members), F32),
        in_specs=[SMEM] * 2 + [VMEM] * 3 + [pl.BlockSpec(memory_space=pl.ANY)],
        out_specs=VMEM,
        compiler_params=limit,
        cost_estimate=cost,
        name="own_share",
    )(here, pattern, pert, weights, innov, to_near)
    for shift in range(1, length):
        trade = [(i, i ^ (shift * PAIR)) for i in range(mem_total)]
        slabs[shift] = lax.ppermute(slabs[shift], "mem", trade)
    root, rows = pl.pallas_call(
        root_kernel,
        out_shape=(shape((mine, members, members), BF16), shape((mine, PAD, members), F32)),
        in_specs=[VMEM] * 3,
        out_specs=(VMEM,) * 2,
        compiler_params=limit,
        cost_estimate=pl.CostEstimate(
            flops=mine * 15 * 2 * members**3, bytes_accessed=2**20, transcendentals=0
        ),
        name="root",
    )(own, from_far, from_near)
    updated = pl.pallas_call(
        apply_kernel,
        out_shape=shape((members, span), BF16),
        in_specs=[SMEM] + [VMEM] * (2 + length),
        out_specs=VMEM,
        scratch_shapes=[pltpu.VMEM((members, span), BF16)],
        compiler_params=limit,
        cost_estimate=pl.CostEstimate(
            flops=2 * members**2 * span, bytes_accessed=2**19, transcendentals=0
        ),
        name="apply",
    )(here, root, rows, *slabs)
    pieces = lax.all_to_all(
        updated.reshape(mem_total, local, span), "mem", split_axis=0, concat_axis=0
    )
    return jnp.swapaxes(pieces, 0, 1).reshape(local, points)


def solution(mesh):
    in_specs = (
        P("mem", "lon"),
        P("lon", None, None),
        P("lon", None),
        P("lon", None),
        P("lon"),
        P("lon", None),
    )
    out_specs = P("mem", "lon")
    return jax.shard_map(body, mesh=mesh, in_specs=in_specs, out_specs=out_specs, check_vma=False)
```

```python
import functools

import jax
import jax.numpy as jnp
from jax import lax
from jax.experimental import pallas as pl
from jax.experimental.pallas import tpu as pltpu
from jax.sharding import PartitionSpec as P

ITERS = 6
PAD = 16
CHUNK = 4
PAIR = 2
F32 = jnp.float32
BF16 = jnp.bfloat16

VMEM = pl.BlockSpec(memory_space=pltpu.VMEM)
SMEM = pl.BlockSpec(memory_space=pltpu.SMEM)
HBM = pl.BlockSpec(memory_space=pltpu.HBM)


def stay(value):
    return pltpu.with_memory_space_constraint(value, pltpu.HBM)


def split(value):
    high = value.astype(BF16)
    return high, (value - high.astype(F32)).astype(BF16)


def product(left, right):
    lhs = jnp.concatenate([left[0], left[0], left[1]], axis=1)
    rhs = jnp.concatenate([right[0], right[1], right[0]], axis=0)
    return jnp.dot(lhs, rhs, preferred_element_type=F32)


def share(pattern, row, side, patches, pert, weights, innov):
    blocks, _, width = pert.shape
    left, right = [], []
    for slot in range(pattern.shape[0]):
        position = pattern[slot, row]
        block = position - side * blocks
        here = jnp.logical_and(block >= 0, block < blocks)
        block = jnp.clip(block, 0, blocks - 1)
        spot = jnp.full((1, width), position, jnp.int32).astype(F32)
        rank = jnp.full((1, width), row, jnp.int32).astype(F32)
        offset = (spot + 0.5) / blocks - 1.0 - (rank + 0.5) / patches
        taper = jnp.exp(-0.5 * offset * offset) * jnp.where(here, 1.0, 0.0)
        picked = pert[block]
        weight = (taper * weights[pl.ds(block, 1), :]).astype(BF16)
        vector = jnp.broadcast_to(taper * innov[pl.ds(block, 1), :], (PAD, width)).astype(BF16)
        left.append(jnp.concatenate([weight * picked, vector], axis=0))
        right.append(picked)
    return lax.dot_general(
        jnp.concatenate(left, axis=1),
        jnp.concatenate(right, axis=1),
        (((1,), (1,)), ((), ())),
        preferred_element_type=F32,
    )


def perturb_kernel(
    count_all, hx, value_all, rinv_all, pert, weights, innov, raw, count, value, rinv, sems, small
):
    blocks, members, width = raw.shape
    smalls = [
        pltpu.make_async_copy(source, target, small.at[i])
        for i, (source, target) in enumerate(
            ((count_all, count), (value_all, value), (rinv_all, rinv))
        )
    ]
    copies = [
        pltpu.make_async_copy(hx.at[pl.ds(i, CHUNK)], raw.at[pl.ds(i, CHUNK)], sems.at[i // CHUNK])
        for i in range(0, blocks, CHUNK)
    ]
    for copy in smalls + copies:
        copy.start()
    for copy in smalls:
        copy.wait()
    lane = lax.broadcasted_iota(jnp.int32, (1, width), 1)
    for block in range(blocks):
        if block % CHUNK == 0:
            copies[block // CHUNK].wait()
        member = raw[block].astype(F32)
        mean = jnp.sum(member, axis=0, keepdims=True) / members
        pert[block] = (member - mean).astype(BF16)
        weight = jnp.where(lane < count[block], rinv[block : block + 1, :], 0.0)
        gap = weight * (value[block : block + 1, :] - mean)
        weights[block : block + 1, :] = weight.astype(BF16).astype(F32)
        innov[block : block + 1, :] = gap


def own_kernel(patches, here, pattern, pert, weights, innov, sent, own):
    mine = own.shape[0]
    for patch in range(mine):
        row = here[0] * mine + patch
        own[patch] = share(pattern, row, 1, patches, pert, weights, innov)


def pack(part, out, patch):
    _, padded, half = out.shape
    members = padded - PAD
    above = lax.broadcasted_iota(jnp.int32, (half, half), 0)
    across = lax.broadcasted_iota(jnp.int32, (half, half), 1)
    corner = part[half:members, half:]
    out[patch, :half, :] = part[:half, half:].astype(BF16)
    out[patch, half:members, :] = jnp.where(above >= across, part[:half, :half], corner).astype(
        BF16
    )
    diagonal = jnp.sum(jnp.where(above == across, corner, 0.0), axis=0, keepdims=True)
    force = part[members : members + 1]
    index = lax.broadcasted_iota(jnp.int32, (PAD, half), 0)
    tail = jnp.zeros((PAD, half), F32)
    for i, value in enumerate((diagonal, force[:, :half], force[:, half:])):
        high, low = split(value)
        tail = jnp.where(index == 2 * i, high.astype(F32), tail)
        tail = jnp.where(index == 2 * i + 1, low.astype(F32), tail)
    out[patch, members:, :] = tail.astype(BF16)


def far_kernel(patches, here, side, pattern, pert, weights, innov, out):
    mine = out.shape[0]
    for patch in range(mine):
        row = here[0] * mine + patch
        pack(share(pattern, row, side[0], patches, pert, weights, innov), out, patch)


def near_kernel(patches, here, side, pattern, pert, weights, innov, state, paired, sent, out, *rest):
    slabs, sems = rest[:-1], rest[-1]
    span = slabs[0].shape[2]
    length = len(slabs)
    layer, place = here[0] // PAIR, here[0] % PAIR
    moves = []
    for shift, slab in enumerate(slabs):
        target = (layer ^ shift) * PAIR + place
        cols = pl.ds(pl.multiple_of(target * span, span), span)
        moves.append((state.at[:, cols], slab.at[place]))
        moves.append((paired.at[:, cols], slab.at[1 - place]))
    moves = [pltpu.make_async_copy(*move, sems.at[i]) for i, move in enumerate(moves)]
    for move in moves:
        move.start()
    far_kernel(patches, here, side, pattern, pert, weights, innov, out)
    for move in moves:
        move.wait()


def total(value):
    return jnp.sum(jnp.sum(value, axis=0, keepdims=True), axis=1, keepdims=True)


def root_kernel(own, before, after, root_out, rows_out):
    mine, _, members = own.shape
    half = members // 2
    above = lax.broadcasted_iota(jnp.int32, (half, half), 0)
    across = lax.broadcasted_iota(jnp.int32, (half, half), 1)
    row = lax.broadcasted_iota(jnp.int32, (members, members), 0)
    col = lax.broadcasted_iota(jnp.int32, (members, members), 1)
    diagonal = row == col

    def dot(left, right):
        return jnp.dot(left, right, preferred_element_type=F32)

    each = range(mine)
    rest, factor, scale, forcing = [], [], [], []
    base = members - 1.0
    for patch in each:
        packed = before[patch].astype(F32) + after[patch].astype(F32)
        upper = packed[:half]
        mixed = packed[half:members]
        last = packed[members:]
        corner = last[0:1] + last[1:2]
        force = jnp.concatenate([last[2:3] + last[3:4], last[4:5] + last[5:6]], axis=1)
        flipped = mixed.T
        first = jnp.where(above >= across, mixed, flipped)
        second = jnp.where(above < across, mixed, flipped)
        second = jnp.where(above == across, corner, second)
        far = jnp.concatenate(
            [
                jnp.concatenate([first, upper], axis=1),
                jnp.concatenate([upper.T, second], axis=1),
            ],
            axis=0,
        )
        grams = own[patch, :members, :] + far
        trace = total(jnp.where(diagonal, grams, 0.0))
        norm = jnp.sqrt(total(grams * grams) + 2.0 * base * trace + base * base * members)
        scale.append(norm)
        forcing.append(force + own[patch, members : members + 1, :])
        factor.append(1.5 - 0.5 * (trace / members + base) / norm)
        level = trace / members
        rest.append((grams - jnp.where(diagonal, level, 0.0)) * (-0.5 / norm))
    lead, tail = list(factor), list(rest)
    small = [rest[p].astype(BF16) for p in each]
    squares = [dot(small[p], small[p]) for p in each]
    for step in range(1, ITERS):
        cubes = [dot(squares[p].astype(BF16), small[p]) for p in each]
        for p in each:
            f = factor[p]
            rest[p] = (
                (3.0 * f * f - 3.0 * f) * rest[p] + (3.0 * f - 1.5) * squares[p] + cubes[p]
            )
            factor[p] = 1.5 - 1.5 * f * f + f * f * f
            small[p] = rest[p].astype(BF16)
        for p in each:
            narrow = tail[p].astype(BF16)
            if step < ITERS - 1:
                both = dot(jnp.concatenate([small[p], narrow], axis=0), small[p])
                squares[p], cross = both[:members], both[members:]
            else:
                cross = dot(narrow, small[p])
            tail[p] = factor[p] * tail[p] + lead[p] * rest[p] + cross
            lead[p] = factor[p] * lead[p]
    for p in each:
        high = tail[p].astype(BF16)
        root_out[p] = high
        force = jnp.broadcast_to(forcing[p], (PAD, members))
        gain = (lead[p] * force + dot(force.astype(BF16), high)) / scale[p]
        index = lax.broadcasted_iota(jnp.int32, (PAD, members), 0)
        spread = jnp.sqrt(base) / jnp.sqrt(scale[p])
        rows_out[p] = jnp.where(index == 0, gain, jnp.where(index == 1, lead[p], spread))


def apply_kernel(here, root, rows, *rest):
    slabs, (out, columns) = rest[:-2], rest[-2:]
    mine, members, _ = root.shape
    points = out.shape[1] // mine
    length = len(slabs)
    _, local, _ = slabs[0].shape
    for shift, slab in enumerate(slabs):
        source = (here[0] // PAIR) ^ shift
        for i in range(PAIR):
            place = pl.ds(pl.multiple_of((source * PAIR + i) * local, local), local)
            columns[place, :] = slab[i]
    for p in range(mine):
        cols = slice(p * points, (p + 1) * points)
        member = columns[:, cols].astype(F32)
        mean = jnp.sum(member, axis=0, keepdims=True) / members
        deviation = member - mean
        spread = rows[p, 1:2, :points] * deviation + jnp.dot(
            root[p], deviation.astype(BF16), preferred_element_type=F32
        )
        shift = mean + product(split(rows[p]), split(spread))[0:1]
        out[:, cols] = (shift + rows[p, 2:3, :points] * spread).astype(BF16)


def body(state, hx, obs_value, obs_rinv, obs_count, loc_pattern):
    blocks, members, width = hx.shape
    patches, uses = loc_pattern.shape
    mem_total = lax.axis_size("mem")
    mine = patches // mem_total
    local, points = state.shape
    ring = lax.axis_size("lon")
    near = [(i, i + 1 - 2 * (i % 2)) for i in range(ring)]
    far = [(i, (i - 1 + 2 * (i % 2)) % ring) for i in range(ring)]
    odd = lax.axis_index("lon") % 2
    here, near_side, far_side = (
        value.astype(jnp.int32).reshape(1) for value in (lax.axis_index("mem"), 2 * odd, 2 - 2 * odd)
    )
    shape = jax.ShapeDtypeStruct
    padded = members + PAD

    span = points // mem_total
    length = mem_total // PAIR
    swap = [(i, i ^ 1) for i in range(mem_total)]
    assert mem_total & (mem_total - 1) == 0

    def trade(layers):
        return [(i, i ^ (layers * PAIR)) for i in range(mem_total)]


    pattern = loc_pattern.T
    far_pattern = lax.ppermute(pattern, "lon", far)
    near_pattern = lax.ppermute(pattern, "lon", near)
    paired = lax.ppermute(state, "mem", swap)
    limit = pltpu.CompilerParams(vmem_limit_bytes=16 * 1024 * 1024)
    gram = 2 * padded * members * uses * width
    pert, weights, innov = pl.pallas_call(
        perturb_kernel,
        out_shape=(
            shape((blocks, members, width), BF16),
            shape((blocks, width), F32),
            shape((blocks, width), F32),
        ),
        in_specs=[HBM] * 4,
        out_specs=(VMEM,) * 3,
        scratch_shapes=[
            pltpu.VMEM((blocks, members, width), BF16),
            pltpu.SMEM(obs_count.shape, jnp.int32),
            pltpu.VMEM(obs_value.shape, F32),
            pltpu.VMEM(obs_rinv.shape, F32),
            pltpu.SemaphoreType.DMA((blocks // CHUNK,)),
            pltpu.SemaphoreType.DMA((3,)),
        ],
        compiler_params=limit,
        cost_estimate=pl.CostEstimate(
            flops=hx.size * 4, bytes_accessed=2 * hx.size * 2, transcendentals=0
        ),
        name="perturb",
    )(*(stay(value) for value in (obs_count, hx, obs_value, obs_rinv)))
    packed = shape((mine, padded, members // 2), BF16)
    slab = shape((PAIR, local, span), BF16)
    cost = pl.CostEstimate(flops=mine * gram, bytes_accessed=hx.size, transcendentals=0)
    to_far = pl.pallas_call(
        functools.partial(far_kernel, patches),
        out_shape=packed,
        in_specs=[SMEM] * 3 + [VMEM] * 3,
        out_specs=VMEM,
        compiler_params=limit,
        cost_estimate=cost,
        name="far_share",
    )(here, far_side, far_pattern, pert, weights, innov)
    from_far = lax.ppermute(to_far, "lon", far)
    to_near, *slabs = pl.pallas_call(
        functools.partial(near_kernel, patches),
        out_shape=(packed,) + (slab,) * length,
        in_specs=[SMEM] * 3 + [VMEM] * 3 + [HBM] * 2 + [pl.BlockSpec(memory_space=pl.ANY)],
        out_specs=(VMEM,) * (1 + length),
        scratch_shapes=[pltpu.SemaphoreType.DMA((PAIR * length,))],
        compiler_params=limit,
        cost_estimate=cost,
        name="near_share",
    )(here, near_side, near_pattern, pert, weights, innov, state, paired, to_far)
    from_near = lax.ppermute(to_near, "lon", near)
    own = pl.pallas_call(
        functools.partial(own_kernel, patches),
        out_shape=shape((mine, padded, members), F32),
        in_specs=[SMEM] * 2 + [VMEM] * 3 + [pl.BlockSpec(memory_space=pl.ANY)],
        out_specs=VMEM,
        compiler_params=limit,
        cost_estimate=cost,
        name="own_share",
    )(here, pattern, pert, weights, innov, to_near)
    legs = {}
    for shift in sorted(range(1, length), key=lambda value: -value.bit_count()):
        legs[shift] = [1 << bit for bit in range(length) if shift >> bit & 1]
        slabs[shift] = lax.ppermute(slabs[shift], "mem", trade(legs[shift][0]))
    for turn in range(1, length.bit_length() - 1):
        held = [shift for shift in legs if len(legs[shift]) > turn]
        moved, _ = lax.optimization_barrier(([slabs[shift] for shift in held], own))
        for shift, slab in zip(held, moved):
            slabs[shift] = lax.ppermute(slab, "mem", trade(legs[shift][turn]))
    root, rows = pl.pallas_call(
        root_kernel,
        out_shape=(shape((mine, members, members), BF16), shape((mine, PAD, members), F32)),
        in_specs=[VMEM] * 3,
        out_specs=(VMEM,) * 2,
        compiler_params=limit,
        cost_estimate=pl.CostEstimate(
            flops=mine * 15 * 2 * members**3, bytes_accessed=2**20, transcendentals=0
        ),
        name="root",
    )(own, from_far, from_near)
    updated = pl.pallas_call(
        apply_kernel,
        out_shape=shape((members, span), BF16),
        in_specs=[SMEM] + [VMEM] * (2 + length),
        out_specs=VMEM,
        scratch_shapes=[pltpu.VMEM((members, span), BF16)],
        compiler_params=limit,
        cost_estimate=pl.CostEstimate(
            flops=2 * members**2 * span, bytes_accessed=2**19, transcendentals=0
        ),
        name="apply",
    )(here, root, rows, *slabs)
    pieces = lax.all_to_all(
        updated.reshape(mem_total, local, span), "mem", split_axis=0, concat_axis=0
    )
    return jnp.swapaxes(pieces, 0, 1).reshape(local, points)


def solution(mesh):
    in_specs = (
        P("mem", "lon"),
        P("lon", None, None),
        P("lon", None),
        P("lon", None),
        P("lon"),
        P("lon", None),
    )
    out_specs = P("mem", "lon")
    return jax.shard_map(body, mesh=mesh, in_specs=in_specs, out_specs=out_specs, check_vma=False)
```

```python
import functools

import jax
import jax.numpy as jnp
from jax import lax
from jax.experimental import pallas as pl
from jax.experimental.pallas import tpu as pltpu
from jax.sharding import PartitionSpec as P

ITERS = 6
PAD = 16
CHUNK = 4
PAIR = 2
F32 = jnp.float32
BF16 = jnp.bfloat16

VMEM = pl.BlockSpec(memory_space=pltpu.VMEM)
SMEM = pl.BlockSpec(memory_space=pltpu.SMEM)
HBM = pl.BlockSpec(memory_space=pltpu.HBM)


def stay(value):
    return pltpu.with_memory_space_constraint(value, pltpu.HBM)


def split(value):
    high = value.astype(BF16)
    return high, (value - high.astype(F32)).astype(BF16)


def product(left, right):
    lhs = jnp.concatenate([left[0], left[0], left[1]], axis=1)
    rhs = jnp.concatenate([right[0], right[1], right[0]], axis=0)
    return jnp.dot(lhs, rhs, preferred_element_type=F32)


def share(pattern, row, side, patches, pert, weights, innov):
    blocks, _, width = pert.shape
    left, right = [], []
    for slot in range(pattern.shape[0]):
        position = pattern[slot, row]
        block = position - side * blocks
        here = jnp.logical_and(block >= 0, block < blocks)
        block = jnp.clip(block, 0, blocks - 1)
        spot = jnp.full((1, width), position, jnp.int32).astype(F32)
        rank = jnp.full((1, width), row, jnp.int32).astype(F32)
        offset = (spot + 0.5) / blocks - 1.0 - (rank + 0.5) / patches
        taper = jnp.exp(-0.5 * offset * offset) * jnp.where(here, 1.0, 0.0)
        picked = pert[block]
        weight = (taper * weights[pl.ds(block, 1), :]).astype(BF16)
        vector = jnp.broadcast_to(taper * innov[pl.ds(block, 1), :], (PAD, width)).astype(BF16)
        left.append(jnp.concatenate([weight * picked, vector], axis=0))
        right.append(picked)
    return lax.dot_general(
        jnp.concatenate(left, axis=1),
        jnp.concatenate(right, axis=1),
        (((1,), (1,)), ((), ())),
        preferred_element_type=F32,
    )


def own_kernel(
    patches,
    here,
    count_all,
    pattern_all,
    hx,
    value_all,
    rinv_all,
    pert,
    weights,
    innov,
    own,
    raw,
    count,
    pattern,
    value,
    rinv,
    sems,
    small,
):
    blocks, members, width = raw.shape
    smalls = [
        pltpu.make_async_copy(source, target, small.at[i])
        for i, (source, target) in enumerate(
            ((count_all, count), (value_all, value), (rinv_all, rinv), (pattern_all, pattern))
        )
    ]
    copies = [
        pltpu.make_async_copy(hx.at[pl.ds(i, CHUNK)], raw.at[pl.ds(i, CHUNK)], sems.at[i // CHUNK])
        for i in range(0, blocks, CHUNK)
    ]
    for copy in smalls + copies:
        copy.start()
    for copy in smalls:
        copy.wait()
    lane = lax.broadcasted_iota(jnp.int32, (1, width), 1)
    for block in range(blocks):
        if block % CHUNK == 0:
            copies[block // CHUNK].wait()
        member = raw[block].astype(F32)
        mean = jnp.sum(member, axis=0, keepdims=True) / members
        pert[block] = (member - mean).astype(BF16)
        weight = jnp.where(lane < count[block], rinv[block : block + 1, :], 0.0)
        gap = weight * (value[block : block + 1, :] - mean)
        weights[block : block + 1, :] = weight.astype(BF16).astype(F32)
        innov[block : block + 1, :] = gap
    mine = own.shape[0]
    for patch in range(mine):
        row = here[0] * mine + patch
        own[patch] = share(pattern, row, 1, patches, pert, weights, innov)


def pack(part, out, patch):
    _, padded, half = out.shape
    members = padded - PAD
    above = lax.broadcasted_iota(jnp.int32, (half, half), 0)
    across = lax.broadcasted_iota(jnp.int32, (half, half), 1)
    corner = part[half:members, half:]
    out[patch, :half, :] = part[:half, half:].astype(BF16)
    out[patch, half:members, :] = jnp.where(above >= across, part[:half, :half], corner).astype(
        BF16
    )
    diagonal = jnp.sum(jnp.where(above == across, corner, 0.0), axis=0, keepdims=True)
    force = part[members : members + 1]
    index = lax.broadcasted_iota(jnp.int32, (PAD, half), 0)
    tail = jnp.zeros((PAD, half), F32)
    for i, value in enumerate((diagonal, force[:, :half], force[:, half:])):
        high, low = split(value)
        tail = jnp.where(index == 2 * i, high.astype(F32), tail)
        tail = jnp.where(index == 2 * i + 1, low.astype(F32), tail)
    out[patch, members:, :] = tail.astype(BF16)


def far_kernel(patches, here, side, pattern, pert, weights, innov, out):
    mine = out.shape[0]
    for patch in range(mine):
        row = here[0] * mine + patch
        pack(share(pattern, row, side[0], patches, pert, weights, innov), out, patch)


def near_kernel(patches, here, side, pattern, pert, weights, innov, state, paired, sent, out, *rest):
    slabs, sems = rest[:-1], rest[-1]
    span = slabs[0].shape[2]
    length = len(slabs)
    layer, place = here[0] // PAIR, here[0] % PAIR
    moves = []
    for shift, slab in enumerate(slabs):
        target = (layer ^ shift) * PAIR + place
        cols = pl.ds(pl.multiple_of(target * span, span), span)
        moves.append((state.at[:, cols], slab.at[place]))
        moves.append((paired.at[:, cols], slab.at[1 - place]))
    moves = [pltpu.make_async_copy(*move, sems.at[i]) for i, move in enumerate(moves)]
    for move in moves:
        move.start()
    far_kernel(patches, here, side, pattern, pert, weights, innov, out)
    for move in moves:
        move.wait()


def total(value):
    return jnp.sum(jnp.sum(value, axis=0, keepdims=True), axis=1, keepdims=True)


def root_kernel(own, before, after, root_out, rows_out):
    mine, _, members = own.shape
    half = members // 2
    above = lax.broadcasted_iota(jnp.int32, (half, half), 0)
    across = lax.broadcasted_iota(jnp.int32, (half, half), 1)
    row = lax.broadcasted_iota(jnp.int32, (members, members), 0)
    col = lax.broadcasted_iota(jnp.int32, (members, members), 1)
    diagonal = row == col

    def dot(left, right):
        return jnp.dot(left, right, preferred_element_type=F32)

    each = range(mine)
    rest, factor, scale, forcing = [], [], [], []
    base = members - 1.0
    for patch in each:
        packed = before[patch].astype(F32) + after[patch].astype(F32)
        upper = packed[:half]
        mixed = packed[half:members]
        last = packed[members:]
        corner = last[0:1] + last[1:2]
        force = jnp.concatenate([last[2:3] + last[3:4], last[4:5] + last[5:6]], axis=1)
        flipped = mixed.T
        first = jnp.where(above >= across, mixed, flipped)
        second = jnp.where(above < across, mixed, flipped)
        second = jnp.where(above == across, corner, second)
        far = jnp.concatenate(
            [
                jnp.concatenate([first, upper], axis=1),
                jnp.concatenate([upper.T, second], axis=1),
            ],
            axis=0,
        )
        grams = own[patch, :members, :] + far
        trace = total(jnp.where(diagonal, grams, 0.0))
        norm = jnp.sqrt(total(grams * grams) + 2.0 * base * trace + base * base * members)
        scale.append(norm)
        forcing.append(force + own[patch, members : members + 1, :])
        factor.append(1.5 - 0.5 * (trace / members + base) / norm)
        level = trace / members
        rest.append((grams - jnp.where(diagonal, level, 0.0)) * (-0.5 / norm))
    lead, tail = list(factor), list(rest)
    small = [rest[p].astype(BF16) for p in each]
    squares = [dot(small[p], small[p]) for p in each]
    for step in range(1, ITERS):
        cubes = [dot(squares[p].astype(BF16), small[p]) for p in each]
        for p in each:
            f = factor[p]
            rest[p] = (
                (3.0 * f * f - 3.0 * f) * rest[p] + (3.0 * f - 1.5) * squares[p] + cubes[p]
            )
            factor[p] = 1.5 - 1.5 * f * f + f * f * f
            small[p] = rest[p].astype(BF16)
        for p in each:
            narrow = tail[p].astype(BF16)
            if step < ITERS - 1:
                both = dot(jnp.concatenate([small[p], narrow], axis=0), small[p])
                squares[p], cross = both[:members], both[members:]
            else:
                cross = dot(narrow, small[p])
            tail[p] = factor[p] * tail[p] + lead[p] * rest[p] + cross
            lead[p] = factor[p] * lead[p]
    for p in each:
        high = tail[p].astype(BF16)
        root_out[p] = high
        force = jnp.broadcast_to(forcing[p], (PAD, members))
        gain = (lead[p] * force + dot(force.astype(BF16), high)) / scale[p]
        index = lax.broadcasted_iota(jnp.int32, (PAD, members), 0)
        spread = jnp.sqrt(base) / jnp.sqrt(scale[p])
        rows_out[p] = jnp.where(index == 0, gain, jnp.where(index == 1, lead[p], spread))


def apply_kernel(here, root, rows, *rest):
    slabs, (out, columns) = rest[:-2], rest[-2:]
    mine, members, _ = root.shape
    points = out.shape[1] // mine
    length = len(slabs)
    _, local, _ = slabs[0].shape
    for shift, slab in enumerate(slabs):
        source = (here[0] // PAIR) ^ shift
        for i in range(PAIR):
            place = pl.ds(pl.multiple_of((source * PAIR + i) * local, local), local)
            columns[place, :] = slab[i]
    for p in range(mine):
        cols = slice(p * points, (p + 1) * points)
        member = columns[:, cols].astype(F32)
        mean = jnp.sum(member, axis=0, keepdims=True) / members
        deviation = member - mean
        spread = rows[p, 1:2, :points] * deviation + jnp.dot(
            root[p], deviation.astype(BF16), preferred_element_type=F32
        )
        shift = mean + product(split(rows[p]), split(spread))[0:1]
        out[:, cols] = (shift + rows[p, 2:3, :points] * spread).astype(BF16)


def body(state, hx, obs_value, obs_rinv, obs_count, loc_pattern):
    blocks, members, width = hx.shape
    patches, uses = loc_pattern.shape
    mem_total = lax.axis_size("mem")
    mine = patches // mem_total
    local, points = state.shape
    ring = lax.axis_size("lon")
    near = [(i, i + 1 - 2 * (i % 2)) for i in range(ring)]
    far = [(i, (i - 1 + 2 * (i % 2)) % ring) for i in range(ring)]
    odd = lax.axis_index("lon") % 2
    here, near_side, far_side = (
        value.astype(jnp.int32).reshape(1) for value in (lax.axis_index("mem"), 2 * odd, 2 - 2 * odd)
    )
    shape = jax.ShapeDtypeStruct
    padded = members + PAD

    span = points // mem_total
    length = mem_total // PAIR
    swap = [(i, i ^ 1) for i in range(mem_total)]
    assert mem_total & (mem_total - 1) == 0

    pattern = loc_pattern.T
    far_pattern = lax.ppermute(pattern, "lon", far)
    near_pattern = lax.ppermute(pattern, "lon", near)
    paired = lax.ppermute(state, "mem", swap)
    limit = pltpu.CompilerParams(vmem_limit_bytes=16 * 1024 * 1024)
    gram = 2 * padded * members * uses * width
    pert, weights, innov, own = pl.pallas_call(
        functools.partial(own_kernel, patches),
        out_shape=(
            shape((blocks, members, width), BF16),
            shape((blocks, width), F32),
            shape((blocks, width), F32),
            shape((mine, padded, members), F32),
        ),
        in_specs=[SMEM] + [HBM] * 5,
        out_specs=(VMEM,) * 4,
        scratch_shapes=[
            pltpu.VMEM((blocks, members, width), BF16),
            pltpu.SMEM(obs_count.shape, jnp.int32),
            pltpu.SMEM(pattern.shape, jnp.int32),
            pltpu.VMEM(obs_value.shape, F32),
            pltpu.VMEM(obs_rinv.shape, F32),
            pltpu.SemaphoreType.DMA((blocks // CHUNK,)),
            pltpu.SemaphoreType.DMA((4,)),
        ],
        compiler_params=limit,
        cost_estimate=pl.CostEstimate(
            flops=hx.size * 4 + mine * gram, bytes_accessed=2 * hx.size * 2, transcendentals=0
        ),
        name="own_share",
    )(here, *(stay(value) for value in (obs_count, pattern, hx, obs_value, obs_rinv)))
    packed = shape((mine, padded, members // 2), BF16)
    slab = shape((PAIR, local, span), BF16)
    cost = pl.CostEstimate(flops=mine * gram, bytes_accessed=hx.size, transcendentals=0)
    to_far = pl.pallas_call(
        functools.partial(far_kernel, patches),
        out_shape=packed,
        in_specs=[SMEM] * 3 + [VMEM] * 3,
        out_specs=VMEM,
        compiler_params=limit,
        cost_estimate=cost,
        name="far_share",
    )(here, far_side, far_pattern, pert, weights, innov)
    from_far = lax.ppermute(to_far, "lon", far)
    to_near, *slabs = pl.pallas_call(
        functools.partial(near_kernel, patches),
        out_shape=(packed,) + (slab,) * length,
        in_specs=[SMEM] * 3 + [VMEM] * 3 + [HBM] * 2 + [pl.BlockSpec(memory_space=pl.ANY)],
        out_specs=(VMEM,) * (1 + length),
        scratch_shapes=[pltpu.SemaphoreType.DMA((PAIR * length,))],
        compiler_params=limit,
        cost_estimate=cost,
        name="near_share",
    )(here, near_side, near_pattern, pert, weights, innov, state, paired, to_far)
    from_near = lax.ppermute(to_near, "lon", near)
    for shift in [*range(2, length), 1]:
        trade = [(i, i ^ (shift * PAIR)) for i in range(mem_total)]
        slabs[shift] = lax.ppermute(slabs[shift], "mem", trade)
    root, rows = pl.pallas_call(
        root_kernel,
        out_shape=(shape((mine, members, members), BF16), shape((mine, PAD, members), F32)),
        in_specs=[VMEM] * 3,
        out_specs=(VMEM,) * 2,
        compiler_params=limit,
        cost_estimate=pl.CostEstimate(
            flops=mine * 15 * 2 * members**3, bytes_accessed=2**20, transcendentals=0
        ),
        name="root",
    )(own, from_far, from_near)
    updated = pl.pallas_call(
        apply_kernel,
        out_shape=shape((members, span), BF16),
        in_specs=[SMEM] + [VMEM] * (2 + length),
        out_specs=VMEM,
        scratch_shapes=[pltpu.VMEM((members, span), BF16)],
        compiler_params=limit,
        cost_estimate=pl.CostEstimate(
            flops=2 * members**2 * span, bytes_accessed=2**19, transcendentals=0
        ),
        name="apply",
    )(here, root, rows, *slabs)
    pieces = lax.all_to_all(
        updated.reshape(mem_total, local, span), "mem", split_axis=0, concat_axis=0
    )
    return jnp.swapaxes(pieces, 0, 1).reshape(local, points)


def solution(mesh):
    in_specs = (
        P("mem", "lon"),
        P("lon", None, None),
        P("lon", None),
        P("lon", None),
        P("lon"),
        P("lon", None),
    )
    out_specs = P("mem", "lon")
    return jax.shard_map(body, mesh=mesh, in_specs=in_specs, out_specs=out_specs, check_vma=False)
```

```python
import functools

import jax
import jax.numpy as jnp
from jax import lax
from jax.experimental import pallas as pl
from jax.experimental.pallas import tpu as pltpu
from jax.sharding import PartitionSpec as P

ITERS = 6
PAD = 16
CHUNK = 4
PAIR = 2
F32 = jnp.float32
BF16 = jnp.bfloat16

VMEM = pl.BlockSpec(memory_space=pltpu.VMEM)
SMEM = pl.BlockSpec(memory_space=pltpu.SMEM)
HBM = pl.BlockSpec(memory_space=pltpu.HBM)


def turns(length):
    return [0, *range(2, length), 1][:length]


def stay(value):
    return pltpu.with_memory_space_constraint(value, pltpu.HBM)


def split(value):
    high = value.astype(BF16)
    return high, (value - high.astype(F32)).astype(BF16)


def product(left, right):
    lhs = jnp.concatenate([left[0], left[0], left[1]], axis=1)
    rhs = jnp.concatenate([right[0], right[1], right[0]], axis=0)
    return jnp.dot(lhs, rhs, preferred_element_type=F32)


def share(pattern, row, side, patches, pert, weights, innov):
    blocks, _, width = pert.shape
    left, right = [], []
    for slot in range(pattern.shape[0]):
        position = pattern[slot, row]
        block = position - side * blocks
        here = jnp.logical_and(block >= 0, block < blocks)
        block = jnp.clip(block, 0, blocks - 1)
        spot = jnp.full((1, width), position, jnp.int32).astype(F32)
        rank = jnp.full((1, width), row, jnp.int32).astype(F32)
        offset = (spot + 0.5) / blocks - 1.0 - (rank + 0.5) / patches
        taper = jnp.exp(-0.5 * offset * offset) * jnp.where(here, 1.0, 0.0)
        picked = pert[block]
        weight = (taper * weights[pl.ds(block, 1), :]).astype(BF16)
        vector = jnp.broadcast_to(taper * innov[pl.ds(block, 1), :], (PAD, width)).astype(BF16)
        left.append(jnp.concatenate([weight * picked, vector], axis=0))
        right.append(picked)
    return lax.dot_general(
        jnp.concatenate(left, axis=1),
        jnp.concatenate(right, axis=1),
        (((1,), (1,)), ((), ())),
        preferred_element_type=F32,
    )


def own_kernel(
    patches,
    here,
    count_all,
    pattern_all,
    hx,
    value_all,
    rinv_all,
    pert,
    weights,
    innov,
    own,
    raw,
    count,
    pattern,
    value,
    rinv,
    sems,
    small,
):
    blocks, members, width = raw.shape
    smalls = [
        pltpu.make_async_copy(source, target, small.at[i])
        for i, (source, target) in enumerate(
            ((count_all, count), (value_all, value), (rinv_all, rinv), (pattern_all, pattern))
        )
    ]
    copies = [
        pltpu.make_async_copy(hx.at[pl.ds(i, CHUNK)], raw.at[pl.ds(i, CHUNK)], sems.at[i // CHUNK])
        for i in range(0, blocks, CHUNK)
    ]
    for copy in smalls + copies:
        copy.start()
    for copy in smalls:
        copy.wait()
    lane = lax.broadcasted_iota(jnp.int32, (1, width), 1)
    for block in range(blocks):
        if block % CHUNK == 0:
            copies[block // CHUNK].wait()
        member = raw[block].astype(F32)
        mean = jnp.sum(member, axis=0, keepdims=True) / members
        pert[block] = (member - mean).astype(BF16)
        weight = jnp.where(lane < count[block], rinv[block : block + 1, :], 0.0)
        gap = weight * (value[block : block + 1, :] - mean)
        weights[block : block + 1, :] = weight.astype(BF16).astype(F32)
        innov[block : block + 1, :] = gap
    mine = own.shape[0]
    for patch in range(mine):
        row = here[0] * mine + patch
        own[patch] = share(pattern, row, 1, patches, pert, weights, innov)


def pack(part, out, patch):
    _, padded, half = out.shape
    members = padded - PAD
    above = lax.broadcasted_iota(jnp.int32, (half, half), 0)
    across = lax.broadcasted_iota(jnp.int32, (half, half), 1)
    corner = part[half:members, half:]
    out[patch, :half, :] = part[:half, half:].astype(BF16)
    out[patch, half:members, :] = jnp.where(above >= across, part[:half, :half], corner).astype(
        BF16
    )
    diagonal = jnp.sum(jnp.where(above == across, corner, 0.0), axis=0, keepdims=True)
    force = part[members : members + 1]
    index = lax.broadcasted_iota(jnp.int32, (PAD, half), 0)
    tail = jnp.zeros((PAD, half), F32)
    for i, value in enumerate((diagonal, force[:, :half], force[:, half:])):
        high, low = split(value)
        tail = jnp.where(index == 2 * i, high.astype(F32), tail)
        tail = jnp.where(index == 2 * i + 1, low.astype(F32), tail)
    out[patch, members:, :] = tail.astype(BF16)


def far_kernel(patches, here, side, pattern, pert, weights, innov, out):
    mine = out.shape[0]
    for patch in range(mine):
        row = here[0] * mine + patch
        pack(share(pattern, row, side[0], patches, pert, weights, innov), out, patch)


def near_kernel(patches, here, side, pattern, pert, weights, innov, state, paired, sent, out, *rest):
    slabs, sems = rest[:-1], rest[-1]
    span = slabs[0].shape[2]
    length = len(slabs)
    layer, place = here[0] // PAIR, here[0] % PAIR
    moves = []
    for shift, slab in zip(turns(length), slabs):
        target = (layer ^ shift) * PAIR + place
        cols = pl.ds(pl.multiple_of(target * span, span), span)
        moves.append((state.at[:, cols], slab.at[place]))
        moves.append((paired.at[:, cols], slab.at[1 - place]))
    moves = [pltpu.make_async_copy(*move, sems.at[i]) for i, move in enumerate(moves)]
    for move in moves:
        move.start()
    far_kernel(patches, here, side, pattern, pert, weights, innov, out)
    for move in moves:
        move.wait()


def total(value):
    return jnp.sum(jnp.sum(value, axis=0, keepdims=True), axis=1, keepdims=True)


def root_kernel(own, before, after, root_out, rows_out):
    mine, _, members = own.shape
    half = members // 2
    above = lax.broadcasted_iota(jnp.int32, (half, half), 0)
    across = lax.broadcasted_iota(jnp.int32, (half, half), 1)
    row = lax.broadcasted_iota(jnp.int32, (members, members), 0)
    col = lax.broadcasted_iota(jnp.int32, (members, members), 1)
    diagonal = row == col

    def dot(left, right):
        return jnp.dot(left, right, preferred_element_type=F32)

    each = range(mine)
    rest, factor, scale, forcing = [], [], [], []
    base = members - 1.0
    for patch in each:
        packed = before[patch].astype(F32) + after[patch].astype(F32)
        upper = packed[:half]
        mixed = packed[half:members]
        last = packed[members:]
        corner = last[0:1] + last[1:2]
        force = jnp.concatenate([last[2:3] + last[3:4], last[4:5] + last[5:6]], axis=1)
        flipped = mixed.T
        first = jnp.where(above >= across, mixed, flipped)
        second = jnp.where(above < across, mixed, flipped)
        second = jnp.where(above == across, corner, second)
        far = jnp.concatenate(
            [
                jnp.concatenate([first, upper], axis=1),
                jnp.concatenate([upper.T, second], axis=1),
            ],
            axis=0,
        )
        grams = own[patch, :members, :] + far
        blocks = grams[:half, :half] + grams[half:, half:]
        trace = total(jnp.where(above == across, blocks, 0.0))
        norm = jnp.sqrt(total(grams * grams) + 2.0 * base * trace + base * base * members)
        scale.append(norm)
        forcing.append(force + own[patch, members : members + 1, :])
        factor.append(1.5 - 0.5 * (trace / members + base) / norm)
        level = trace / members
        rest.append((grams - jnp.where(diagonal, level, 0.0)) * (-0.5 / norm))
    small = [rest[p].astype(BF16) for p in each]
    lead, tail = list(factor), list(small)
    squares = [dot(small[p], small[p]) for p in each]
    for step in range(1, ITERS):
        cubes = [dot(squares[p].astype(BF16), small[p]) for p in each]
        for p in each:
            f = factor[p]
            rest[p] = (
                (3.0 * f * f - 3.0 * f) * rest[p] + (3.0 * f - 1.5) * squares[p] + cubes[p]
            )
            factor[p] = 1.5 - 1.5 * f * f + f * f * f
            small[p] = rest[p].astype(BF16)
        for p in each:
            narrow = tail[p]
            if step < ITERS - 1:
                both = dot(jnp.concatenate([small[p], narrow], axis=0), small[p])
                squares[p], cross = both[:members], both[members:]
            else:
                cross = dot(narrow, small[p])
            tail[p] = (factor[p] * narrow.astype(F32) + lead[p] * rest[p] + cross).astype(BF16)
            lead[p] = factor[p] * lead[p]
    for p in each:
        high = tail[p]
        root_out[p] = high
        force = jnp.broadcast_to(forcing[p], (PAD, members))
        gain = (lead[p] * force + dot(force.astype(BF16), high)) / scale[p]
        index = lax.broadcasted_iota(jnp.int32, (PAD, members), 0)
        spread = jnp.sqrt(base) / jnp.sqrt(scale[p])
        rows_out[p] = jnp.where(index == 0, gain, jnp.where(index == 1, lead[p], spread))


def apply_kernel(here, root, rows, *rest):
    slabs, (out, columns) = rest[:-2], rest[-2:]
    mine, members, _ = root.shape
    points = out.shape[1] // mine
    length = len(slabs)
    _, local, _ = slabs[0].shape
    for shift, slab in zip(turns(length), slabs):
        source = (here[0] // PAIR) ^ shift
        for i in range(PAIR):
            place = pl.ds(pl.multiple_of((source * PAIR + i) * local, local), local)
            columns[place, :] = slab[i]
    for p in range(mine):
        cols = slice(p * points, (p + 1) * points)
        member = columns[:, cols].astype(F32)
        mean = jnp.sum(member, axis=0, keepdims=True) / members
        deviation = member - mean
        spread = rows[p, 1:2, :points] * deviation + jnp.dot(
            root[p], deviation.astype(BF16), preferred_element_type=F32
        )
        shift = mean + product(split(rows[p]), split(spread))[0:1]
        out[:, cols] = (shift + rows[p, 2:3, :points] * spread).astype(BF16)


def body(state, hx, obs_value, obs_rinv, obs_count, loc_pattern):
    blocks, members, width = hx.shape
    patches, uses = loc_pattern.shape
    mem_total = lax.axis_size("mem")
    mine = patches // mem_total
    local, points = state.shape
    ring = lax.axis_size("lon")
    near = [(i, i + 1 - 2 * (i % 2)) for i in range(ring)]
    far = [(i, (i - 1 + 2 * (i % 2)) % ring) for i in range(ring)]
    odd = lax.axis_index("lon") % 2
    here, near_side, far_side = (
        value.astype(jnp.int32).reshape(1) for value in (lax.axis_index("mem"), 2 * odd, 2 - 2 * odd)
    )
    shape = jax.ShapeDtypeStruct
    padded = members + PAD

    span = points // mem_total
    length = mem_total // PAIR
    swap = [(i, i ^ 1) for i in range(mem_total)]
    assert mem_total & (mem_total - 1) == 0

    pattern = loc_pattern.T
    far_pattern = lax.ppermute(pattern, "lon", far)
    near_pattern = lax.ppermute(pattern, "lon", near)
    paired = lax.ppermute(state, "mem", swap)
    limit = pltpu.CompilerParams(vmem_limit_bytes=16 * 1024 * 1024)
    gram = 2 * padded * members * uses * width
    pert, weights, innov, own = pl.pallas_call(
        functools.partial(own_kernel, patches),
        out_shape=(
            shape((blocks, members, width), BF16),
            shape((blocks, width), F32),
            shape((blocks, width), F32),
            shape((mine, padded, members), F32),
        ),
        in_specs=[SMEM] + [HBM] * 5,
        out_specs=(VMEM,) * 4,
        scratch_shapes=[
            pltpu.VMEM((blocks, members, width), BF16),
            pltpu.SMEM(obs_count.shape, jnp.int32),
            pltpu.SMEM(pattern.shape, jnp.int32),
            pltpu.VMEM(obs_value.shape, F32),
            pltpu.VMEM(obs_rinv.shape, F32),
            pltpu.SemaphoreType.DMA((blocks // CHUNK,)),
            pltpu.SemaphoreType.DMA((4,)),
        ],
        compiler_params=limit,
        cost_estimate=pl.CostEstimate(
            flops=hx.size * 4 + mine * gram, bytes_accessed=2 * hx.size * 2, transcendentals=0
        ),
        name="own_share",
    )(here, *(stay(value) for value in (obs_count, pattern, hx, obs_value, obs_rinv)))
    packed = shape((mine, padded, members // 2), BF16)
    slab = shape((PAIR, local, span), BF16)
    cost = pl.CostEstimate(flops=mine * gram, bytes_accessed=hx.size, transcendentals=0)
    to_far = pl.pallas_call(
        functools.partial(far_kernel, patches),
        out_shape=packed,
        in_specs=[SMEM] * 3 + [VMEM] * 3,
        out_specs=VMEM,
        compiler_params=limit,
        cost_estimate=cost,
        name="far_share",
    )(here, far_side, far_pattern, pert, weights, innov)
    from_far = lax.ppermute(to_far, "lon", far)
    to_near, *slabs = pl.pallas_call(
        functools.partial(near_kernel, patches),
        out_shape=(packed,) + (slab,) * length,
        in_specs=[SMEM] * 3 + [VMEM] * 3 + [HBM] * 2 + [pl.BlockSpec(memory_space=pl.ANY)],
        out_specs=(VMEM,) * (1 + length),
        scratch_shapes=[pltpu.SemaphoreType.DMA((PAIR * length,))],
        compiler_params=limit,
        cost_estimate=cost,
        name="near_share",
    )(here, near_side, near_pattern, pert, weights, innov, state, paired, to_far)
    from_near = lax.ppermute(to_near, "lon", near)
    for i, shift in enumerate(turns(length)):
        if shift:
            trade = [(j, j ^ (shift * PAIR)) for j in range(mem_total)]
            slabs[i] = lax.ppermute(slabs[i], "mem", trade)
    root, rows = pl.pallas_call(
        root_kernel,
        out_shape=(shape((mine, members, members), BF16), shape((mine, PAD, members), F32)),
        in_specs=[VMEM] * 3,
        out_specs=(VMEM,) * 2,
        compiler_params=limit,
        cost_estimate=pl.CostEstimate(
            flops=mine * 15 * 2 * members**3, bytes_accessed=2**20, transcendentals=0
        ),
        name="root",
    )(own, from_far, from_near)
    updated = pl.pallas_call(
        apply_kernel,
        out_shape=shape((members, span), BF16),
        in_specs=[SMEM] + [VMEM] * (2 + length),
        out_specs=VMEM,
        scratch_shapes=[pltpu.VMEM((members, span), BF16)],
        compiler_params=limit,
        cost_estimate=pl.CostEstimate(
            flops=2 * members**2 * span, bytes_accessed=2**19, transcendentals=0
        ),
        name="apply",
    )(here, root, rows, *slabs)
    pieces = lax.all_to_all(
        updated.reshape(mem_total, local, span), "mem", split_axis=0, concat_axis=0
    )
    return jnp.swapaxes(pieces, 0, 1).reshape(local, points)


def solution(mesh):
    in_specs = (
        P("mem", "lon"),
        P("lon", None, None),
        P("lon", None),
        P("lon", None),
        P("lon"),
        P("lon", None),
    )
    out_specs = P("mem", "lon")
    return jax.shard_map(body, mesh=mesh, in_specs=in_specs, out_specs=out_specs, check_vma=False)
```

```python
import functools

import jax
import jax.numpy as jnp
from jax import lax
from jax.experimental import pallas as pl
from jax.experimental.pallas import tpu as pltpu
from jax.sharding import PartitionSpec as P

ITERS = 6
PAD = 16
CHUNK = 4
PAIR = 2
F32 = jnp.float32
BF16 = jnp.bfloat16

VMEM = pl.BlockSpec(memory_space=pltpu.VMEM)
SMEM = pl.BlockSpec(memory_space=pltpu.SMEM)
HBM = pl.BlockSpec(memory_space=pltpu.HBM)


def turns(length):
    return [0, *range(2, length), 1][:length]


def stay(value):
    return pltpu.with_memory_space_constraint(value, pltpu.HBM)


def split(value):
    high = value.astype(BF16)
    return high, (value - high.astype(F32)).astype(BF16)


def product(left, right):
    lhs = jnp.concatenate([left[0], left[0], left[1]], axis=1)
    rhs = jnp.concatenate([right[0], right[1], right[0]], axis=0)
    return jnp.dot(lhs, rhs, preferred_element_type=F32)


def share(pattern, row, side, patches, pert, weights, innov):
    blocks, _, width = pert.shape
    left, right = [], []
    for slot in range(pattern.shape[0]):
        position = pattern[slot, row]
        block = position - side * blocks
        here = jnp.logical_and(block >= 0, block < blocks)
        block = jnp.clip(block, 0, blocks - 1)
        spot = jnp.full((1, width), position, jnp.int32).astype(F32)
        rank = jnp.full((1, width), row, jnp.int32).astype(F32)
        offset = (spot + 0.5) / blocks - 1.0 - (rank + 0.5) / patches
        taper = jnp.exp(-0.5 * offset * offset) * jnp.where(here, 1.0, 0.0)
        picked = pert[block]
        weight = (taper * weights[pl.ds(block, 1), :]).astype(BF16)
        vector = jnp.broadcast_to(taper * innov[pl.ds(block, 1), :], (PAD, width)).astype(BF16)
        left.append(jnp.concatenate([weight * picked, vector], axis=0))
        right.append(picked)
    return lax.dot_general(
        jnp.concatenate(left, axis=1),
        jnp.concatenate(right, axis=1),
        (((1,), (1,)), ((), ())),
        preferred_element_type=F32,
    )


def first_kernel(
    patches,
    here,
    side,
    count_all,
    pattern_all,
    hx,
    value_all,
    rinv_all,
    near_all,
    pert,
    weights,
    innov,
    own,
    to_near,
    raw,
    count,
    pattern,
    near_pattern,
    value,
    rinv,
    sems,
    small,
):
    blocks, members, width = raw.shape
    smalls = [
        pltpu.make_async_copy(source, target, small.at[i])
        for i, (source, target) in enumerate(
            ((count_all, count), (value_all, value), (rinv_all, rinv), (pattern_all, pattern), (near_all, near_pattern))
        )
    ]
    copies = [
        pltpu.make_async_copy(hx.at[pl.ds(i, CHUNK)], raw.at[pl.ds(i, CHUNK)], sems.at[i // CHUNK])
        for i in range(0, blocks, CHUNK)
    ]
    for copy in smalls + copies:
        copy.start()
    for copy in smalls:
        copy.wait()
    lane = lax.broadcasted_iota(jnp.int32, (1, width), 1)
    for block in range(blocks):
        if block % CHUNK == 0:
            copies[block // CHUNK].wait()
        member = raw[block].astype(F32)
        mean = jnp.sum(member, axis=0, keepdims=True) / members
        pert[block] = (member - mean).astype(BF16)
        weight = jnp.where(lane < count[block], rinv[block : block + 1, :], 0.0)
        gap = weight * (value[block : block + 1, :] - mean)
        weights[block : block + 1, :] = weight.astype(BF16).astype(F32)
        innov[block : block + 1, :] = gap
    mine = own.shape[0]
    for patch in range(mine):
        row = here[0] * mine + patch
        own[patch] = share(pattern, row, 1, patches, pert, weights, innov)
        part = share(near_pattern, row, side[0], patches, pert, weights, innov)
        pack(part, to_near, patch)


def pack(part, out, patch):
    _, padded, half = out.shape
    members = padded - PAD
    above = lax.broadcasted_iota(jnp.int32, (half, half), 0)
    across = lax.broadcasted_iota(jnp.int32, (half, half), 1)
    corner = part[half:members, half:]
    out[patch, :half, :] = part[:half, half:].astype(BF16)
    out[patch, half:members, :] = jnp.where(above >= across, part[:half, :half], corner).astype(
        BF16
    )
    diagonal = jnp.sum(jnp.where(above == across, corner, 0.0), axis=0, keepdims=True)
    force = part[members : members + 1]
    index = lax.broadcasted_iota(jnp.int32, (PAD, half), 0)
    tail = jnp.zeros((PAD, half), F32)
    for i, value in enumerate((diagonal, force[:, :half], force[:, half:])):
        high, low = split(value)
        tail = jnp.where(index == 2 * i, high.astype(F32), tail)
        tail = jnp.where(index == 2 * i + 1, low.astype(F32), tail)
    out[patch, members:, :] = tail.astype(BF16)


def far_kernel(patches, here, side, pattern, pert, weights, innov, state, paired, out, *slabs):
    span = slabs[0].shape[2]
    length = len(slabs)
    layer, place = here[0] // PAIR, here[0] % PAIR
    for shift, slab in zip(turns(length), slabs):
        target = (layer ^ shift) * PAIR + place
        cols = pl.ds(pl.multiple_of(target * span, span), span)
        slab[place] = state[:, cols]
        slab[1 - place] = paired[:, cols]
    mine = out.shape[0]
    for patch in range(mine):
        row = here[0] * mine + patch
        pack(share(pattern, row, side[0], patches, pert, weights, innov), out, patch)


def total(value):
    return jnp.sum(jnp.sum(value, axis=0, keepdims=True), axis=1, keepdims=True)


def root_kernel(own, before, after, root_out, rows_out):
    mine, _, members = own.shape
    half = members // 2
    above = lax.broadcasted_iota(jnp.int32, (half, half), 0)
    across = lax.broadcasted_iota(jnp.int32, (half, half), 1)
    row = lax.broadcasted_iota(jnp.int32, (members, members), 0)
    col = lax.broadcasted_iota(jnp.int32, (members, members), 1)
    diagonal = row == col

    def dot(left, right):
        return jnp.dot(left, right, preferred_element_type=F32)

    each = range(mine)
    rest, factor, scale, forcing = [], [], [], []
    base = members - 1.0
    for patch in each:
        packed = before[patch].astype(F32) + after[patch].astype(F32)
        upper = packed[:half]
        mixed = packed[half:members]
        last = packed[members:]
        corner = last[0:1] + last[1:2]
        force = jnp.concatenate([last[2:3] + last[3:4], last[4:5] + last[5:6]], axis=1)
        flipped = mixed.T
        first = jnp.where(above >= across, mixed, flipped)
        second = jnp.where(above < across, mixed, flipped)
        second = jnp.where(above == across, corner, second)
        far = jnp.concatenate(
            [
                jnp.concatenate([first, upper], axis=1),
                jnp.concatenate([upper.T, second], axis=1),
            ],
            axis=0,
        )
        grams = own[patch, :members, :] + far
        blocks = grams[:half, :half] + grams[half:, half:]
        trace = total(jnp.where(above == across, blocks, 0.0))
        norm = jnp.sqrt(total(grams * grams) + 2.0 * base * trace + base * base * members)
        scale.append(norm)
        forcing.append(force + own[patch, members : members + 1, :])
        factor.append(1.5 - 0.5 * (trace / members + base) / norm)
        level = trace / members
        rest.append((grams - jnp.where(diagonal, level, 0.0)) * (-0.5 / norm))
    small = [rest[p].astype(BF16) for p in each]
    lead, tail = list(factor), list(small)
    squares = [dot(small[p], small[p]) for p in each]
    for step in range(1, ITERS):
        cubes = [dot(squares[p].astype(BF16), small[p]) for p in each]
        for p in each:
            f = factor[p]
            rest[p] = (
                (3.0 * f * f - 3.0 * f) * rest[p] + (3.0 * f - 1.5) * squares[p] + cubes[p]
            )
            factor[p] = 1.5 - 1.5 * f * f + f * f * f
            small[p] = rest[p].astype(BF16)
        for p in each:
            narrow = tail[p]
            if step < ITERS - 1:
                both = dot(jnp.concatenate([small[p], narrow], axis=0), small[p])
                squares[p], cross = both[:members], both[members:]
            else:
                cross = dot(narrow, small[p])
            tail[p] = (factor[p] * narrow.astype(F32) + lead[p] * rest[p] + cross).astype(BF16)
            lead[p] = factor[p] * lead[p]
    for p in each:
        high = tail[p]
        root_out[p] = high
        force = jnp.broadcast_to(forcing[p], (PAD, members))
        gain = (lead[p] * force + dot(force.astype(BF16), high)) / scale[p]
        index = lax.broadcasted_iota(jnp.int32, (PAD, members), 0)
        spread = jnp.sqrt(base) / jnp.sqrt(scale[p])
        rows_out[p] = jnp.where(index == 0, gain, jnp.where(index == 1, lead[p], spread))


def apply_kernel(here, root, rows, *rest):
    slabs, (out, columns) = rest[:-2], rest[-2:]
    mine, members, _ = root.shape
    points = out.shape[1] // mine
    length = len(slabs)
    _, local, _ = slabs[0].shape
    for shift, slab in zip(turns(length), slabs):
        source = (here[0] // PAIR) ^ shift
        for i in range(PAIR):
            place = pl.ds(pl.multiple_of((source * PAIR + i) * local, local), local)
            columns[place, :] = slab[i]
    for p in range(mine):
        cols = slice(p * points, (p + 1) * points)
        member = columns[:, cols].astype(F32)
        mean = jnp.sum(member, axis=0, keepdims=True) / members
        deviation = member - mean
        spread = rows[p, 1:2, :points] * deviation + jnp.dot(
            root[p], deviation.astype(BF16), preferred_element_type=F32
        )
        shift = mean + product(split(rows[p]), split(spread))[0:1]
        out[:, cols] = (shift + rows[p, 2:3, :points] * spread).astype(BF16)


def body(state, hx, obs_value, obs_rinv, obs_count, loc_pattern):
    blocks, members, width = hx.shape
    patches, uses = loc_pattern.shape
    mem_total = lax.axis_size("mem")
    mine = patches // mem_total
    local, points = state.shape
    ring = lax.axis_size("lon")
    near = [(i, i + 1 - 2 * (i % 2)) for i in range(ring)]
    far = [(i, (i - 1 + 2 * (i % 2)) % ring) for i in range(ring)]
    odd = lax.axis_index("lon") % 2
    here, near_side, far_side = (
        value.astype(jnp.int32).reshape(1) for value in (lax.axis_index("mem"), 2 * odd, 2 - 2 * odd)
    )
    shape = jax.ShapeDtypeStruct
    padded = members + PAD

    span = points // mem_total
    length = mem_total // PAIR
    swap = [(i, i ^ 1) for i in range(mem_total)]
    assert mem_total & (mem_total - 1) == 0

    pattern = loc_pattern.T
    near_pattern = lax.ppermute(pattern, "lon", near)
    far_pattern = lax.ppermute(pattern, "lon", far)
    paired = lax.ppermute(state, "mem", swap)
    limit = pltpu.CompilerParams(vmem_limit_bytes=16 * 1024 * 1024)
    gram = 2 * padded * members * uses * width
    packed = shape((mine, padded, members // 2), BF16)
    slab = shape((PAIR, local, span), BF16)
    pert, weights, innov, own, to_near = pl.pallas_call(
        functools.partial(first_kernel, patches),
        out_shape=(
            shape((blocks, members, width), BF16),
            shape((blocks, width), F32),
            shape((blocks, width), F32),
            shape((mine, padded, members), F32),
            packed,
        ),
        in_specs=[SMEM] * 2 + [HBM] * 5 + [pl.BlockSpec(memory_space=pl.ANY)],
        out_specs=(VMEM,) * 5,
        scratch_shapes=[
            pltpu.VMEM((blocks, members, width), BF16),
            pltpu.SMEM(obs_count.shape, jnp.int32),
            pltpu.SMEM(pattern.shape, jnp.int32),
            pltpu.SMEM(pattern.shape, jnp.int32),
            pltpu.VMEM(obs_value.shape, F32),
            pltpu.VMEM(obs_rinv.shape, F32),
            pltpu.SemaphoreType.DMA((blocks // CHUNK,)),
            pltpu.SemaphoreType.DMA((5,)),
        ],
        compiler_params=limit,
        cost_estimate=pl.CostEstimate(
            flops=hx.size * 4 + 2 * mine * gram, bytes_accessed=4 * hx.size, transcendentals=0
        ),
        name="first_shares",
    )(
        here,
        near_side,
        *(stay(value) for value in (obs_count, pattern, hx, obs_value, obs_rinv)),
        near_pattern,
    )
    to_far, *slabs = pl.pallas_call(
        functools.partial(far_kernel, patches),
        out_shape=(packed,) + (slab,) * length,
        in_specs=[SMEM] * 3 + [VMEM] * 5,
        out_specs=(VMEM,) * (1 + length),
        compiler_params=limit,
        cost_estimate=pl.CostEstimate(
            flops=mine * gram, bytes_accessed=hx.size, transcendentals=0
        ),
        name="far_share",
    )(here, far_side, far_pattern, pert, weights, innov, state, paired)
    from_far = lax.ppermute(to_far, "lon", far)
    from_near = lax.ppermute(lax.optimization_barrier((to_near, to_far))[0], "lon", near)
    for i, shift in enumerate(turns(length)):
        if shift:
            trade = [(j, j ^ (shift * PAIR)) for j in range(mem_total)]
            slabs[i] = lax.ppermute(slabs[i], "mem", trade)
    root, rows = pl.pallas_call(
        root_kernel,
        out_shape=(shape((mine, members, members), BF16), shape((mine, PAD, members), F32)),
        in_specs=[VMEM] * 3,
        out_specs=(VMEM,) * 2,
        compiler_params=limit,
        cost_estimate=pl.CostEstimate(
            flops=mine * 15 * 2 * members**3, bytes_accessed=2**20, transcendentals=0
        ),
        name="root",
    )(own, from_near, from_far)
    updated = pl.pallas_call(
        apply_kernel,
        out_shape=shape((members, span), BF16),
        in_specs=[SMEM] + [VMEM] * (2 + length),
        out_specs=VMEM,
        scratch_shapes=[pltpu.VMEM((members, span), BF16)],
        compiler_params=limit,
        cost_estimate=pl.CostEstimate(
            flops=2 * members**2 * span, bytes_accessed=2**19, transcendentals=0
        ),
        name="apply",
    )(here, root, rows, *slabs)
    pieces = lax.all_to_all(
        updated.reshape(mem_total, local, span), "mem", split_axis=0, concat_axis=0
    )
    return jnp.swapaxes(pieces, 0, 1).reshape(local, points)


def solution(mesh):
    in_specs = (
        P("mem", "lon"),
        P("lon", None, None),
        P("lon", None),
        P("lon", None),
        P("lon"),
        P("lon", None),
    )
    out_specs = P("mem", "lon")
    return jax.shard_map(body, mesh=mesh, in_specs=in_specs, out_specs=out_specs, check_vma=False)
```

```python
import functools

import jax
import jax.numpy as jnp
from jax import lax
from jax.experimental import pallas as pl
from jax.experimental.pallas import tpu as pltpu
from jax.sharding import PartitionSpec as P

ITERS = 6
PAD = 16
CHUNK = 4
PAIR = 2
F32 = jnp.float32
BF16 = jnp.bfloat16

VMEM = pl.BlockSpec(memory_space=pltpu.VMEM)
SMEM = pl.BlockSpec(memory_space=pltpu.SMEM)
HBM = pl.BlockSpec(memory_space=pltpu.HBM)


def turns(length):
    return [0, *range(2, length), 1][:length]


def stay(value):
    return pltpu.with_memory_space_constraint(value, pltpu.HBM)


def split(value):
    high = value.astype(BF16)
    return high, (value - high.astype(F32)).astype(BF16)


def product(left, right):
    lhs = jnp.concatenate([left[0], left[0], left[1]], axis=1)
    rhs = jnp.concatenate([right[0], right[1], right[0]], axis=0)
    return jnp.dot(lhs, rhs, preferred_element_type=F32)


def share(pattern, row, side, patches, pert, weights, innov):
    blocks, _, width = pert.shape
    left, right = [], []
    for slot in range(pattern.shape[0]):
        position = pattern[slot, row]
        block = position - side * blocks
        here = jnp.logical_and(block >= 0, block < blocks)
        block = jnp.clip(block, 0, blocks - 1)
        spot = jnp.full((1, width), position, jnp.int32).astype(F32)
        rank = jnp.full((1, width), row, jnp.int32).astype(F32)
        offset = (spot + 0.5) / blocks - 1.0 - (rank + 0.5) / patches
        taper = jnp.exp(-0.5 * offset * offset) * jnp.where(here, 1.0, 0.0)
        picked = pert[block]
        weight = (taper * weights[pl.ds(block, 1), :]).astype(BF16)
        vector = jnp.broadcast_to(taper * innov[pl.ds(block, 1), :], (PAD, width)).astype(BF16)
        left.append(jnp.concatenate([weight * picked, vector], axis=0))
        right.append(picked)
    return lax.dot_general(
        jnp.concatenate(left, axis=1),
        jnp.concatenate(right, axis=1),
        (((1,), (1,)), ((), ())),
        preferred_element_type=F32,
    )


def own_kernel(
    patches,
    here,
    count_all,
    pattern_all,
    hx,
    value_all,
    rinv_all,
    state,
    pert,
    weights,
    innov,
    own,
    half,
    raw,
    count,
    pattern,
    value,
    rinv,
    sems,
    small,
    cut,
):
    blocks, members, width = raw.shape
    smalls = [
        pltpu.make_async_copy(source, target, small.at[i])
        for i, (source, target) in enumerate(
            ((count_all, count), (value_all, value), (rinv_all, rinv), (pattern_all, pattern))
        )
    ]
    copies = [
        pltpu.make_async_copy(hx.at[pl.ds(i, CHUNK)], raw.at[pl.ds(i, CHUNK)], sems.at[i // CHUNK])
        for i in range(0, blocks, CHUNK)
    ]
    length, _, span = half.shape
    cuts = []
    for layer in range(length):
        start = (layer * PAIR + 1 - here[0] % PAIR) * span
        cols = pl.ds(pl.multiple_of(start, span), span)
        cuts.append(pltpu.make_async_copy(state.at[:, cols], half.at[layer], cut.at[layer]))
    for copy in smalls + copies + cuts:
        copy.start()
    for copy in smalls:
        copy.wait()
    lane = lax.broadcasted_iota(jnp.int32, (1, width), 1)
    for block in range(blocks):
        if block % CHUNK == 0:
            copies[block // CHUNK].wait()
        member = raw[block].astype(F32)
        mean = jnp.sum(member, axis=0, keepdims=True) / members
        pert[block] = (member - mean).astype(BF16)
        weight = jnp.where(lane < count[block], rinv[block : block + 1, :], 0.0)
        gap = weight * (value[block : block + 1, :] - mean)
        weights[block : block + 1, :] = weight.astype(BF16).astype(F32)
        innov[block : block + 1, :] = gap
    mine = own.shape[0]
    for patch in range(mine):
        row = here[0] * mine + patch
        own[patch] = share(pattern, row, 1, patches, pert, weights, innov)
    for copy in cuts:
        copy.wait()


def pack(part, out, patch):
    _, padded, half = out.shape
    members = padded - PAD
    above = lax.broadcasted_iota(jnp.int32, (half, half), 0)
    across = lax.broadcasted_iota(jnp.int32, (half, half), 1)
    corner = part[half:members, half:]
    out[patch, :half, :] = part[:half, half:].astype(BF16)
    out[patch, half:members, :] = jnp.where(above >= across, part[:half, :half], corner).astype(
        BF16
    )
    diagonal = jnp.sum(jnp.where(above == across, corner, 0.0), axis=0, keepdims=True)
    force = part[members : members + 1]
    index = lax.broadcasted_iota(jnp.int32, (PAD, half), 0)
    tail = jnp.zeros((PAD, half), F32)
    for i, value in enumerate((diagonal, force[:, :half], force[:, half:])):
        high, low = split(value)
        tail = jnp.where(index == 2 * i, high.astype(F32), tail)
        tail = jnp.where(index == 2 * i + 1, low.astype(F32), tail)
    out[patch, members:, :] = tail.astype(BF16)


def far_kernel(patches, here, side, pattern, pert, weights, innov, out):
    mine = out.shape[0]
    for patch in range(mine):
        row = here[0] * mine + patch
        pack(share(pattern, row, side[0], patches, pert, weights, innov), out, patch)


def near_kernel(patches, here, side, pattern, pert, weights, innov, state, paired, sent, out, *slabs):
    span = slabs[0].shape[2]
    length = len(slabs)
    layer, place = here[0] // PAIR, here[0] % PAIR
    for shift, slab in zip(turns(length), slabs):
        target = layer ^ shift
        start = (target * PAIR + place) * span
        slab[place] = state[:, pl.ds(pl.multiple_of(start, span), span)]
        slab[1 - place] = paired[target]
    far_kernel(patches, here, side, pattern, pert, weights, innov, out)


def total(value):
    return jnp.sum(jnp.sum(value, axis=0, keepdims=True), axis=1, keepdims=True)


def root_kernel(own, before, after, root_out, rows_out):
    mine, _, members = own.shape
    half = members // 2
    above = lax.broadcasted_iota(jnp.int32, (half, half), 0)
    across = lax.broadcasted_iota(jnp.int32, (half, half), 1)
    row = lax.broadcasted_iota(jnp.int32, (members, members), 0)
    col = lax.broadcasted_iota(jnp.int32, (members, members), 1)
    diagonal = row == col

    def dot(left, right):
        return jnp.dot(left, right, preferred_element_type=F32)

    each = range(mine)
    rest, factor, scale, forcing = [], [], [], []
    base = members - 1.0
    for patch in each:
        packed = before[patch].astype(F32) + after[patch].astype(F32)
        upper = packed[:half]
        mixed = packed[half:members]
        last = packed[members:]
        corner = last[0:1] + last[1:2]
        force = jnp.concatenate([last[2:3] + last[3:4], last[4:5] + last[5:6]], axis=1)
        flipped = mixed.T
        first = jnp.where(above >= across, mixed, flipped)
        second = jnp.where(above < across, mixed, flipped)
        second = jnp.where(above == across, corner, second)
        far = jnp.concatenate(
            [
                jnp.concatenate([first, upper], axis=1),
                jnp.concatenate([upper.T, second], axis=1),
            ],
            axis=0,
        )
        grams = own[patch, :members, :] + far
        blocks = grams[:half, :half] + grams[half:, half:]
        trace = total(jnp.where(above == across, blocks, 0.0))
        norm = jnp.sqrt(total(grams * grams) + 2.0 * base * trace + base * base * members)
        scale.append(norm)
        forcing.append(force + own[patch, members : members + 1, :])
        factor.append(1.5 - 0.5 * (trace / members + base) / norm)
        level = trace / members
        rest.append((grams - jnp.where(diagonal, level, 0.0)) * (-0.5 / norm))
    small = [rest[p].astype(BF16) for p in each]
    lead, tail = list(factor), list(small)
    squares = [dot(small[p], small[p]) for p in each]
    for step in range(1, ITERS):
        cubes = [dot(squares[p].astype(BF16), small[p]) for p in each]
        for p in each:
            f = factor[p]
            rest[p] = (
                (3.0 * f * f - 3.0 * f) * rest[p] + (3.0 * f - 1.5) * squares[p] + cubes[p]
            )
            factor[p] = 1.5 - 1.5 * f * f + f * f * f
            small[p] = rest[p].astype(BF16)
        for p in each:
            narrow = tail[p]
            if step < ITERS - 1:
                both = dot(jnp.concatenate([small[p], narrow], axis=0), small[p])
                squares[p], cross = both[:members], both[members:]
            else:
                cross = dot(narrow, small[p])
            tail[p] = (factor[p] * narrow.astype(F32) + lead[p] * rest[p] + cross).astype(BF16)
            lead[p] = factor[p] * lead[p]
    for p in each:
        high = tail[p]
        root_out[p] = high
        force = jnp.broadcast_to(forcing[p], (PAD, members))
        gain = (lead[p] * force + dot(force.astype(BF16), high)) / scale[p]
        index = lax.broadcasted_iota(jnp.int32, (PAD, members), 0)
        spread = jnp.sqrt(base) / jnp.sqrt(scale[p])
        rows_out[p] = jnp.where(index == 0, gain, jnp.where(index == 1, lead[p], spread))


def apply_kernel(here, root, rows, *rest):
    slabs, (out, columns) = rest[:-2], rest[-2:]
    mine, members, _ = root.shape
    points = out.shape[1] // mine
    length = len(slabs)
    _, local, _ = slabs[0].shape
    for shift, slab in zip(turns(length), slabs):
        source = (here[0] // PAIR) ^ shift
        for i in range(PAIR):
            place = pl.ds(pl.multiple_of((source * PAIR + i) * local, local), local)
            columns[place, :] = slab[i]
    for p in range(mine):
        cols = slice(p * points, (p + 1) * points)
        member = columns[:, cols].astype(F32)
        mean = jnp.sum(member, axis=0, keepdims=True) / members
        deviation = member - mean
        spread = rows[p, 1:2, :points] * deviation + jnp.dot(
            root[p], deviation.astype(BF16), preferred_element_type=F32
        )
        shift = mean + product(split(rows[p]), split(spread))[0:1]
        out[:, cols] = (shift + rows[p, 2:3, :points] * spread).astype(BF16)


def body(state, hx, obs_value, obs_rinv, obs_count, loc_pattern):
    blocks, members, width = hx.shape
    patches, uses = loc_pattern.shape
    mem_total = lax.axis_size("mem")
    mine = patches // mem_total
    local, points = state.shape
    ring = lax.axis_size("lon")
    near = [(i, i + 1 - 2 * (i % 2)) for i in range(ring)]
    far = [(i, (i - 1 + 2 * (i % 2)) % ring) for i in range(ring)]
    odd = lax.axis_index("lon") % 2
    here, near_side, far_side = (
        value.astype(jnp.int32).reshape(1) for value in (lax.axis_index("mem"), 2 * odd, 2 - 2 * odd)
    )
    shape = jax.ShapeDtypeStruct
    padded = members + PAD

    span = points // mem_total
    length = mem_total // PAIR
    swap = [(i, i ^ 1) for i in range(mem_total)]
    assert mem_total & (mem_total - 1) == 0

    pattern = loc_pattern.T
    far_pattern = lax.ppermute(pattern, "lon", far)
    near_pattern = lax.ppermute(pattern, "lon", near)
    limit = pltpu.CompilerParams(vmem_limit_bytes=16 * 1024 * 1024)
    gram = 2 * padded * members * uses * width
    pert, weights, innov, own, given = pl.pallas_call(
        functools.partial(own_kernel, patches),
        out_shape=(
            shape((blocks, members, width), BF16),
            shape((blocks, width), F32),
            shape((blocks, width), F32),
            shape((mine, padded, members), F32),
            shape((length, local, span), BF16),
        ),
        in_specs=[SMEM] + [HBM] * 6,
        out_specs=(VMEM,) * 5,
        scratch_shapes=[
            pltpu.VMEM((blocks, members, width), BF16),
            pltpu.SMEM(obs_count.shape, jnp.int32),
            pltpu.SMEM(pattern.shape, jnp.int32),
            pltpu.VMEM(obs_value.shape, F32),
            pltpu.VMEM(obs_rinv.shape, F32),
            pltpu.SemaphoreType.DMA((blocks // CHUNK,)),
            pltpu.SemaphoreType.DMA((4,)),
            pltpu.SemaphoreType.DMA((length,)),
        ],
        compiler_params=limit,
        cost_estimate=pl.CostEstimate(
            flops=hx.size * 4 + mine * gram, bytes_accessed=2 * hx.size * 2, transcendentals=0
        ),
        name="own_share",
    )(here, *(stay(value) for value in (obs_count, pattern, hx, obs_value, obs_rinv, state)))
    given, far_pattern, near_pattern = lax.optimization_barrier((given, far_pattern, near_pattern))
    paired = lax.ppermute(given, "mem", swap)
    packed = shape((mine, padded, members // 2), BF16)
    slab = shape((PAIR, local, span), BF16)
    cost = pl.CostEstimate(flops=mine * gram, bytes_accessed=hx.size, transcendentals=0)
    to_far = pl.pallas_call(
        functools.partial(far_kernel, patches),
        out_shape=packed,
        in_specs=[SMEM] * 3 + [VMEM] * 3,
        out_specs=VMEM,
        compiler_params=limit,
        cost_estimate=cost,
        name="far_share",
    )(here, far_side, far_pattern, pert, weights, innov)
    from_far = lax.ppermute(to_far, "lon", far)
    to_near, *slabs = pl.pallas_call(
        functools.partial(near_kernel, patches),
        out_shape=(packed,) + (slab,) * length,
        in_specs=[SMEM] * 3 + [VMEM] * 5 + [pl.BlockSpec(memory_space=pl.ANY)],
        out_specs=(VMEM,) * (1 + length),
        compiler_params=limit,
        cost_estimate=cost,
        name="near_share",
    )(here, near_side, near_pattern, pert, weights, innov, state, paired, to_far)
    from_near = lax.ppermute(to_near, "lon", near)
    for i, shift in enumerate(turns(length)):
        if shift:
            trade = [(j, j ^ (shift * PAIR)) for j in range(mem_total)]
            slabs[i] = lax.ppermute(slabs[i], "mem", trade)
    root, rows = pl.pallas_call(
        root_kernel,
        out_shape=(shape((mine, members, members), BF16), shape((mine, PAD, members), F32)),
        in_specs=[VMEM] * 3,
        out_specs=(VMEM,) * 2,
        compiler_params=limit,
        cost_estimate=pl.CostEstimate(
            flops=mine * 15 * 2 * members**3, bytes_accessed=2**20, transcendentals=0
        ),
        name="root",
    )(own, from_far, from_near)
    updated = pl.pallas_call(
        apply_kernel,
        out_shape=shape((members, span), BF16),
        in_specs=[SMEM] + [VMEM] * (2 + length),
        out_specs=VMEM,
        scratch_shapes=[pltpu.VMEM((members, span), BF16)],
        compiler_params=limit,
        cost_estimate=pl.CostEstimate(
            flops=2 * members**2 * span, bytes_accessed=2**19, transcendentals=0
        ),
        name="apply",
    )(here, root, rows, *slabs)
    pieces = lax.all_to_all(
        updated.reshape(mem_total, local, span), "mem", split_axis=0, concat_axis=0
    )
    return jnp.swapaxes(pieces, 0, 1).reshape(local, points)


def solution(mesh):
    in_specs = (
        P("mem", "lon"),
        P("lon", None, None),
        P("lon", None),
        P("lon", None),
        P("lon"),
        P("lon", None),
    )
    out_specs = P("mem", "lon")
    return jax.shard_map(body, mesh=mesh, in_specs=in_specs, out_specs=out_specs, check_vma=False)
```

```python
import functools

import jax
import jax.numpy as jnp
from jax import lax
from jax.experimental import pallas as pl
from jax.experimental.pallas import tpu as pltpu
from jax.sharding import PartitionSpec as P

ITERS = 6
PAD = 16
CHUNK = 4
PAIR = 2
F32 = jnp.float32
BF16 = jnp.bfloat16

VMEM = pl.BlockSpec(memory_space=pltpu.VMEM)
SMEM = pl.BlockSpec(memory_space=pltpu.SMEM)
HBM = pl.BlockSpec(memory_space=pltpu.HBM)


def turns(length):
    return [0, *range(2, length), 1][:length]


def stay(value):
    return pltpu.with_memory_space_constraint(value, pltpu.HBM)


def split(value):
    high = value.astype(BF16)
    return high, (value - high.astype(F32)).astype(BF16)


def product(left, right):
    lhs = jnp.concatenate([left[0], left[0], left[1]], axis=1)
    rhs = jnp.concatenate([right[0], right[1], right[0]], axis=0)
    return jnp.dot(lhs, rhs, preferred_element_type=F32)


def share(pattern, row, side, patches, pert, weights, innov):
    blocks, _, width = pert.shape
    left, right = [], []
    for slot in range(pattern.shape[0]):
        position = pattern[slot, row]
        block = position - side * blocks
        here = jnp.logical_and(block >= 0, block < blocks)
        block = jnp.clip(block, 0, blocks - 1)
        spot = jnp.full((1, width), position, jnp.int32).astype(F32)
        rank = jnp.full((1, width), row, jnp.int32).astype(F32)
        offset = (spot + 0.5) / blocks - 1.0 - (rank + 0.5) / patches
        taper = jnp.exp(-0.5 * offset * offset) * jnp.where(here, 1.0, 0.0)
        picked = pert[block]
        weight = (taper * weights[pl.ds(block, 1), :]).astype(BF16)
        vector = jnp.broadcast_to(taper * innov[pl.ds(block, 1), :], (PAD, width)).astype(BF16)
        left.append(jnp.concatenate([weight * picked, vector], axis=0))
        right.append(picked)
    return lax.dot_general(
        jnp.concatenate(left, axis=1),
        jnp.concatenate(right, axis=1),
        (((1,), (1,)), ((), ())),
        preferred_element_type=F32,
    )


def perturb_kernel(
    count_all, hx, value_all, rinv_all, pert, weights, innov, raw, count, value, rinv, sems, small
):
    blocks, members, width = raw.shape
    smalls = [
        pltpu.make_async_copy(source, target, small.at[i])
        for i, (source, target) in enumerate(
            ((count_all, count), (value_all, value), (rinv_all, rinv))
        )
    ]
    copies = [
        pltpu.make_async_copy(hx.at[pl.ds(i, CHUNK)], raw.at[pl.ds(i, CHUNK)], sems.at[i // CHUNK])
        for i in range(0, blocks, CHUNK)
    ]
    for copy in smalls + copies:
        copy.start()
    for copy in smalls:
        copy.wait()
    lane = lax.broadcasted_iota(jnp.int32, (1, width), 1)
    for block in range(blocks):
        if block % CHUNK == 0:
            copies[block // CHUNK].wait()
        member = raw[block].astype(F32)
        mean = jnp.sum(member, axis=0, keepdims=True) / members
        pert[block] = (member - mean).astype(BF16)
        weight = jnp.where(lane < count[block], rinv[block : block + 1, :], 0.0)
        gap = weight * (value[block : block + 1, :] - mean)
        weights[block : block + 1, :] = weight.astype(BF16).astype(F32)
        innov[block : block + 1, :] = gap


def own_kernel(patches, here, pattern, pert, weights, innov, sent, own):
    mine = own.shape[0]
    for patch in range(mine):
        row = here[0] * mine + patch
        own[patch] = share(pattern, row, 1, patches, pert, weights, innov)


def pack(part, out, patch):
    _, padded, half = out.shape
    members = padded - PAD
    above = lax.broadcasted_iota(jnp.int32, (half, half), 0)
    across = lax.broadcasted_iota(jnp.int32, (half, half), 1)
    corner = part[half:members, half:]
    out[patch, :half, :] = part[:half, half:].astype(BF16)
    out[patch, half:members, :] = jnp.where(above >= across, part[:half, :half], corner).astype(
        BF16
    )
    diagonal = jnp.sum(jnp.where(above == across, corner, 0.0), axis=0, keepdims=True)
    force = part[members : members + 1]
    index = lax.broadcasted_iota(jnp.int32, (PAD, half), 0)
    tail = jnp.zeros((PAD, half), F32)
    for i, value in enumerate((diagonal, force[:, :half], force[:, half:])):
        high, low = split(value)
        tail = jnp.where(index == 2 * i, high.astype(F32), tail)
        tail = jnp.where(index == 2 * i + 1, low.astype(F32), tail)
    out[patch, members:, :] = tail.astype(BF16)


def neighbour_kernel(
    patches,
    here,
    far_side,
    near_side,
    far_pattern,
    near_pattern,
    pert,
    weights,
    innov,
    state,
    paired,
    to_far,
    to_near,
    *slabs,
):
    span = slabs[0].shape[2]
    length = len(slabs)
    layer, place = here[0] // PAIR, here[0] % PAIR
    for shift, slab in zip(turns(length), slabs):
        target = (layer ^ shift) * PAIR + place
        cols = pl.ds(pl.multiple_of(target * span, span), span)
        slab[place] = state[:, cols]
        slab[1 - place] = paired[:, cols]
    mine = to_far.shape[0]
    for pattern, side, out in (
        (far_pattern, far_side, to_far),
        (near_pattern, near_side, to_near),
    ):
        for patch in range(mine):
            row = here[0] * mine + patch
            pack(share(pattern, row, side[0], patches, pert, weights, innov), out, patch)


def total(value):
    return jnp.sum(jnp.sum(value, axis=0, keepdims=True), axis=1, keepdims=True)


def root_kernel(own, before, after, root_out, rows_out):
    mine, _, members = own.shape
    half = members // 2
    above = lax.broadcasted_iota(jnp.int32, (half, half), 0)
    across = lax.broadcasted_iota(jnp.int32, (half, half), 1)
    row = lax.broadcasted_iota(jnp.int32, (members, members), 0)
    col = lax.broadcasted_iota(jnp.int32, (members, members), 1)
    diagonal = row == col

    def dot(left, right):
        return jnp.dot(left, right, preferred_element_type=F32)

    each = range(mine)
    rest, factor, scale, forcing = [], [], [], []
    base = members - 1.0
    for patch in each:
        packed = before[patch].astype(F32) + after[patch].astype(F32)
        upper = packed[:half]
        mixed = packed[half:members]
        last = packed[members:]
        corner = last[0:1] + last[1:2]
        force = jnp.concatenate([last[2:3] + last[3:4], last[4:5] + last[5:6]], axis=1)
        flipped = mixed.T
        first = jnp.where(above >= across, mixed, flipped)
        second = jnp.where(above < across, mixed, flipped)
        second = jnp.where(above == across, corner, second)
        far = jnp.concatenate(
            [
                jnp.concatenate([first, upper], axis=1),
                jnp.concatenate([upper.T, second], axis=1),
            ],
            axis=0,
        )
        grams = own[patch, :members, :] + far
        blocks = grams[:half, :half] + grams[half:, half:]
        trace = total(jnp.where(above == across, blocks, 0.0))
        norm = jnp.sqrt(total(grams * grams) + 2.0 * base * trace + base * base * members)
        scale.append(norm)
        forcing.append(force + own[patch, members : members + 1, :])
        factor.append(1.5 - 0.5 * (trace / members + base) / norm)
        level = trace / members
        rest.append((grams - jnp.where(diagonal, level, 0.0)) * (-0.5 / norm))
    small = [rest[p].astype(BF16) for p in each]
    lead, tail = list(factor), list(small)
    squares = [dot(small[p], small[p]) for p in each]
    for step in range(1, ITERS):
        cubes = [dot(squares[p].astype(BF16), small[p]) for p in each]
        for p in each:
            f = factor[p]
            rest[p] = (
                (3.0 * f * f - 3.0 * f) * rest[p] + (3.0 * f - 1.5) * squares[p] + cubes[p]
            )
            factor[p] = 1.5 - 1.5 * f * f + f * f * f
            small[p] = rest[p].astype(BF16)
        for p in each:
            narrow = tail[p]
            if step < ITERS - 1:
                both = dot(jnp.concatenate([small[p], narrow], axis=0), small[p])
                squares[p], cross = both[:members], both[members:]
            else:
                cross = dot(narrow, small[p])
            tail[p] = (factor[p] * narrow.astype(F32) + lead[p] * rest[p] + cross).astype(BF16)
            lead[p] = factor[p] * lead[p]
    for p in each:
        high = tail[p]
        root_out[p] = high
        force = jnp.broadcast_to(forcing[p], (PAD, members))
        gain = (lead[p] * force + dot(force.astype(BF16), high)) / scale[p]
        index = lax.broadcasted_iota(jnp.int32, (PAD, members), 0)
        spread = jnp.sqrt(base) / jnp.sqrt(scale[p])
        rows_out[p] = jnp.where(index == 0, gain, jnp.where(index == 1, lead[p], spread))


def apply_kernel(here, root, rows, *rest):
    slabs, (out, columns) = rest[:-2], rest[-2:]
    mine, members, _ = root.shape
    points = out.shape[1] // mine
    length = len(slabs)
    _, local, _ = slabs[0].shape
    for shift, slab in zip(turns(length), slabs):
        source = (here[0] // PAIR) ^ shift
        for i in range(PAIR):
            place = pl.ds(pl.multiple_of((source * PAIR + i) * local, local), local)
            columns[place, :] = slab[i]
    for p in range(mine):
        cols = slice(p * points, (p + 1) * points)
        member = columns[:, cols].astype(F32)
        mean = jnp.sum(member, axis=0, keepdims=True) / members
        deviation = member - mean
        spread = rows[p, 1:2, :points] * deviation + jnp.dot(
            root[p], deviation.astype(BF16), preferred_element_type=F32
        )
        shift = mean + product(split(rows[p]), split(spread))[0:1]
        out[:, cols] = (shift + rows[p, 2:3, :points] * spread).astype(BF16)


def body(state, hx, obs_value, obs_rinv, obs_count, loc_pattern):
    blocks, members, width = hx.shape
    patches, uses = loc_pattern.shape
    mem_total = lax.axis_size("mem")
    mine = patches // mem_total
    local, points = state.shape
    ring = lax.axis_size("lon")
    near = [(i, i + 1 - 2 * (i % 2)) for i in range(ring)]
    far = [(i, (i - 1 + 2 * (i % 2)) % ring) for i in range(ring)]
    odd = lax.axis_index("lon") % 2
    here, near_side, far_side = (
        value.astype(jnp.int32).reshape(1) for value in (lax.axis_index("mem"), 2 * odd, 2 - 2 * odd)
    )
    shape = jax.ShapeDtypeStruct
    padded = members + PAD

    span = points // mem_total
    length = mem_total // PAIR
    swap = [(i, i ^ 1) for i in range(mem_total)]
    assert mem_total & (mem_total - 1) == 0

    pattern = loc_pattern.T
    far_pattern = lax.ppermute(pattern, "lon", far)
    near_pattern = lax.ppermute(pattern, "lon", near)
    paired = lax.ppermute(state, "mem", swap)
    limit = pltpu.CompilerParams(vmem_limit_bytes=16 * 1024 * 1024)
    gram = 2 * padded * members * uses * width
    pert, weights, innov = pl.pallas_call(
        perturb_kernel,
        out_shape=(
            shape((blocks, members, width), BF16),
            shape((blocks, width), F32),
            shape((blocks, width), F32),
        ),
        in_specs=[HBM] * 4,
        out_specs=(VMEM,) * 3,
        scratch_shapes=[
            pltpu.VMEM((blocks, members, width), BF16),
            pltpu.SMEM(obs_count.shape, jnp.int32),
            pltpu.VMEM(obs_value.shape, F32),
            pltpu.VMEM(obs_rinv.shape, F32),
            pltpu.SemaphoreType.DMA((blocks // CHUNK,)),
            pltpu.SemaphoreType.DMA((3,)),
        ],
        compiler_params=limit,
        cost_estimate=pl.CostEstimate(
            flops=hx.size * 4, bytes_accessed=2 * hx.size * 2, transcendentals=0
        ),
        name="perturb",
    )(*(stay(value) for value in (obs_count, hx, obs_value, obs_rinv)))
    packed = shape((mine, padded, members // 2), BF16)
    slab = shape((PAIR, local, span), BF16)
    cost = pl.CostEstimate(flops=mine * gram, bytes_accessed=hx.size, transcendentals=0)
    to_far, to_near, *slabs = pl.pallas_call(
        functools.partial(neighbour_kernel, patches),
        out_shape=(packed,) * 2 + (slab,) * length,
        in_specs=[SMEM] * 5 + [VMEM] * 5,
        out_specs=(VMEM,) * (2 + length),
        compiler_params=limit,
        cost_estimate=cost,
        name="neighbour_shares",
    )(here, far_side, near_side, far_pattern, near_pattern, pert, weights, innov, state, paired)
    from_far = lax.ppermute(to_far, "lon", far)
    from_near = lax.ppermute(to_near, "lon", near)
    own = pl.pallas_call(
        functools.partial(own_kernel, patches),
        out_shape=shape((mine, padded, members), F32),
        in_specs=[SMEM] * 2 + [VMEM] * 3 + [pl.BlockSpec(memory_space=pl.ANY)],
        out_specs=VMEM,
        compiler_params=limit,
        cost_estimate=cost,
        name="own_share",
    )(here, pattern, pert, weights, innov, to_near)
    for i, shift in enumerate(turns(length)):
        if shift:
            trade = [(j, j ^ (shift * PAIR)) for j in range(mem_total)]
            slabs[i] = lax.ppermute(slabs[i], "mem", trade)
    root, rows = pl.pallas_call(
        root_kernel,
        out_shape=(shape((mine, members, members), BF16), shape((mine, PAD, members), F32)),
        in_specs=[VMEM] * 3,
        out_specs=(VMEM,) * 2,
        compiler_params=limit,
        cost_estimate=pl.CostEstimate(
            flops=mine * 15 * 2 * members**3, bytes_accessed=2**20, transcendentals=0
        ),
        name="root",
    )(own, from_far, from_near)
    updated = pl.pallas_call(
        apply_kernel,
        out_shape=shape((members, span), BF16),
        in_specs=[SMEM] + [VMEM] * (2 + length),
        out_specs=VMEM,
        scratch_shapes=[pltpu.VMEM((members, span), BF16)],
        compiler_params=limit,
        cost_estimate=pl.CostEstimate(
            flops=2 * members**2 * span, bytes_accessed=2**19, transcendentals=0
        ),
        name="apply",
    )(here, root, rows, *slabs)
    pieces = lax.all_to_all(
        updated.reshape(mem_total, local, span), "mem", split_axis=0, concat_axis=0
    )
    return jnp.swapaxes(pieces, 0, 1).reshape(local, points)


def solution(mesh):
    in_specs = (
        P("mem", "lon"),
        P("lon", None, None),
        P("lon", None),
        P("lon", None),
        P("lon"),
        P("lon", None),
    )
    out_specs = P("mem", "lon")
    return jax.shard_map(body, mesh=mesh, in_specs=in_specs, out_specs=out_specs, check_vma=False)
```

```python
import functools

import jax
import jax.numpy as jnp
from jax import lax
from jax.experimental import pallas as pl
from jax.experimental.pallas import tpu as pltpu
from jax.sharding import PartitionSpec as P

ITERS = 6
PAD = 16
CHUNK = 4
PAIR = 2
F32 = jnp.float32
BF16 = jnp.bfloat16

VMEM = pl.BlockSpec(memory_space=pltpu.VMEM)
SMEM = pl.BlockSpec(memory_space=pltpu.SMEM)
HBM = pl.BlockSpec(memory_space=pltpu.HBM)


def turns(length):
    return [0, *range(2, length), 1][:length]


def stay(value):
    return pltpu.with_memory_space_constraint(value, pltpu.HBM)


def split(value):
    high = value.astype(BF16)
    return high, (value - high.astype(F32)).astype(BF16)


def product(left, right):
    lhs = jnp.concatenate([left[0], left[0], left[1]], axis=1)
    rhs = jnp.concatenate([right[0], right[1], right[0]], axis=0)
    return jnp.dot(lhs, rhs, preferred_element_type=F32)


def share(pattern, row, side, patches, pert, weights, innov):
    blocks, _, width = pert.shape
    left, right = [], []
    for slot in range(pattern.shape[0]):
        position = pattern[slot, row]
        block = position - side * blocks
        here = jnp.logical_and(block >= 0, block < blocks)
        block = jnp.clip(block, 0, blocks - 1)
        spot = jnp.full((1, width), position, jnp.int32).astype(F32)
        rank = jnp.full((1, width), row, jnp.int32).astype(F32)
        offset = (spot + 0.5) / blocks - 1.0 - (rank + 0.5) / patches
        taper = jnp.exp(-0.5 * offset * offset) * jnp.where(here, 1.0, 0.0)
        picked = pert[block]
        weight = (taper * weights[pl.ds(block, 1), :]).astype(BF16)
        vector = jnp.broadcast_to(taper * innov[pl.ds(block, 1), :], (PAD, width)).astype(BF16)
        left.append(jnp.concatenate([weight * picked, vector], axis=0))
        right.append(picked)
    return lax.dot_general(
        jnp.concatenate(left, axis=1),
        jnp.concatenate(right, axis=1),
        (((1,), (1,)), ((), ())),
        preferred_element_type=F32,
    )


def own_kernel(
    patches,
    count_all,
    pattern_all,
    hx,
    value_all,
    rinv_all,
    pert,
    weights,
    innov,
    own,
    raw,
    count,
    pattern,
    value,
    rinv,
    sems,
    small,
):
    blocks, members, width = raw.shape
    smalls = [
        pltpu.make_async_copy(source, target, small.at[i])
        for i, (source, target) in enumerate(
            ((count_all, count), (value_all, value), (rinv_all, rinv), (pattern_all, pattern))
        )
    ]
    copies = [
        pltpu.make_async_copy(hx.at[pl.ds(i, CHUNK)], raw.at[pl.ds(i, CHUNK)], sems.at[i // CHUNK])
        for i in range(0, blocks, CHUNK)
    ]
    for copy in smalls + copies:
        copy.start()
    for copy in smalls:
        copy.wait()
    lane = lax.broadcasted_iota(jnp.int32, (1, width), 1)
    for block in range(blocks):
        if block % CHUNK == 0:
            copies[block // CHUNK].wait()
        member = raw[block].astype(F32)
        mean = jnp.sum(member, axis=0, keepdims=True) / members
        pert[block] = (member - mean).astype(BF16)
        weight = jnp.where(lane < count[block], rinv[block : block + 1, :], 0.0)
        gap = weight * (value[block : block + 1, :] - mean)
        weights[block : block + 1, :] = weight.astype(BF16).astype(F32)
        innov[block : block + 1, :] = gap
    mine = own.shape[0]
    for patch in range(mine):
        row = lax.axis_index("mem") * mine + patch
        own[patch] = share(pattern, row, 1, patches, pert, weights, innov)


def pack(part, out, patch):
    _, padded, half = out.shape
    members = padded - PAD
    above = lax.broadcasted_iota(jnp.int32, (half, half), 0)
    across = lax.broadcasted_iota(jnp.int32, (half, half), 1)
    corner = part[half:members, half:]
    out[patch, :half, :] = part[:half, half:].astype(BF16)
    out[patch, half:members, :] = jnp.where(above >= across, part[:half, :half], corner).astype(
        BF16
    )
    diagonal = jnp.sum(jnp.where(above == across, corner, 0.0), axis=0, keepdims=True)
    force = part[members : members + 1]
    index = lax.broadcasted_iota(jnp.int32, (PAD, half), 0)
    tail = jnp.zeros((PAD, half), F32)
    for i, value in enumerate((diagonal, force[:, :half], force[:, half:])):
        high, low = split(value)
        tail = jnp.where(index == 2 * i, high.astype(F32), tail)
        tail = jnp.where(index == 2 * i + 1, low.astype(F32), tail)
    out[patch, members:, :] = tail.astype(BF16)


def neighbour(patches, side, pattern, pert, weights, innov, out):
    mine = out.shape[0]
    for patch in range(mine):
        row = lax.axis_index("mem") * mine + patch
        pack(share(pattern, row, side, patches, pert, weights, innov), out, patch)


def far_kernel(patches, pattern, pert, weights, innov, out):
    side = 2 - 2 * (lax.axis_index("lon") % 2)
    neighbour(patches, side, pattern, pert, weights, innov, out)


def near_kernel(patches, pattern, pert, weights, innov, state, paired, sent, out, *slabs):
    span = slabs[0].shape[2]
    length = len(slabs)
    layer, place = lax.axis_index("mem") // PAIR, lax.axis_index("mem") % PAIR
    for shift, slab in zip(turns(length), slabs):
        target = (layer ^ shift) * PAIR + place
        cols = pl.ds(pl.multiple_of(target * span, span), span)
        slab[place] = state[:, cols]
        slab[1 - place] = paired[:, cols]
    neighbour(patches, 2 * (lax.axis_index("lon") % 2), pattern, pert, weights, innov, out)


def total(value):
    return jnp.sum(jnp.sum(value, axis=0, keepdims=True), axis=1, keepdims=True)


def root_kernel(own, before, after, root_out, rows_out):
    mine, _, members = own.shape
    half = members // 2
    above = lax.broadcasted_iota(jnp.int32, (half, half), 0)
    across = lax.broadcasted_iota(jnp.int32, (half, half), 1)
    row = lax.broadcasted_iota(jnp.int32, (members, members), 0)
    col = lax.broadcasted_iota(jnp.int32, (members, members), 1)
    diagonal = row == col

    def dot(left, right):
        return jnp.dot(left, right, preferred_element_type=F32)

    each = range(mine)
    rest, factor, scale, forcing = [], [], [], []
    base = members - 1.0
    for patch in each:
        packed = before[patch].astype(F32) + after[patch].astype(F32)
        upper = packed[:half]
        mixed = packed[half:members]
        last = packed[members:]
        corner = last[0:1] + last[1:2]
        force = jnp.concatenate([last[2:3] + last[3:4], last[4:5] + last[5:6]], axis=1)
        flipped = mixed.T
        first = jnp.where(above >= across, mixed, flipped)
        second = jnp.where(above < across, mixed, flipped)
        second = jnp.where(above == across, corner, second)
        far = jnp.concatenate(
            [
                jnp.concatenate([first, upper], axis=1),
                jnp.concatenate([upper.T, second], axis=1),
            ],
            axis=0,
        )
        grams = own[patch, :members, :] + far
        blocks = grams[:half, :half] + grams[half:, half:]
        trace = total(jnp.where(above == across, blocks, 0.0))
        norm = jnp.sqrt(total(grams * grams) + 2.0 * base * trace + base * base * members)
        scale.append(norm)
        forcing.append(force + own[patch, members : members + 1, :])
        factor.append(1.5 - 0.5 * (trace / members + base) / norm)
        level = trace / members
        rest.append((grams - jnp.where(diagonal, level, 0.0)) * (-0.5 / norm))
    small = [rest[p].astype(BF16) for p in each]
    lead, tail = list(factor), list(small)
    squares = [dot(small[p], small[p]) for p in each]
    for step in range(1, ITERS):
        cubes = [dot(squares[p].astype(BF16), small[p]) for p in each]
        for p in each:
            f = factor[p]
            rest[p] = (
                (3.0 * f * f - 3.0 * f) * rest[p] + (3.0 * f - 1.5) * squares[p] + cubes[p]
            )
            factor[p] = 1.5 - 1.5 * f * f + f * f * f
            small[p] = rest[p].astype(BF16)
        for p in each:
            narrow = tail[p]
            if step < ITERS - 1:
                both = dot(jnp.concatenate([small[p], narrow], axis=0), small[p])
                squares[p], cross = both[:members], both[members:]
            else:
                cross = dot(narrow, small[p])
            tail[p] = (factor[p] * narrow.astype(F32) + lead[p] * rest[p] + cross).astype(BF16)
            lead[p] = factor[p] * lead[p]
    for p in each:
        high = tail[p]
        root_out[p] = high
        force = jnp.broadcast_to(forcing[p], (PAD, members))
        gain = (lead[p] * force + dot(force.astype(BF16), high)) / scale[p]
        index = lax.broadcasted_iota(jnp.int32, (PAD, members), 0)
        spread = jnp.sqrt(base) / jnp.sqrt(scale[p])
        rows_out[p] = jnp.where(index == 0, gain, jnp.where(index == 1, lead[p], spread))


def apply_kernel(root, rows, *rest):
    slabs, (out, columns) = rest[:-2], rest[-2:]
    mine, members, _ = root.shape
    points = out.shape[1] // mine
    length = len(slabs)
    _, local, _ = slabs[0].shape
    for shift, slab in zip(turns(length), slabs):
        source = (lax.axis_index("mem") // PAIR) ^ shift
        for i in range(PAIR):
            place = pl.ds(pl.multiple_of((source * PAIR + i) * local, local), local)
            columns[place, :] = slab[i]
    for p in range(mine):
        cols = slice(p * points, (p + 1) * points)
        member = columns[:, cols].astype(F32)
        mean = jnp.sum(member, axis=0, keepdims=True) / members
        deviation = member - mean
        spread = rows[p, 1:2, :points] * deviation + jnp.dot(
            root[p], deviation.astype(BF16), preferred_element_type=F32
        )
        shift = mean + product(split(rows[p]), split(spread))[0:1]
        out[:, cols] = (shift + rows[p, 2:3, :points] * spread).astype(BF16)


def body(state, hx, obs_value, obs_rinv, obs_count, loc_pattern):
    blocks, members, width = hx.shape
    patches, uses = loc_pattern.shape
    mem_total = lax.axis_size("mem")
    mine = patches // mem_total
    local, points = state.shape
    ring = lax.axis_size("lon")
    near = [(i, i + 1 - 2 * (i % 2)) for i in range(ring)]
    far = [(i, (i - 1 + 2 * (i % 2)) % ring) for i in range(ring)]
    shape = jax.ShapeDtypeStruct
    padded = members + PAD

    span = points // mem_total
    length = mem_total // PAIR
    swap = [(i, i ^ 1) for i in range(mem_total)]
    assert mem_total & (mem_total - 1) == 0

    pattern = loc_pattern.T
    far_pattern = lax.ppermute(pattern, "lon", far)
    near_pattern = lax.ppermute(pattern, "lon", near)
    paired = lax.ppermute(state, "mem", swap)
    limit = pltpu.CompilerParams(vmem_limit_bytes=16 * 1024 * 1024)
    gram = 2 * padded * members * uses * width
    pert, weights, innov, own = pl.pallas_call(
        functools.partial(own_kernel, patches),
        out_shape=(
            shape((blocks, members, width), BF16),
            shape((blocks, width), F32),
            shape((blocks, width), F32),
            shape((mine, padded, members), F32),
        ),
        in_specs=[HBM] * 5,
        out_specs=(VMEM,) * 4,
        scratch_shapes=[
            pltpu.VMEM((blocks, members, width), BF16),
            pltpu.SMEM(obs_count.shape, jnp.int32),
            pltpu.SMEM(pattern.shape, jnp.int32),
            pltpu.VMEM(obs_value.shape, F32),
            pltpu.VMEM(obs_rinv.shape, F32),
            pltpu.SemaphoreType.DMA((blocks // CHUNK,)),
            pltpu.SemaphoreType.DMA((4,)),
        ],
        compiler_params=limit,
        cost_estimate=pl.CostEstimate(
            flops=hx.size * 4 + mine * gram, bytes_accessed=2 * hx.size * 2, transcendentals=0
        ),
        name="own_share",
    )(*(stay(value) for value in (obs_count, pattern, hx, obs_value, obs_rinv)))
    packed = shape((mine, padded, members // 2), BF16)
    slab = shape((PAIR, local, span), BF16)
    cost = pl.CostEstimate(flops=mine * gram, bytes_accessed=hx.size, transcendentals=0)
    to_far = pl.pallas_call(
        functools.partial(far_kernel, patches),
        out_shape=packed,
        in_specs=[SMEM] + [VMEM] * 3,
        out_specs=VMEM,
        compiler_params=limit,
        cost_estimate=cost,
        name="far_share",
    )(far_pattern, pert, weights, innov)
    from_far = lax.ppermute(to_far, "lon", far)
    to_near, *slabs = pl.pallas_call(
        functools.partial(near_kernel, patches),
        out_shape=(packed,) + (slab,) * length,
        in_specs=[SMEM] + [VMEM] * 5 + [pl.BlockSpec(memory_space=pl.ANY)],
        out_specs=(VMEM,) * (1 + length),
        compiler_params=limit,
        cost_estimate=cost,
        name="near_share",
    )(near_pattern, pert, weights, innov, state, paired, to_far)
    from_near = lax.ppermute(to_near, "lon", near)
    for i, shift in enumerate(turns(length)):
        if shift:
            trade = [(j, j ^ (shift * PAIR)) for j in range(mem_total)]
            slabs[i] = lax.ppermute(slabs[i], "mem", trade)
    root, rows = pl.pallas_call(
        root_kernel,
        out_shape=(shape((mine, members, members), BF16), shape((mine, PAD, members), F32)),
        in_specs=[VMEM] * 3,
        out_specs=(VMEM,) * 2,
        compiler_params=limit,
        cost_estimate=pl.CostEstimate(
            flops=mine * 15 * 2 * members**3, bytes_accessed=2**20, transcendentals=0
        ),
        name="root",
    )(own, from_far, from_near)
    updated = pl.pallas_call(
        apply_kernel,
        out_shape=shape((members, span), BF16),
        in_specs=[VMEM] * (2 + length),
        out_specs=VMEM,
        scratch_shapes=[pltpu.VMEM((members, span), BF16)],
        compiler_params=limit,
        cost_estimate=pl.CostEstimate(
            flops=2 * members**2 * span, bytes_accessed=2**19, transcendentals=0
        ),
        name="apply",
    )(root, rows, *slabs)
    pieces = lax.all_to_all(
        updated.reshape(mem_total, local, span), "mem", split_axis=0, concat_axis=0
    )
    return jnp.swapaxes(pieces, 0, 1).reshape(local, points)


def solution(mesh):
    in_specs = (
        P("mem", "lon"),
        P("lon", None, None),
        P("lon", None),
        P("lon", None),
        P("lon"),
        P("lon", None),
    )
    out_specs = P("mem", "lon")
    return jax.shard_map(body, mesh=mesh, in_specs=in_specs, out_specs=out_specs, check_vma=False)
```

```python
import functools

import jax
import jax.numpy as jnp
from jax import lax
from jax.experimental import pallas as pl
from jax.experimental.pallas import tpu as pltpu
from jax.sharding import PartitionSpec as P

ITERS = 6
PAD = 16
CHUNK = 4
PAIR = 2
F32 = jnp.float32
BF16 = jnp.bfloat16

VMEM = pl.BlockSpec(memory_space=pltpu.VMEM)
SMEM = pl.BlockSpec(memory_space=pltpu.SMEM)
HBM = pl.BlockSpec(memory_space=pltpu.HBM)


def turns(length):
    return [0, *range(2, length), 1][:length]


def stay(value):
    return pltpu.with_memory_space_constraint(value, pltpu.HBM)


def split(value):
    high = value.astype(BF16)
    return high, (value - high.astype(F32)).astype(BF16)


def product(left, right):
    lhs = jnp.concatenate([left[0], left[0], left[1]], axis=1)
    rhs = jnp.concatenate([right[0], right[1], right[0]], axis=0)
    return jnp.dot(lhs, rhs, preferred_element_type=F32)


def share(pattern, row, side, patches, pert, weights, innov):
    blocks, _, width = pert.shape
    left, right = [], []
    for slot in range(pattern.shape[0]):
        position = pattern[slot, row]
        block = position - side * blocks
        here = jnp.logical_and(block >= 0, block < blocks)
        block = jnp.clip(block, 0, blocks - 1)
        spot = jnp.full((1, width), position, jnp.int32).astype(F32)
        rank = jnp.full((1, width), row, jnp.int32).astype(F32)
        offset = (spot + 0.5) / blocks - 1.0 - (rank + 0.5) / patches
        taper = jnp.exp(-0.5 * offset * offset) * jnp.where(here, 1.0, 0.0)
        picked = pert[block]
        weight = (taper * weights[pl.ds(block, 1), :]).astype(BF16)
        vector = jnp.broadcast_to(taper * innov[pl.ds(block, 1), :], (PAD, width)).astype(BF16)
        left.append(jnp.concatenate([weight * picked, vector], axis=0))
        right.append(picked)
    return lax.dot_general(
        jnp.concatenate(left, axis=1),
        jnp.concatenate(right, axis=1),
        (((1,), (1,)), ((), ())),
        preferred_element_type=F32,
    )


def own_kernel(
    patches,
    count_all,
    pattern_all,
    hx,
    value_all,
    rinv_all,
    pert,
    weights,
    innov,
    own,
    raw,
    count,
    pattern,
    value,
    rinv,
    sems,
    small,
):
    blocks, members, width = raw.shape
    smalls = [
        pltpu.make_async_copy(source, target, small.at[i])
        for i, (source, target) in enumerate(
            ((count_all, count), (value_all, value), (rinv_all, rinv), (pattern_all, pattern))
        )
    ]
    copies = [
        pltpu.make_async_copy(hx.at[pl.ds(i, CHUNK)], raw.at[pl.ds(i, CHUNK)], sems.at[i // CHUNK])
        for i in range(0, blocks, CHUNK)
    ]
    for copy in smalls + copies:
        copy.start()
    for copy in smalls:
        copy.wait()
    lane = lax.broadcasted_iota(jnp.int32, (1, width), 1)
    ones = jnp.ones((PAD, members), BF16)
    for block in range(blocks):
        if block % CHUNK == 0:
            copies[block // CHUNK].wait()
        member = raw[block].astype(F32)
        sums = jnp.dot(ones, raw[block], preferred_element_type=F32)
        mean = sums[0:1] / members
        pert[block] = (member - mean).astype(BF16)
        weight = jnp.where(lane < count[block], rinv[block : block + 1, :], 0.0)
        gap = weight * (value[block : block + 1, :] - mean)
        weights[block : block + 1, :] = weight.astype(BF16).astype(F32)
        innov[block : block + 1, :] = gap
    mine = own.shape[0]
    for patch in range(mine):
        row = lax.axis_index("mem") * mine + patch
        own[patch] = share(pattern, row, 1, patches, pert, weights, innov)


def pack(part, out, patch):
    _, padded, half = out.shape
    members = padded - PAD
    above = lax.broadcasted_iota(jnp.int32, (half, half), 0)
    across = lax.broadcasted_iota(jnp.int32, (half, half), 1)
    corner = part[half:members, half:]
    out[patch, :half, :] = part[:half, half:].astype(BF16)
    out[patch, half:members, :] = jnp.where(above >= across, part[:half, :half], corner).astype(
        BF16
    )
    diagonal = jnp.sum(jnp.where(above == across, corner, 0.0), axis=0, keepdims=True)
    force = part[members : members + 1]
    index = lax.broadcasted_iota(jnp.int32, (PAD, half), 0)
    tail = jnp.zeros((PAD, half), F32)
    for i, value in enumerate((diagonal, force[:, :half], force[:, half:])):
        high, low = split(value)
        tail = jnp.where(index == 2 * i, high.astype(F32), tail)
        tail = jnp.where(index == 2 * i + 1, low.astype(F32), tail)
    out[patch, members:, :] = tail.astype(BF16)


def neighbour(patches, side, pattern, pert, weights, innov, out):
    mine = out.shape[0]
    for patch in range(mine):
        row = lax.axis_index("mem") * mine + patch
        pack(share(pattern, row, side, patches, pert, weights, innov), out, patch)


def far_kernel(patches, pattern, pert, weights, innov, out):
    side = 2 - 2 * (lax.axis_index("lon") % 2)
    neighbour(patches, side, pattern, pert, weights, innov, out)


def near_kernel(patches, pattern, pert, weights, innov, state, paired, sent, out, *slabs):
    span = slabs[0].shape[2]
    length = len(slabs)
    layer, place = lax.axis_index("mem") // PAIR, lax.axis_index("mem") % PAIR
    for shift, slab in zip(turns(length), slabs):
        target = (layer ^ shift) * PAIR + place
        cols = pl.ds(pl.multiple_of(target * span, span), span)
        slab[place] = state[:, cols]
        slab[1 - place] = paired[:, cols]
    neighbour(patches, 2 * (lax.axis_index("lon") % 2), pattern, pert, weights, innov, out)


def total(value):
    return jnp.sum(jnp.sum(value, axis=0, keepdims=True), axis=1, keepdims=True)


def root_kernel(own, before, after, root_out, rows_out):
    mine, _, members = own.shape
    half = members // 2
    above = lax.broadcasted_iota(jnp.int32, (half, half), 0)
    across = lax.broadcasted_iota(jnp.int32, (half, half), 1)
    row = lax.broadcasted_iota(jnp.int32, (members, members), 0)
    col = lax.broadcasted_iota(jnp.int32, (members, members), 1)
    diagonal = row == col

    def dot(left, right):
        return jnp.dot(left, right, preferred_element_type=F32)

    def advance(tail, lead, factor, rest, cross):
        return (factor * tail.astype(F32) + lead * rest + cross).astype(BF16), factor * lead

    each = range(mine)
    rest, factor, scale, forcing = [], [], [], []
    base = members - 1.0
    for patch in each:
        packed = before[patch].astype(F32) + after[patch].astype(F32)
        upper = packed[:half]
        mixed = packed[half:members]
        last = packed[members:]
        corner = last[0:1] + last[1:2]
        force = jnp.concatenate([last[2:3] + last[3:4], last[4:5] + last[5:6]], axis=1)
        flipped = mixed.T
        first = jnp.where(above >= across, mixed, flipped)
        second = jnp.where(above < across, mixed, flipped)
        second = jnp.where(above == across, corner, second)
        far = jnp.concatenate(
            [
                jnp.concatenate([first, upper], axis=1),
                jnp.concatenate([upper.T, second], axis=1),
            ],
            axis=0,
        )
        grams = own[patch, :members, :] + far
        blocks = grams[:half, :half] + grams[half:, half:]
        trace = total(jnp.where(above == across, blocks, 0.0))
        norm = jnp.sqrt(total(grams * grams) + 2.0 * base * trace + base * base * members)
        scale.append(norm)
        forcing.append(force + own[patch, members : members + 1, :])
        factor.append(1.5 - 0.5 * (trace / members + base) / norm)
        level = trace / members
        rest.append((grams - jnp.where(diagonal, level, 0.0)) * (-0.5 / norm))
    small = [rest[p].astype(BF16) for p in each]
    lead, tail = [None] * mine, [None] * mine
    squares = [dot(small[p], small[p]) for p in each]
    for step in range(ITERS - 1):
        cubes, crosses, old = [None] * mine, [None] * mine, []
        for p in each:
            square = squares[p].astype(BF16)
            if step == 0:
                cubes[p] = dot(square, small[p])
            else:
                both = dot(jnp.concatenate([square, tail[p]], axis=0), small[p])
                cubes[p], crosses[p] = both[:members], both[members:]
        for p in each:
            f = factor[p]
            old.append((f, rest[p]))
            rest[p] = (
                (3.0 * f * f - 3.0 * f) * rest[p] + (3.0 * f - 1.5) * squares[p] + cubes[p]
            )
            factor[p] = 1.5 - 1.5 * f * f + f * f * f
            past, small[p] = small[p], rest[p].astype(BF16)
            if step == 0:
                lead[p], tail[p] = f, past
        if step < ITERS - 2:
            squares = [dot(small[p], small[p]) for p in each]
        if step > 0:
            for p in each:
                tail[p], lead[p] = advance(tail[p], lead[p], *old[p], crosses[p])
    for p in each:
        cross = dot(tail[p], small[p])
        tail[p], lead[p] = advance(tail[p], lead[p], factor[p], rest[p], cross)
    for p in each:
        high = tail[p]
        root_out[p] = high
        force = jnp.broadcast_to(forcing[p], (PAD, members))
        gain = (lead[p] * force + dot(force.astype(BF16), high)) / scale[p]
        index = lax.broadcasted_iota(jnp.int32, (PAD, members), 0)
        spread = jnp.sqrt(base) / jnp.sqrt(scale[p])
        rows_out[p] = jnp.where(index == 0, gain, jnp.where(index == 1, lead[p], spread))


def apply_kernel(root, rows, *rest):
    slabs, (out, columns) = rest[:-2], rest[-2:]
    mine, members, _ = root.shape
    points = out.shape[1] // mine
    length = len(slabs)
    _, local, _ = slabs[0].shape
    for shift, slab in zip(turns(length), slabs):
        source = (lax.axis_index("mem") // PAIR) ^ shift
        for i in range(PAIR):
            place = pl.ds(pl.multiple_of((source * PAIR + i) * local, local), local)
            columns[place, :] = slab[i]
    for p in range(mine):
        cols = slice(p * points, (p + 1) * points)
        member = columns[:, cols].astype(F32)
        mean = jnp.sum(member, axis=0, keepdims=True) / members
        deviation = member - mean
        spread = rows[p, 1:2, :points] * deviation + jnp.dot(
            root[p], deviation.astype(BF16), preferred_element_type=F32
        )
        shift = mean + product(split(rows[p]), split(spread))[0:1]
        out[:, cols] = (shift + rows[p, 2:3, :points] * spread).astype(BF16)


def body(state, hx, obs_value, obs_rinv, obs_count, loc_pattern):
    blocks, members, width = hx.shape
    patches, uses = loc_pattern.shape
    mem_total = lax.axis_size("mem")
    mine = patches // mem_total
    local, points = state.shape
    ring = lax.axis_size("lon")
    near = [(i, i + 1 - 2 * (i % 2)) for i in range(ring)]
    far = [(i, (i - 1 + 2 * (i % 2)) % ring) for i in range(ring)]
    shape = jax.ShapeDtypeStruct
    padded = members + PAD

    span = points // mem_total
    length = mem_total // PAIR
    swap = [(i, i ^ 1) for i in range(mem_total)]
    assert mem_total & (mem_total - 1) == 0

    pattern = loc_pattern.T
    far_pattern = lax.ppermute(pattern, "lon", far)
    near_pattern = lax.ppermute(pattern, "lon", near)
    paired = lax.ppermute(state, "mem", swap)
    limit = pltpu.CompilerParams(vmem_limit_bytes=16 * 1024 * 1024)
    gram = 2 * padded * members * uses * width
    pert, weights, innov, own = pl.pallas_call(
        functools.partial(own_kernel, patches),
        out_shape=(
            shape((blocks, members, width), BF16),
            shape((blocks, width), F32),
            shape((blocks, width), F32),
            shape((mine, padded, members), F32),
        ),
        in_specs=[HBM] * 5,
        out_specs=(VMEM,) * 4,
        scratch_shapes=[
            pltpu.VMEM((blocks, members, width), BF16),
            pltpu.SMEM(obs_count.shape, jnp.int32),
            pltpu.SMEM(pattern.shape, jnp.int32),
            pltpu.VMEM(obs_value.shape, F32),
            pltpu.VMEM(obs_rinv.shape, F32),
            pltpu.SemaphoreType.DMA((blocks // CHUNK,)),
            pltpu.SemaphoreType.DMA((4,)),
        ],
        compiler_params=limit,
        cost_estimate=pl.CostEstimate(
            flops=hx.size * 4 + mine * gram, bytes_accessed=2 * hx.size * 2, transcendentals=0
        ),
        name="own_share",
    )(*(stay(value) for value in (obs_count, pattern, hx, obs_value, obs_rinv)))
    packed = shape((mine, padded, members // 2), BF16)
    slab = shape((PAIR, local, span), BF16)
    cost = pl.CostEstimate(flops=mine * gram, bytes_accessed=hx.size, transcendentals=0)
    to_far = pl.pallas_call(
        functools.partial(far_kernel, patches),
        out_shape=packed,
        in_specs=[SMEM] + [VMEM] * 3,
        out_specs=VMEM,
        compiler_params=limit,
        cost_estimate=cost,
        name="far_share",
    )(far_pattern, pert, weights, innov)
    from_far = lax.ppermute(to_far, "lon", far)
    to_near, *slabs = pl.pallas_call(
        functools.partial(near_kernel, patches),
        out_shape=(packed,) + (slab,) * length,
        in_specs=[SMEM] + [VMEM] * 5 + [pl.BlockSpec(memory_space=pl.ANY)],
        out_specs=(VMEM,) * (1 + length),
        compiler_params=limit,
        cost_estimate=cost,
        name="near_share",
    )(near_pattern, pert, weights, innov, state, paired, to_far)
    from_near = lax.ppermute(to_near, "lon", near)
    for i, shift in enumerate(turns(length)):
        if shift:
            trade = [(j, j ^ (shift * PAIR)) for j in range(mem_total)]
            slabs[i] = lax.ppermute(slabs[i], "mem", trade)
    root, rows = pl.pallas_call(
        root_kernel,
        out_shape=(shape((mine, members, members), BF16), shape((mine, PAD, members), F32)),
        in_specs=[VMEM] * 3,
        out_specs=(VMEM,) * 2,
        compiler_params=limit,
        cost_estimate=pl.CostEstimate(
            flops=mine * 15 * 2 * members**3, bytes_accessed=2**20, transcendentals=0
        ),
        name="root",
    )(own, from_far, from_near)
    updated = pl.pallas_call(
        apply_kernel,
        out_shape=shape((members, span), BF16),
        in_specs=[VMEM] * (2 + length),
        out_specs=VMEM,
        scratch_shapes=[pltpu.VMEM((members, span), BF16)],
        compiler_params=limit,
        cost_estimate=pl.CostEstimate(
            flops=2 * members**2 * span, bytes_accessed=2**19, transcendentals=0
        ),
        name="apply",
    )(root, rows, *slabs)
    pieces = lax.all_to_all(
        updated.reshape(mem_total, local, span), "mem", split_axis=0, concat_axis=0
    )
    return jnp.swapaxes(pieces, 0, 1).reshape(local, points)


def solution(mesh):
    in_specs = (
        P("mem", "lon"),
        P("lon", None, None),
        P("lon", None),
        P("lon", None),
        P("lon"),
        P("lon", None),
    )
    out_specs = P("mem", "lon")
    return jax.shard_map(body, mesh=mesh, in_specs=in_specs, out_specs=out_specs, check_vma=False)
```

```python
import functools

import jax
import jax.numpy as jnp
from jax import lax
from jax.experimental import pallas as pl
from jax.experimental.pallas import tpu as pltpu
from jax.sharding import PartitionSpec as P

ITERS = 6
PAD = 16
CHUNK = 8
PAIR = 2
F32 = jnp.float32
BF16 = jnp.bfloat16

VMEM = pl.BlockSpec(memory_space=pltpu.VMEM)
SMEM = pl.BlockSpec(memory_space=pltpu.SMEM)
HBM = pl.BlockSpec(memory_space=pltpu.HBM)


def turns(length):
    return [0, *range(2, length), 1][:length]


def stay(value):
    return pltpu.with_memory_space_constraint(value, pltpu.HBM)


def split(value):
    high = value.astype(BF16)
    return high, (value - high.astype(F32)).astype(BF16)


def product(left, right):
    lhs = jnp.concatenate([left[0], left[0], left[1]], axis=1)
    rhs = jnp.concatenate([right[0], right[1], right[0]], axis=0)
    return jnp.dot(lhs, rhs, preferred_element_type=F32)


def share(pattern, row, side, patches, pert, weights, innov):
    blocks, _, width = pert.shape
    left, right = [], []
    for slot in range(pattern.shape[0]):
        position = pattern[slot, row]
        block = position - side * blocks
        here = jnp.logical_and(block >= 0, block < blocks)
        block = jnp.clip(block, 0, blocks - 1)
        spot = jnp.full((1, width), position, jnp.int32).astype(F32)
        rank = jnp.full((1, width), row, jnp.int32).astype(F32)
        offset = (spot + 0.5) / blocks - 1.0 - (rank + 0.5) / patches
        taper = jnp.exp(-0.5 * offset * offset) * jnp.where(here, 1.0, 0.0)
        picked = pert[block]
        weight = (taper * weights[pl.ds(block, 1), :]).astype(BF16)
        vector = jnp.broadcast_to(taper * innov[pl.ds(block, 1), :], (PAD, width)).astype(BF16)
        left.append(jnp.concatenate([weight * picked, vector], axis=0))
        right.append(picked)
    return lax.dot_general(
        jnp.concatenate(left, axis=1),
        jnp.concatenate(right, axis=1),
        (((1,), (1,)), ((), ())),
        preferred_element_type=F32,
    )


def own_kernel(
    patches,
    count_all,
    pattern_all,
    hx,
    value_all,
    rinv_all,
    pert,
    weights,
    innov,
    own,
    raw,
    count,
    pattern,
    value,
    rinv,
    sems,
    small,
):
    blocks, members, width = raw.shape
    smalls = [
        pltpu.make_async_copy(source, target, small.at[i])
        for i, (source, target) in enumerate(
            ((count_all, count), (value_all, value), (rinv_all, rinv), (pattern_all, pattern))
        )
    ]
    copies = [
        pltpu.make_async_copy(hx.at[pl.ds(i, CHUNK)], raw.at[pl.ds(i, CHUNK)], sems.at[i // CHUNK])
        for i in range(0, blocks, CHUNK)
    ]
    for copy in smalls + copies:
        copy.start()
    for copy in smalls:
        copy.wait()
    lane = lax.broadcasted_iota(jnp.int32, (1, width), 1)
    for block in range(blocks):
        if block % CHUNK == 0:
            copies[block // CHUNK].wait()
        member = raw[block].astype(F32)
        mean = jnp.sum(member, axis=0, keepdims=True) * (1.0 / members)
        pert[block] = (member - mean).astype(BF16)
        weight = jnp.where(lane < count[block], rinv[block : block + 1, :], 0.0)
        gap = weight * (value[block : block + 1, :] - mean)
        weights[block : block + 1, :] = weight.astype(BF16).astype(F32)
        innov[block : block + 1, :] = gap
    mine = own.shape[0]
    for patch in range(mine):
        row = lax.axis_index("mem") * mine + patch
        own[patch] = share(pattern, row, 1, patches, pert, weights, innov)


def pack(part, out, patch):
    _, padded, half = out.shape
    members = padded - PAD
    above = lax.broadcasted_iota(jnp.int32, (half, half), 0)
    across = lax.broadcasted_iota(jnp.int32, (half, half), 1)
    corner = part[half:members, half:]
    out[patch, :half, :] = part[:half, half:].astype(BF16)
    out[patch, half:members, :] = jnp.where(above >= across, part[:half, :half], corner).astype(
        BF16
    )
    diagonal = jnp.sum(jnp.where(above == across, corner, 0.0), axis=0, keepdims=True)
    force = part[members : members + 1]
    index = lax.broadcasted_iota(jnp.int32, (PAD, half), 0)
    tail = jnp.zeros((PAD, half), F32)
    for i, value in enumerate((diagonal, force[:, :half], force[:, half:])):
        high, low = split(value)
        tail = jnp.where(index == 2 * i, high.astype(F32), tail)
        tail = jnp.where(index == 2 * i + 1, low.astype(F32), tail)
    out[patch, members:, :] = tail.astype(BF16)


def neighbour(patches, side, pattern, pert, weights, innov, out):
    mine = out.shape[0]
    for patch in range(mine):
        row = lax.axis_index("mem") * mine + patch
        pack(share(pattern, row, side, patches, pert, weights, innov), out, patch)


def far_kernel(patches, pattern, pert, weights, innov, out):
    side = 2 - 2 * (lax.axis_index("lon") % 2)
    neighbour(patches, side, pattern, pert, weights, innov, out)


def near_kernel(patches, pattern, pert, weights, innov, state, paired, sent, out, *slabs):
    span = slabs[0].shape[2]
    length = len(slabs)
    layer, place = lax.axis_index("mem") // PAIR, lax.axis_index("mem") % PAIR
    for shift, slab in zip(turns(length), slabs):
        target = (layer ^ shift) * PAIR + place
        cols = pl.ds(pl.multiple_of(target * span, span), span)
        slab[place] = state[:, cols]
        slab[1 - place] = paired[:, cols]
    neighbour(patches, 2 * (lax.axis_index("lon") % 2), pattern, pert, weights, innov, out)


def total(value):
    return jnp.sum(jnp.sum(value, axis=0, keepdims=True), axis=1, keepdims=True)


def root_kernel(own, before, after, root_out, rows_out):
    mine, _, members = own.shape
    half = members // 2
    above = lax.broadcasted_iota(jnp.int32, (half, half), 0)
    across = lax.broadcasted_iota(jnp.int32, (half, half), 1)
    row = lax.broadcasted_iota(jnp.int32, (members, members), 0)
    col = lax.broadcasted_iota(jnp.int32, (members, members), 1)
    diagonal = row == col

    def dot(left, right):
        return jnp.dot(left, right, preferred_element_type=F32)

    each = range(mine)
    rest, factor, scale, forcing = [], [], [], []
    base = members - 1.0
    for patch in each:
        packed = before[patch].astype(F32) + after[patch].astype(F32)
        upper = packed[:half]
        mixed = packed[half:members]
        last = packed[members:]
        corner = last[0:1] + last[1:2]
        force = jnp.concatenate([last[2:3] + last[3:4], last[4:5] + last[5:6]], axis=1)
        flipped = mixed.T
        first = jnp.where(above >= across, mixed, flipped)
        second = jnp.where(above < across, mixed, flipped)
        second = jnp.where(above == across, corner, second)
        far = jnp.concatenate(
            [
                jnp.concatenate([first, upper], axis=1),
                jnp.concatenate([upper.T, second], axis=1),
            ],
            axis=0,
        )
        grams = own[patch, :members, :] + far
        blocks = grams[:half, :half] + grams[half:, half:]
        trace = total(jnp.where(above == across, blocks, 0.0))
        norm = jnp.sqrt(total(grams * grams) + 2.0 * base * trace + base * base * members)
        scale.append(norm)
        forcing.append(force + own[patch, members : members + 1, :])
        factor.append(1.5 - 0.5 * (trace / members + base) / norm)
        level = trace / members
        rest.append((grams - jnp.where(diagonal, level, 0.0)) * (-0.5 / norm))
    small = [rest[p].astype(BF16) for p in each]
    lead, tail = list(factor), list(small)
    squares = [dot(small[p], small[p]) for p in each]
    for step in range(1, ITERS):
        cubes = [dot(squares[p].astype(BF16), small[p]) for p in each]
        for p in each:
            f = factor[p]
            rest[p] = (
                (3.0 * f * f - 3.0 * f) * rest[p] + (3.0 * f - 1.5) * squares[p] + cubes[p]
            )
            factor[p] = 1.5 - 1.5 * f * f + f * f * f
            small[p] = rest[p].astype(BF16)
        for p in each:
            narrow = tail[p]
            if step < ITERS - 1:
                both = dot(jnp.concatenate([small[p], narrow], axis=0), small[p])
                squares[p], cross = both[:members], both[members:]
            else:
                cross = dot(narrow, small[p])
            tail[p] = (factor[p] * narrow.astype(F32) + lead[p] * rest[p] + cross).astype(BF16)
            lead[p] = factor[p] * lead[p]
    for p in each:
        high = tail[p]
        root_out[p] = high
        force = jnp.broadcast_to(forcing[p], (PAD, members))
        gain = (lead[p] * force + dot(force.astype(BF16), high)) / scale[p]
        index = lax.broadcasted_iota(jnp.int32, (PAD, members), 0)
        spread = jnp.sqrt(base) / jnp.sqrt(scale[p])
        rows_out[p] = jnp.where(index == 0, gain, jnp.where(index == 1, lead[p], spread))


def apply_kernel(root, rows, *rest):
    slabs, (out, columns) = rest[:-2], rest[-2:]
    mine, members, _ = root.shape
    points = out.shape[1] // mine
    length = len(slabs)
    _, local, _ = slabs[0].shape
    for shift, slab in zip(turns(length), slabs):
        source = (lax.axis_index("mem") // PAIR) ^ shift
        for i in range(PAIR):
            place = pl.ds(pl.multiple_of((source * PAIR + i) * local, local), local)
            columns[place, :] = slab[i]
    for p in range(mine):
        cols = slice(p * points, (p + 1) * points)
        member = columns[:, cols].astype(F32)
        mean = jnp.sum(member, axis=0, keepdims=True) / members
        deviation = member - mean
        spread = rows[p, 1:2, :points] * deviation + jnp.dot(
            root[p], deviation.astype(BF16), preferred_element_type=F32
        )
        shift = mean + product(split(rows[p]), split(spread))[0:1]
        out[:, cols] = (shift + rows[p, 2:3, :points] * spread).astype(BF16)


def body(state, hx, obs_value, obs_rinv, obs_count, loc_pattern):
    blocks, members, width = hx.shape
    patches, uses = loc_pattern.shape
    mem_total = lax.axis_size("mem")
    mine = patches // mem_total
    local, points = state.shape
    ring = lax.axis_size("lon")
    near = [(i, i + 1 - 2 * (i % 2)) for i in range(ring)]
    far = [(i, (i - 1 + 2 * (i % 2)) % ring) for i in range(ring)]
    shape = jax.ShapeDtypeStruct
    padded = members + PAD

    span = points // mem_total
    length = mem_total // PAIR
    swap = [(i, i ^ 1) for i in range(mem_total)]
    assert mem_total & (mem_total - 1) == 0

    pattern = loc_pattern.T
    far_pattern = lax.ppermute(pattern, "lon", far)
    near_pattern = lax.ppermute(pattern, "lon", near)
    paired = lax.ppermute(state, "mem", swap)
    limit = pltpu.CompilerParams(vmem_limit_bytes=16 * 1024 * 1024)
    gram = 2 * padded * members * uses * width
    pert, weights, innov, own = pl.pallas_call(
        functools.partial(own_kernel, patches),
        out_shape=(
            shape((blocks, members, width), BF16),
            shape((blocks, width), F32),
            shape((blocks, width), F32),
            shape((mine, padded, members), F32),
        ),
        in_specs=[HBM] * 5,
        out_specs=(VMEM,) * 4,
        scratch_shapes=[
            pltpu.VMEM((blocks, members, width), BF16),
            pltpu.SMEM(obs_count.shape, jnp.int32),
            pltpu.SMEM(pattern.shape, jnp.int32),
            pltpu.VMEM(obs_value.shape, F32),
            pltpu.VMEM(obs_rinv.shape, F32),
            pltpu.SemaphoreType.DMA((blocks // CHUNK,)),
            pltpu.SemaphoreType.DMA((4,)),
        ],
        compiler_params=limit,
        cost_estimate=pl.CostEstimate(
            flops=hx.size * 4 + mine * gram, bytes_accessed=2 * hx.size * 2, transcendentals=0
        ),
        name="own_share",
    )(*(stay(value) for value in (obs_count, pattern, hx, obs_value, obs_rinv)))
    packed = shape((mine, padded, members // 2), BF16)
    slab = shape((PAIR, local, span), BF16)
    cost = pl.CostEstimate(flops=mine * gram, bytes_accessed=hx.size, transcendentals=0)
    to_far = pl.pallas_call(
        functools.partial(far_kernel, patches),
        out_shape=packed,
        in_specs=[SMEM] + [VMEM] * 3,
        out_specs=VMEM,
        compiler_params=limit,
        cost_estimate=cost,
        name="far_share",
    )(far_pattern, pert, weights, innov)
    from_far = lax.ppermute(to_far, "lon", far)
    to_near, *slabs = pl.pallas_call(
        functools.partial(near_kernel, patches),
        out_shape=(packed,) + (slab,) * length,
        in_specs=[SMEM] + [VMEM] * 5 + [pl.BlockSpec(memory_space=pl.ANY)],
        out_specs=(VMEM,) * (1 + length),
        compiler_params=limit,
        cost_estimate=cost,
        name="near_share",
    )(near_pattern, pert, weights, innov, state, paired, to_far)
    from_near = lax.ppermute(to_near, "lon", near)
    for i, shift in enumerate(turns(length)):
        if shift:
            trade = [(j, j ^ (shift * PAIR)) for j in range(mem_total)]
            slabs[i] = lax.ppermute(slabs[i], "mem", trade)
    root, rows = pl.pallas_call(
        root_kernel,
        out_shape=(shape((mine, members, members), BF16), shape((mine, PAD, members), F32)),
        in_specs=[VMEM] * 3,
        out_specs=(VMEM,) * 2,
        compiler_params=limit,
        cost_estimate=pl.CostEstimate(
            flops=mine * 15 * 2 * members**3, bytes_accessed=2**20, transcendentals=0
        ),
        name="root",
    )(own, from_far, from_near)
    updated = pl.pallas_call(
        apply_kernel,
        out_shape=shape((members, span), BF16),
        in_specs=[VMEM] * (2 + length),
        out_specs=VMEM,
        scratch_shapes=[pltpu.VMEM((members, span), BF16)],
        compiler_params=limit,
        cost_estimate=pl.CostEstimate(
            flops=2 * members**2 * span, bytes_accessed=2**19, transcendentals=0
        ),
        name="apply",
    )(root, rows, *slabs)
    pieces = lax.all_to_all(
        updated.reshape(mem_total, local, span), "mem", split_axis=0, concat_axis=0
    )
    return jnp.swapaxes(pieces, 0, 1).reshape(local, points)


def solution(mesh):
    in_specs = (
        P("mem", "lon"),
        P("lon", None, None),
        P("lon", None),
        P("lon", None),
        P("lon"),
        P("lon", None),
    )
    out_specs = P("mem", "lon")
    return jax.shard_map(body, mesh=mesh, in_specs=in_specs, out_specs=out_specs, check_vma=False)
```

```python
import functools

import jax
import jax.numpy as jnp
from jax import lax
from jax.experimental import pallas as pl
from jax.experimental.pallas import tpu as pltpu
from jax.sharding import PartitionSpec as P

ITERS = 6
PAD = 16
CHUNK = 8
PAIR = 2
F32 = jnp.float32
BF16 = jnp.bfloat16

VMEM = pl.BlockSpec(memory_space=pltpu.VMEM)
SMEM = pl.BlockSpec(memory_space=pltpu.SMEM)
HBM = pl.BlockSpec(memory_space=pltpu.HBM)


def turns(length):
    return [0, *range(2, length), 1][:length]


def stay(value):
    return pltpu.with_memory_space_constraint(value, pltpu.HBM)


def split(value):
    high = value.astype(BF16)
    return high, (value - high.astype(F32)).astype(BF16)


def product(left, right):
    lhs = jnp.concatenate([left[0], left[0], left[1]], axis=1)
    rhs = jnp.concatenate([right[0], right[1], right[0]], axis=0)
    return jnp.dot(lhs, rhs, preferred_element_type=F32)


def share(pattern, row, side, patches, pert, weights, innov):
    blocks, _, width = pert.shape
    left, right = [], []
    for slot in range(pattern.shape[0]):
        position = pattern[slot, row]
        block = position - side * blocks
        here = jnp.logical_and(block >= 0, block < blocks)
        block = jnp.clip(block, 0, blocks - 1)
        spot = jnp.full((1, width), position, jnp.int32).astype(F32)
        rank = jnp.full((1, width), row, jnp.int32).astype(F32)
        offset = (spot + 0.5) / blocks - 1.0 - (rank + 0.5) / patches
        taper = jnp.exp(-0.5 * offset * offset) * jnp.where(here, 1.0, 0.0)
        picked = pert[block]
        weight = (taper * weights[pl.ds(block, 1), :]).astype(BF16)
        vector = jnp.broadcast_to(taper * innov[pl.ds(block, 1), :], (PAD, width)).astype(BF16)
        left.append(jnp.concatenate([weight * picked, vector], axis=0))
        right.append(picked)
    return lax.dot_general(
        jnp.concatenate(left, axis=1),
        jnp.concatenate(right, axis=1),
        (((1,), (1,)), ((), ())),
        preferred_element_type=F32,
    )


def own_kernel(
    patches,
    count_all,
    pattern_all,
    hx,
    value_all,
    rinv_all,
    pert,
    weights,
    innov,
    own,
    raw,
    count,
    pattern,
    value,
    rinv,
    sems,
    small,
):
    blocks, members, width = raw.shape
    smalls = [
        pltpu.make_async_copy(source, target, small.at[i])
        for i, (source, target) in enumerate(
            ((count_all, count), (value_all, value), (rinv_all, rinv), (pattern_all, pattern))
        )
    ]
    copies = [
        pltpu.make_async_copy(hx.at[pl.ds(i, CHUNK)], raw.at[pl.ds(i, CHUNK)], sems.at[i // CHUNK])
        for i in range(0, blocks, CHUNK)
    ]
    for copy in smalls + copies:
        copy.start()
    for copy in smalls:
        copy.wait()
    lane = lax.broadcasted_iota(jnp.int32, (1, width), 1)
    for block in range(blocks):
        if block % CHUNK == 0:
            copies[block // CHUNK].wait()
        member = raw[block].astype(F32)
        mean = jnp.sum(member, axis=0, keepdims=True) * (1.0 / members)
        pert[block] = (member - mean).astype(BF16)
        weight = jnp.where(lane < count[block], rinv[block : block + 1, :], 0.0)
        gap = weight * (value[block : block + 1, :] - mean)
        weights[block : block + 1, :] = weight.astype(BF16).astype(F32)
        innov[block : block + 1, :] = gap
    mine = own.shape[0]
    for patch in range(mine):
        row = lax.axis_index("mem") * mine + patch
        own[patch] = share(pattern, row, 1, patches, pert, weights, innov)


def pack(part, out, patch):
    _, padded, half = out.shape
    members = padded - PAD
    above = lax.broadcasted_iota(jnp.int32, (half, half), 0)
    across = lax.broadcasted_iota(jnp.int32, (half, half), 1)
    corner = part[half:members, half:]
    out[patch, :half, :] = part[:half, half:].astype(BF16)
    out[patch, half:members, :] = jnp.where(above >= across, part[:half, :half], corner).astype(
        BF16
    )
    diagonal = jnp.sum(jnp.where(above == across, corner, 0.0), axis=0, keepdims=True)
    force = part[members : members + 1]
    index = lax.broadcasted_iota(jnp.int32, (PAD, half), 0)
    tail = jnp.zeros((PAD, half), F32)
    for i, value in enumerate((diagonal, force[:, :half], force[:, half:])):
        high, low = split(value)
        tail = jnp.where(index == 2 * i, high.astype(F32), tail)
        tail = jnp.where(index == 2 * i + 1, low.astype(F32), tail)
    out[patch, members:, :] = tail.astype(BF16)


def neighbour(patches, side, pattern, pert, weights, innov, out):
    mine = out.shape[0]
    for patch in range(mine):
        row = lax.axis_index("mem") * mine + patch
        pack(share(pattern, row, side, patches, pert, weights, innov), out, patch)


def far_kernel(patches, pattern, pert, weights, innov, out):
    side = 2 - 2 * (lax.axis_index("lon") % 2)
    neighbour(patches, side, pattern, pert, weights, innov, out)


def near_kernel(patches, pattern, pert, weights, innov, state, paired, sent, out, *slabs):
    span = slabs[0].shape[2]
    length = len(slabs)
    layer, place = lax.axis_index("mem") // PAIR, lax.axis_index("mem") % PAIR
    for shift, slab in zip(turns(length), slabs):
        target = (layer ^ shift) * PAIR + place
        cols = pl.ds(pl.multiple_of(target * span, span), span)
        slab[place] = state[:, cols]
        slab[1 - place] = paired[:, cols]
    neighbour(patches, 2 * (lax.axis_index("lon") % 2), pattern, pert, weights, innov, out)


def total(value):
    return jnp.sum(jnp.sum(value, axis=0, keepdims=True), axis=1, keepdims=True)


def root_kernel(own, before, after, root_out, rows_out):
    mine, _, members = own.shape
    half = members // 2
    above = lax.broadcasted_iota(jnp.int32, (half, half), 0)
    across = lax.broadcasted_iota(jnp.int32, (half, half), 1)
    row = lax.broadcasted_iota(jnp.int32, (members, members), 0)
    col = lax.broadcasted_iota(jnp.int32, (members, members), 1)
    diagonal = row == col

    def dot(left, right):
        return jnp.dot(left, right, preferred_element_type=F32)

    each = range(mine)
    rest, factor, scale, forcing = [], [], [], []
    base = members - 1.0
    for patch in each:
        packed = before[patch].astype(F32) + after[patch].astype(F32)
        upper = packed[:half]
        mixed = packed[half:members]
        last = packed[members:]
        corner = last[0:1] + last[1:2]
        force = jnp.concatenate([last[2:3] + last[3:4], last[4:5] + last[5:6]], axis=1)
        flipped = mixed.T
        first = jnp.where(above >= across, mixed, flipped)
        second = jnp.where(above < across, mixed, flipped)
        second = jnp.where(above == across, corner, second)
        far = jnp.concatenate(
            [
                jnp.concatenate([first, upper], axis=1),
                jnp.concatenate([upper.T, second], axis=1),
            ],
            axis=0,
        )
        grams = own[patch, :members, :] + far
        blocks = grams[:half, :half] + grams[half:, half:]
        trace = total(jnp.where(above == across, blocks, 0.0))
        norm = jnp.sqrt(total(grams * grams) + 2.0 * base * trace + base * base * members)
        scale.append(norm)
        forcing.append(force + own[patch, members : members + 1, :])
        factor.append(1.5 - 0.5 * (trace / members + base) / norm)
        level = trace / members
        rest.append((grams - jnp.where(diagonal, level, 0.0)) * (-0.5 / norm))
    small = [rest[p].astype(BF16) for p in each]
    lead, tail = list(factor), list(small)
    squares = [dot(small[p], small[p]) for p in each]
    for step in range(1, ITERS):
        cubes = [dot(squares[p].astype(BF16), small[p]) for p in each]
        for p in each:
            f = factor[p]
            rest[p] = (
                (3.0 * f * f - 3.0 * f) * rest[p] + (3.0 * f - 1.5) * squares[p] + cubes[p]
            )
            factor[p] = 1.5 - 1.5 * f * f + f * f * f
            small[p] = rest[p].astype(BF16)
        for p in each:
            narrow = tail[p]
            if step < ITERS - 1:
                both = dot(jnp.concatenate([small[p], narrow], axis=0), small[p])
                squares[p], cross = both[:members], both[members:]
            else:
                cross = dot(narrow, small[p])
            tail[p] = (factor[p] * narrow.astype(F32) + lead[p] * rest[p] + cross).astype(BF16)
            lead[p] = factor[p] * lead[p]
    for p in each:
        high = tail[p]
        root_out[p] = high
        force = jnp.broadcast_to(forcing[p], (PAD, members))
        gain = (lead[p] * force + dot(force.astype(BF16), high)) / scale[p]
        index = lax.broadcasted_iota(jnp.int32, (PAD, members), 0)
        spread = jnp.sqrt(base) / jnp.sqrt(scale[p])
        rows_out[p] = jnp.where(index == 0, gain, jnp.where(index == 1, lead[p], spread))


def apply_kernel(root, rows, *rest):
    slabs, (out, columns) = rest[:-2], rest[-2:]
    mine, members, _ = root.shape
    points = out.shape[3]
    length = len(slabs)
    _, local, _ = slabs[0].shape
    for shift, slab in zip(turns(length), slabs):
        source = (lax.axis_index("mem") // PAIR) ^ shift
        for i in range(PAIR):
            place = pl.ds(pl.multiple_of((source * PAIR + i) * local, local), local)
            columns[place, :] = slab[i]
    for p in range(mine):
        cols = slice(p * points, (p + 1) * points)
        member = columns[:, cols].astype(F32)
        mean = jnp.sum(member, axis=0, keepdims=True) / members
        deviation = member - mean
        spread = rows[p, 1:2, :points] * deviation + jnp.dot(
            root[p], deviation.astype(BF16), preferred_element_type=F32
        )
        shift = mean + product(split(rows[p]), split(spread))[0:1]
        result = (shift + rows[p, 2:3, :points] * spread).astype(BF16)
        out[:, p] = result.reshape(out.shape[0], local, points)


def body(state, hx, obs_value, obs_rinv, obs_count, loc_pattern):
    blocks, members, width = hx.shape
    patches, uses = loc_pattern.shape
    mem_total = lax.axis_size("mem")
    mine = patches // mem_total
    local, points = state.shape
    ring = lax.axis_size("lon")
    near = [(i, i + 1 - 2 * (i % 2)) for i in range(ring)]
    far = [(i, (i - 1 + 2 * (i % 2)) % ring) for i in range(ring)]
    shape = jax.ShapeDtypeStruct
    padded = members + PAD

    span = points // mem_total
    length = mem_total // PAIR
    swap = [(i, i ^ 1) for i in range(mem_total)]
    assert mem_total & (mem_total - 1) == 0

    pattern = loc_pattern.T
    far_pattern = lax.ppermute(pattern, "lon", far)
    near_pattern = lax.ppermute(pattern, "lon", near)
    paired = lax.ppermute(state, "mem", swap)
    limit = pltpu.CompilerParams(vmem_limit_bytes=16 * 1024 * 1024)
    gram = 2 * padded * members * uses * width
    pert, weights, innov, own = pl.pallas_call(
        functools.partial(own_kernel, patches),
        out_shape=(
            shape((blocks, members, width), BF16),
            shape((blocks, width), F32),
            shape((blocks, width), F32),
            shape((mine, padded, members), F32),
        ),
        in_specs=[HBM] * 5,
        out_specs=(VMEM,) * 4,
        scratch_shapes=[
            pltpu.VMEM((blocks, members, width), BF16),
            pltpu.SMEM(obs_count.shape, jnp.int32),
            pltpu.SMEM(pattern.shape, jnp.int32),
            pltpu.VMEM(obs_value.shape, F32),
            pltpu.VMEM(obs_rinv.shape, F32),
            pltpu.SemaphoreType.DMA((blocks // CHUNK,)),
            pltpu.SemaphoreType.DMA((4,)),
        ],
        compiler_params=limit,
        cost_estimate=pl.CostEstimate(
            flops=hx.size * 4 + mine * gram, bytes_accessed=2 * hx.size * 2, transcendentals=0
        ),
        name="own_share",
    )(*(stay(value) for value in (obs_count, pattern, hx, obs_value, obs_rinv)))
    packed = shape((mine, padded, members // 2), BF16)
    slab = shape((PAIR, local, span), BF16)
    cost = pl.CostEstimate(flops=mine * gram, bytes_accessed=hx.size, transcendentals=0)
    to_far = pl.pallas_call(
        functools.partial(far_kernel, patches),
        out_shape=packed,
        in_specs=[SMEM] + [VMEM] * 3,
        out_specs=VMEM,
        compiler_params=limit,
        cost_estimate=cost,
        name="far_share",
    )(far_pattern, pert, weights, innov)
    from_far = lax.ppermute(to_far, "lon", far)
    to_near, *slabs = pl.pallas_call(
        functools.partial(near_kernel, patches),
        out_shape=(packed,) + (slab,) * length,
        in_specs=[SMEM] + [VMEM] * 5 + [pl.BlockSpec(memory_space=pl.ANY)],
        out_specs=(VMEM,) * (1 + length),
        compiler_params=limit,
        cost_estimate=cost,
        name="near_share",
    )(near_pattern, pert, weights, innov, state, paired, to_far)
    from_near = lax.ppermute(to_near, "lon", near)
    for i, shift in enumerate(turns(length)):
        if shift:
            trade = [(j, j ^ (shift * PAIR)) for j in range(mem_total)]
            slabs[i] = lax.ppermute(slabs[i], "mem", trade)
    root, rows = pl.pallas_call(
        root_kernel,
        out_shape=(shape((mine, members, members), BF16), shape((mine, PAD, members), F32)),
        in_specs=[VMEM] * 3,
        out_specs=(VMEM,) * 2,
        compiler_params=limit,
        cost_estimate=pl.CostEstimate(
            flops=mine * 15 * 2 * members**3, bytes_accessed=2**20, transcendentals=0
        ),
        name="root",
    )(own, from_far, from_near)
    updated = pl.pallas_call(
        apply_kernel,
        out_shape=shape((mem_total, mine, local, span // mine), BF16),
        in_specs=[VMEM] * (2 + length),
        out_specs=VMEM,
        scratch_shapes=[pltpu.VMEM((members, span), BF16)],
        compiler_params=limit,
        cost_estimate=pl.CostEstimate(
            flops=2 * members**2 * span, bytes_accessed=2**19, transcendentals=0
        ),
        name="apply",
    )(root, rows, *slabs)
    pieces = lax.all_to_all(updated, "mem", split_axis=0, concat_axis=0)
    return jnp.transpose(pieces, (2, 0, 1, 3)).reshape(local, points)


def solution(mesh):
    in_specs = (
        P("mem", "lon"),
        P("lon", None, None),
        P("lon", None),
        P("lon", None),
        P("lon"),
        P("lon", None),
    )
    out_specs = P("mem", "lon")
    return jax.shard_map(body, mesh=mesh, in_specs=in_specs, out_specs=out_specs, check_vma=False)
```
